32 devices in a mesh: tm: 4 (over y, x), space: 8 (over z, core).
Axes of the slice: x: 2, y: 2, z: 4, core: 2. Of those that a mesh axis runs over, the one named last changes fastest.
Arguments:
- snapshots: bfloat16 [2048, 16384], P('tm', 'space'), may hold values from -13 to 13
- modes_basis: bfloat16 [16384, 64], P('space'), may hold values from -0.046875 to 0.046875
- reg_weights: float32 [2144], replicated, may hold values from 0.3 to 3
Outputs:
- reduced: float32 [2048, 64], P('tm')
- time_rates: float32 [2048, 64], P('tm')
- normal: float32 [2144, 2144], P('tm', 'space')
- right_side: float32 [2144, 64], P('tm')
The draws below stay inside these ranges and needn't reach their ends.
All inputs are finite; a program needn't handle non-finite values.
Results may differ from the reference program's by a relative error of at most 0.0043.
Values sent between devices are 32-bit elements; how exact they have to be, the bound alone decides.
No kernel may reach another device: no remote copies, remote signals or barrier semaphores. Data moves between devices by JAX's collectives and lax.ppermute only.
A program may use at most 128 MiB of HBM per device.

```python
import math
import jax
import jax.numpy as jnp

R = 64
FEATURES = 2144
SNAPS = 2048
NSTATE = 16384


def draw_snapshots(key, part):
    key = jax.random.fold_in(key, 11)
    key_rows, key_cols, key_noise = jax.random.split(key, 3)
    row_scale = jnp.exp(jax.random.uniform(key_rows, (SNAPS, 1), jnp.float32, math.log(0.6), math.log(1.6)))
    col_scale = jnp.exp(jax.random.uniform(key_cols, (1, NSTATE), jnp.float32, math.log(0.6), math.log(1.6)))
    field = jnp.clip(jax.random.normal(key_noise, (SNAPS, NSTATE), jnp.float32), -5.0, 5.0)
    return (row_scale * col_scale * field).astype(jnp.bfloat16)


def block_scale(own_key, extent, cuts, smallest, largest):
    gain = 1.0
    for dim, shards_of in cuts:
        steps = jax.random.uniform(jax.random.fold_in(jax.random.fold_in(own_key, 6), dim), (shards_of,), jnp.float32, smallest / len(cuts), largest / len(cuts))
        gain = gain * jnp.repeat(jnp.exp(steps), extent[dim] // shards_of).reshape((-1,) + (1,) * (len(extent) - 1 - dim))
    return gain


def bell_draw(own_key, shape, width, most, cuts=(), dtype=jnp.bfloat16):
    factor_of = block_scale(own_key, shape, cuts, -0.22, 0.18) if cuts else 1.0
    drawn = jax.random.normal(own_key, shape, jnp.float32) * width * factor_of
    return jnp.minimum(jnp.maximum(drawn, -most), most).astype(dtype)


def setup_inputs(seed: int = 0) -> dict:
    arg_keys = jax.random.split(jax.random.key(seed), 4)
    snapshots = draw_snapshots(jax.random.fold_in(arg_keys[3], 71), 0)
    modes_basis = bell_draw(arg_keys[1], (NSTATE, R), NSTATE ** -0.5, 0.046875, ((0, 8),))
    reg_weights = jnp.clip(jnp.exp(jax.random.uniform(arg_keys[2], (FEATURES,), jnp.float32, math.log(0.3), math.log(3.0))), 0.3, 3.0)
    return dict(snapshots=snapshots, modes_basis=modes_basis, reg_weights=reg_weights)


def features_of(reduced):
    pieces = [reduced]
    for column in range(reduced.shape[1]):
        pieces.append(reduced[:, column:column + 1] * reduced[:, column:])
    return jnp.concatenate(pieces, axis=1).astype(jnp.bfloat16)


def rates_of(reduced):
    central = (reduced[2:] - reduced[:-2]) * 0.5
    first_row = reduced[1:2] - reduced[0:1]
    last_row = reduced[-1:] - reduced[-2:-1]
    return jnp.concatenate([first_row, central, last_row], axis=0)


def reference(snapshots, modes_basis, reg_weights):
    reduced = jnp.dot(snapshots, modes_basis, preferred_element_type=jnp.float32)
    time_rates = rates_of(reduced)
    features = features_of(reduced)
    rates_bf = time_rates.astype(jnp.bfloat16)
    inv_count = 1.0 / SNAPS
    normal = jnp.dot(features.T, features, preferred_element_type=jnp.float32) * inv_count + jnp.diag(reg_weights)
    right_side = jnp.dot(features.T, rates_bf, preferred_element_type=jnp.float32) * inv_count
    return (reduced, time_rates, normal, right_side)
```

```python
import functools

import jax
import jax.numpy as jnp
from jax import lax
from jax.experimental import pallas as pl
from jax.experimental.pallas import tpu as pltpu
from jax.sharding import PartitionSpec as P

NT = (((1,), (1,)), ((), ()))


def round_up(value, step):
    return (value + step - 1) // step * step


def selectors(first, rows, modes, depth):
    feature = first + lax.broadcasted_iota(jnp.int32, (rows, 1), 0)
    mode = lax.broadcasted_iota(jnp.int32, (1, modes), 1)
    start = modes + mode * modes - (mode * (mode - 1)) // 2
    gap = feature - start
    holds = (gap >= 0) & (gap < modes - mode)
    left = jnp.sum(jnp.where(holds, mode, 0), axis=1, keepdims=True)
    right = left + jnp.sum(jnp.where(holds, gap, 0), axis=1, keepdims=True)
    linear = feature < modes
    left = jnp.where(linear, feature, left)
    right = jnp.where(linear, modes, right)
    lane = lax.broadcasted_iota(jnp.int32, (1, depth), 1)
    held = jnp.where(lane < 3 * modes, lax.rem(lane, modes), lane - 2 * modes)
    return (
        jnp.where(held == left, 1.0, 0.0).astype(jnp.bfloat16),
        jnp.where(held == right, 1.0, 0.0).astype(jnp.bfloat16),
    )


def parts_of(block, depth):
    modes, snaps = block.shape
    high = block.astype(jnp.bfloat16)
    rest = block - high.astype(jnp.float32)
    middle = rest.astype(jnp.bfloat16)
    low = (rest - middle.astype(jnp.float32)).astype(jnp.bfloat16)
    tail = depth - 3 * modes
    ones = jnp.where(lax.broadcasted_iota(jnp.int32, (tail, snaps), 0) == 0, 1.0, 0.0)
    return jnp.concatenate([high, middle, low, ones.astype(jnp.bfloat16)], axis=0)


def picked(left, right, parts):
    first = jnp.dot(left, parts, preferred_element_type=jnp.float32)
    second = jnp.dot(right, parts, preferred_element_type=jnp.float32)
    return (first * second).astype(jnp.bfloat16)


def normal_kernel(
    groups, row_block, col_block, place_ref, all_ref, reg_ref,
    reduced_ref, rates_ref, normal_ref, right_ref, col_scratch, acc_scratch,
):
    time_idx = place_ref[0]
    space_idx = place_ref[1]
    modes, snaps = all_ref.shape[1:]
    count = groups * snaps
    rows = round_up(row_block, 16)
    cols = round_up(col_block, 16)
    depth = round_up(3 * modes + 1, 128)
    row_left, row_right = selectors(time_idx * row_block, rows, modes, depth)
    col_left, col_right = selectors(space_idx * col_block, cols, modes, depth)
    lane = lax.broadcasted_iota(jnp.int32, (1, snaps), 1)
    for group in range(groups):
        block = all_ref[group]
        before = all_ref[max(group - 1, 0)][:, snaps - 1 : snaps]
        after = all_ref[min(group + 1, groups - 1)][:, 0:1]
        low = jnp.where(lane == 0, before, pltpu.roll(block, 1, 1))
        high = jnp.where(lane == snaps - 1, after, pltpu.roll(block, snaps - 1, 1))
        rates = (high - low) * 0.5
        if group == 0:
            rates = jnp.where(lane == 0, high - block, rates)
        if group == groups - 1:
            rates = jnp.where(lane == snaps - 1, block - low, rates)

        @pl.when(time_idx == group)
        def _():
            reduced_ref[...] = block.T
            rates_ref[...] = rates.T

        parts = parts_of(block, depth)
        col_scratch[:cols] = picked(col_left, col_right, parts)
        col_scratch[cols:] = rates.astype(jnp.bfloat16)
        row_features = picked(row_left, row_right, parts)
        term = lax.dot_general(row_features, col_scratch[...], NT, preferred_element_type=jnp.float32)
        if group == 0:
            acc_scratch[...] = term
        else:
            acc_scratch[...] += term
    scale = 1.0 / count
    row_ids = time_idx * row_block + lax.broadcasted_iota(jnp.int32, (row_block, col_block), 0)
    col_ids = space_idx * col_block + lax.broadcasted_iota(jnp.int32, (row_block, col_block), 1)
    diagonal = jnp.where(row_ids == col_ids, reg_ref[...], 0.0)
    normal_ref[...] = acc_scratch[:row_block, :col_block] * scale + diagonal
    right_ref[...] = acc_scratch[:row_block, cols:] * scale


def local(snapshots, modes_basis, reg_weights):
    feature_count = reg_weights.shape[0]
    snaps_dev = snapshots.shape[0]
    modes = modes_basis.shape[1]
    tm_count = lax.axis_size("tm")
    space_count = lax.axis_size("space")
    row_block = feature_count // tm_count
    col_block = feature_count // space_count
    time_idx = lax.axis_index("tm")
    space_idx = lax.axis_index("space")
    partial_value = lax.dot_general(
        modes_basis, snapshots, (((0,), (1,)), ((), ())), preferred_element_type=jnp.float32
    )
    spread = lax.all_to_all(partial_value, "space", 0, 0, tiled=True)
    share = jnp.sum(spread.reshape(space_count, modes // space_count, snaps_dev), axis=0)
    copies = jnp.broadcast_to(share[None], (space_count,) + share.shape).reshape(modes, snaps_dev)
    own = lax.all_to_all(copies, "space", 0, 0, tiled=True)
    slots = [own]
    for step in range(1, tm_count):
        slots.append(lax.ppermute(own, "tm", [(i, i ^ step) for i in range(tm_count)]))
    stacked = jnp.stack(slots)
    order = jnp.bitwise_xor(time_idx, jnp.arange(tm_count))
    everyone = jnp.take(stacked, order, axis=0)
    reg_cols = lax.dynamic_slice_in_dim(reg_weights, space_idx * col_block, col_block, 0)[None]
    place = jnp.stack([time_idx, space_idx]).astype(jnp.int32)
    rows = round_up(row_block, 16)
    cols = round_up(col_block, 16)
    vmem = pl.BlockSpec(memory_space=pltpu.VMEM)
    return pl.pallas_call(
        functools.partial(normal_kernel, tm_count, row_block, col_block),
        out_shape=(
            jax.ShapeDtypeStruct((snaps_dev, modes), jnp.float32),
            jax.ShapeDtypeStruct((snaps_dev, modes), jnp.float32),
            jax.ShapeDtypeStruct((row_block, col_block), jnp.float32),
            jax.ShapeDtypeStruct((row_block, modes), jnp.float32),
        ),
        in_specs=[pl.BlockSpec(memory_space=pltpu.SMEM), vmem, vmem],
        out_specs=(vmem,) * 4,
        scratch_shapes=[
            pltpu.VMEM((cols + modes, snaps_dev), jnp.bfloat16),
            pltpu.VMEM((rows, cols + modes), jnp.float32),
        ],
        compiler_params=pltpu.CompilerParams(vmem_limit_bytes=48 * 1024 * 1024),
        name="normal_block",
    )(place, everyone, reg_cols)


def solution(mesh):
    return jax.shard_map(
        local,
        mesh=mesh,
        in_specs=(P("tm", "space"), P("space", None), P()),
        out_specs=(P("tm", None), P("tm", None), P("tm", "space"), P("tm", None)),
        check_vma=False,
    )
```

```python
import functools

import jax
import jax.numpy as jnp
from jax import lax
from jax.experimental import pallas as pl
from jax.experimental.pallas import tpu as pltpu
from jax.sharding import PartitionSpec as P

NT = (((1,), (1,)), ((), ()))


def round_up(value, step):
    return (value + step - 1) // step * step


def tree_sum(terms):
    while len(terms) > 1:
        terms = [terms[i] + terms[i + 1] for i in range(0, len(terms), 2)]
    return terms[0]


def selectors(first, rows, modes, depth):
    feature = first + lax.broadcasted_iota(jnp.int32, (rows, 1), 0)
    mode = lax.broadcasted_iota(jnp.int32, (1, modes), 1)
    start = modes + mode * modes - (mode * (mode - 1)) // 2
    gap = feature - start
    holds = (gap >= 0) & (gap < modes - mode)
    left = jnp.sum(jnp.where(holds, mode, 0), axis=1, keepdims=True)
    right = left + jnp.sum(jnp.where(holds, gap, 0), axis=1, keepdims=True)
    linear = feature < modes
    left = jnp.where(linear, feature, left)
    right = jnp.where(linear, modes, right)
    lane = lax.broadcasted_iota(jnp.int32, (1, depth), 1)
    held = jnp.where(lane < 3 * modes, lax.rem(lane, modes), lane - 2 * modes)
    return (
        jnp.where(held == left, 1.0, 0.0).astype(jnp.bfloat16),
        jnp.where(held == right, 1.0, 0.0).astype(jnp.bfloat16),
    )


def parts_of(block, depth):
    modes, snaps = block.shape
    high = block.astype(jnp.bfloat16)
    rest = block - high.astype(jnp.float32)
    middle = rest.astype(jnp.bfloat16)
    low = (rest - middle.astype(jnp.float32)).astype(jnp.bfloat16)
    tail = depth - 3 * modes
    ones = jnp.where(lax.broadcasted_iota(jnp.int32, (tail, snaps), 0) == 0, 1.0, 0.0)
    return jnp.concatenate([high, middle, low, ones.astype(jnp.bfloat16)], axis=0)


def picked(left, right, parts):
    first = jnp.dot(left, parts, preferred_element_type=jnp.float32)
    second = jnp.dot(right, parts, preferred_element_type=jnp.float32)
    return (first * second).astype(jnp.bfloat16)


def project_kernel(place_ref, basis_ref, snaps_ref, keep_ref, give_ref, basis, held, basis_sem, sems):
    core = place_ref[1] % 2
    _, chunks, half, step = held.shape
    basis_copy = pltpu.make_async_copy(basis_ref, basis, basis_sem)
    basis_copy.start()
    copies = []
    for side in range(2):
        first = pl.multiple_of((core if side else 1 - core) * half, half)
        for chunk in range(chunks):
            copies.append(
                pltpu.make_async_copy(
                    snaps_ref.at[pl.ds(first, half), pl.ds(chunk * step, step)],
                    held.at[side, chunk],
                    sems.at[side, chunk],
                )
            )
            copies[-1].start()
    basis_copy.wait()
    for side, out_ref in enumerate((give_ref, keep_ref)):
        for copy in copies[side * chunks : (side + 1) * chunks]:
            copy.wait()
        terms = [
            lax.dot_general(
                held[side, chunk],
                basis[:, chunk * step : (chunk + 1) * step],
                NT,
                preferred_element_type=jnp.float32,
            )
            for chunk in range(chunks)
        ]
        out_ref[...] = tree_sum(terms).T


def project(place, snapshots, basis):
    snaps, states = snapshots.shape
    modes = basis.shape[0]
    half = snaps // 2
    chunks = 4
    hbm = pl.BlockSpec(memory_space=pltpu.HBM)
    vmem = pl.BlockSpec(memory_space=pltpu.VMEM)
    block = jax.ShapeDtypeStruct((modes, half), jnp.float32)
    return pl.pallas_call(
        project_kernel,
        out_shape=(block, block),
        in_specs=[pl.BlockSpec(memory_space=pltpu.SMEM), hbm, hbm],
        out_specs=(vmem, vmem),
        scratch_shapes=[
            pltpu.VMEM(basis.shape, basis.dtype),
            pltpu.VMEM((2, chunks, half, states // chunks), snapshots.dtype),
            pltpu.SemaphoreType.DMA,
            pltpu.SemaphoreType.DMA((2, chunks)),
        ],
        compiler_params=pltpu.CompilerParams(vmem_limit_bytes=55000 * 1024),
        name="project",
    )(place, basis, snapshots)


def selector_kernel(row_block, col_block, modes, place_ref, left_ref, right_ref):
    cols = round_up(col_block, 16)
    rows = left_ref.shape[0] - cols
    depth = left_ref.shape[1]
    for at, size, first in (
        (0, cols, place_ref[1] * col_block),
        (cols, rows, place_ref[0] * row_block),
    ):
        left, right = selectors(first, size, modes, depth)
        left_ref[at : at + size] = left
        right_ref[at : at + size] = right


def inner_rates(block, half):
    snaps = block.shape[1]
    lane = lax.rem(lax.broadcasted_iota(jnp.int32, (1, snaps), 1), half)
    rates = (pltpu.roll(block, snaps - 1, 1) - pltpu.roll(block, 1, 1)) * 0.5
    return jnp.where((lane == 0) | (lane == half - 1), 0.0, rates)


def column_side(left_ref, right_ref, parts, rates, cols, col_scratch):
    col_scratch[:cols, : rates.shape[1]] = picked(left_ref[:cols], right_ref[:cols], parts)
    col_scratch[cols:, : rates.shape[1]] = rates.astype(jnp.bfloat16)


def terms_of(left_ref, right_ref, block, half, cols, col_scratch):
    parts = parts_of(block, left_ref.shape[1])
    column_side(left_ref, right_ref, parts, inner_rates(block, half), cols, col_scratch)
    row_features = picked(left_ref[cols:], right_ref[cols:], parts)
    return lax.dot_general(
        col_scratch[:, : block.shape[1]], row_features, NT, preferred_element_type=jnp.float32
    )


def stack_kernel(cols, has_before, left_ref, right_ref, *refs):
    block_ref, acc_ref, col_scratch = refs[-3:]
    count, _, half = block_ref.shape
    block = jnp.concatenate([block_ref[slot] for slot in range(count)], axis=1)
    term = terms_of(left_ref, right_ref, block, half, cols, col_scratch)
    acc_ref[...] = refs[0][...] + term if has_before else term


def slot_offset(slot, core, bits):
    plain = sum(((slot >> k) & 1) << k for k in range(bits))
    turned = sum(((slot >> k) & 1) << ((k + 1) % bits) for k in range(bits))
    return jnp.where(core == 0, plain, turned)


def edge_columns(time_idx, core, mine_ref, other_ref, starts, ends):
    groups, modes, half = mine_ref.shape
    width = starts.shape[2]
    for slot in range(groups):
        for source, side in ((mine_ref, core), (other_ref, 1 - core)):
            at = 2 * (time_idx ^ slot_offset(slot, side, (groups - 1).bit_length())) + side
            starts[at] = source[slot, :, :width]
            ends[at] = source[slot, :, half - width :]
    lane = lax.broadcasted_iota(jnp.int32, (1, width), 1)
    heads = jnp.zeros((modes, width), jnp.float32)
    tails = jnp.zeros((modes, width), jnp.float32)
    count = 2 * groups
    for at in range(count):
        pair = (lane == 2 * at) | (lane == 2 * at + 1)
        heads = jnp.where(pair, pltpu.roll(starts[at], 2 * at, 1), heads)
        tails = jnp.where(pair, pltpu.roll(ends[at], (2 * at + 2) % width, 1), tails)
    after = pltpu.roll(heads, width - 1, 1)
    before = pltpu.roll(tails, 1, 1)
    rates = (after - before) * 0.5
    rates = jnp.where(lane == 0, after - heads, rates)
    rates = jnp.where(lane == 2 * count - 1, tails - before, rates)
    edge = jnp.where(lax.rem(lane, 2) == 0, heads, tails)
    inside = lane < 2 * count
    return jnp.where(inside, edge, 0.0), jnp.where(inside, rates, 0.0)


def last_kernel(
    row_block, col_block, row_chunk, place_ref, left_ref, right_ref, before_ref, reg_ref, mine_ref,
    other_ref, reduced_ref, rates_ref, normal_ref, right_side_ref, starts, ends, col_scratch,
    reduced_out, rates_out, normal_out, right_side_out, sems,
):
    time_idx = place_ref[0]
    space_idx = place_ref[1]
    core = space_idx % 2
    groups, modes, half = mine_ref.shape
    snaps = 2 * half
    cols = round_up(col_block, 16)
    depth = left_ref.shape[1]
    copies = []

    def send(source, target):
        copies.append(pltpu.make_async_copy(source, target, sems.at[len(copies)]))
        copies[-1].start()

    edge, edge_rates = edge_columns(time_idx, core, mine_ref, other_ref, starts, ends)
    first = pl.multiple_of(core * half, half)
    second = pl.multiple_of((1 - core) * half, half)
    reduced_out[:, pl.ds(first, half)] = mine_ref[0]
    reduced_out[:, pl.ds(second, half)] = other_ref[0]
    send(reduced_out, reduced_ref)
    own = reduced_out[...]
    width = edge.shape[1]
    own_edges = pltpu.roll(edge_rates, lax.rem(width - 4 * time_idx, width), 1)
    lane = lax.broadcasted_iota(jnp.int32, (1, snaps), 1)
    rates = jnp.where(lane == 0, own_edges[:, 0:1], inner_rates(own, snaps))
    rates_out[...] = jnp.where(lane == snaps - 1, own_edges[:, 3:4], rates)
    send(rates_out, rates_ref)

    block = jnp.concatenate([other_ref[slot] for slot in range(groups)], axis=1)
    parts = parts_of(block, depth)
    edge_parts = parts_of(edge, depth)
    column_side(left_ref, right_ref, parts, inner_rates(block, half), cols, col_scratch)
    edge_rates = edge_rates.astype(jnp.bfloat16)
    scale = 1.0 / (groups * snaps)
    for at in range(0, row_block, row_chunk):
        size = min(row_chunk, row_block - at)
        padded = round_up(size, 16)
        pick = slice(cols + at, cols + at + padded)
        features = picked(left_ref[pick], right_ref[pick], parts)
        edge_features = picked(left_ref[pick], right_ref[pick], edge_parts)
        total = before_ref[:, at : at + padded] + lax.dot_general(
            col_scratch[...], features, NT, preferred_element_type=jnp.float32
        )
        edge_total = lax.dot_general(edge_rates, edge_features, NT, preferred_element_type=jnp.float32)
        col_ids = space_idx * col_block + lax.broadcasted_iota(jnp.int32, (col_block, size), 0)
        row_ids = time_idx * row_block + at + lax.broadcasted_iota(jnp.int32, (col_block, size), 1)
        diagonal = jnp.where(row_ids == col_ids, reg_ref[:, at : at + size], 0.0)
        normal_out[:, at : at + size] = total[:col_block, :size] * scale + diagonal
        right_side_out[:, at : at + size] = (total[cols:] + edge_total)[:, :size] * scale
        send(normal_out.at[:, at : at + size], normal_ref.at[:, at : at + size])
    send(right_side_out, right_side_ref)
    for copy in copies:
        copy.wait()


def swapped(value, axis, distance):
    return lax.ppermute(value, axis, [(i, i ^ distance) for i in range(lax.axis_size(axis))])


def exchanged(value, axis, step, bits, first_bit):
    space_count = lax.axis_size("space")
    tm_count = lax.axis_size("tm")
    perm = []
    for time in range(tm_count):
        for space in range(space_count):
            distance = 1 << (first_bit + (step + space % 2) % bits)
            if axis == "tm":
                target = (time ^ distance) * space_count + space
            else:
                target = time * space_count + (space ^ distance)
            perm.append((time * space_count + space, target))
    return lax.ppermute(value, ("tm", "space"), perm)


def local(snapshots, modes_basis, reg_weights):
    feature_count = reg_weights.shape[0]
    snaps_dev = snapshots.shape[0]
    modes = modes_basis.shape[1]
    tm_count = lax.axis_size("tm")
    space_count = lax.axis_size("space")
    row_block = feature_count // tm_count
    col_block = feature_count // space_count
    rows = round_up(row_block, 16)
    cols = round_up(col_block, 16)
    depth = round_up(3 * modes + 1, 128)
    time_idx = lax.axis_index("tm")
    space_idx = lax.axis_index("space")
    place = jnp.stack([time_idx, space_idx]).astype(jnp.int32)
    smem = pl.BlockSpec(memory_space=pltpu.SMEM)
    vmem = pl.BlockSpec(memory_space=pltpu.VMEM)
    params = pltpu.CompilerParams(vmem_limit_bytes=32 * 1024 * 1024)

    keep, give = project(place, snapshots, modes_basis.T)
    half = keep + swapped(give, "space", 1)
    after, half = lax.optimization_barrier((place, half))
    selector = jax.ShapeDtypeStruct((cols + rows, depth), jnp.bfloat16)
    left, right = pl.pallas_call(
        functools.partial(selector_kernel, row_block, col_block, modes),
        out_shape=(selector, selector),
        in_specs=[smem],
        out_specs=(vmem, vmem),
        compiler_params=params,
        cost_estimate=pl.CostEstimate(flops=10**6, bytes_accessed=10**6, transcendentals=0),
        name="selectors",
    )(after)
    first_row = after[0] * row_block
    reg_rows = lax.dynamic_slice_in_dim(reg_weights, first_row, row_block, 0)[None]

    total = half
    space_bits = (space_count - 1).bit_length() - 1
    for step in range(space_bits):
        total = total + exchanged(total, "space", step, space_bits, 1)
    total, left, right, reg_rows = lax.optimization_barrier((total, left, right, reg_rows))

    acc_shape = jax.ShapeDtypeStruct((cols + modes, rows), jnp.float32)

    def cost(count):
        flops = 2 * count * (2 * depth * (cols + rows) + (cols + modes) * rows)
        return pl.CostEstimate(flops=flops, bytes_accessed=2 * 10**6, transcendentals=0)

    def col_scratch(count):
        return pltpu.VMEM((cols + modes, count), jnp.bfloat16)

    half_snaps = snaps_dev // 2
    def add_terms(acc, block):
        count = block.shape[0] * half_snaps
        before = [] if acc is None else [acc]
        return pl.pallas_call(
            functools.partial(stack_kernel, cols, len(before)),
            out_shape=acc_shape,
            in_specs=[vmem] * (3 + len(before)),
            out_specs=vmem,
            scratch_shapes=[col_scratch(count)],
            input_output_aliases={2: 0} if before else {},
            compiler_params=params,
            cost_estimate=cost(count),
            name="stack_terms",
        )(left, right, *before, block)

    acc = None
    new = total[None]
    mine = new
    time_bits = (tm_count - 1).bit_length()
    for step in range(time_bits):
        got = exchanged(mine, "tm", step, time_bits, 0)
        acc = add_terms(acc, new)
        got, acc = lax.optimization_barrier((got, acc))
        new = got
        mine = jnp.concatenate([mine, got])
    other = swapped(mine, "space", 1)
    acc = add_terms(acc, new)
    width = 128
    row_chunk = 256
    chunks = pl.cdiv(row_block, row_chunk)
    out_shapes = (
        jax.ShapeDtypeStruct((modes, snaps_dev), jnp.float32),
        jax.ShapeDtypeStruct((modes, snaps_dev), jnp.float32),
        jax.ShapeDtypeStruct((col_block, row_block), jnp.float32),
        jax.ShapeDtypeStruct((modes, row_block), jnp.float32),
    )
    outs = pl.pallas_call(
        functools.partial(last_kernel, row_block, col_block, row_chunk),
        out_shape=out_shapes,
        in_specs=[smem] + [vmem] * 6,
        out_specs=(pl.BlockSpec(memory_space=pltpu.HBM),) * 4,
        scratch_shapes=[
            pltpu.VMEM((2 * tm_count, modes, width), jnp.float32),
            pltpu.VMEM((2 * tm_count, modes, width), jnp.float32),
            col_scratch(tm_count * half_snaps),
            *[pltpu.VMEM(shape.shape, shape.dtype) for shape in out_shapes],
            pltpu.SemaphoreType.DMA((3 + chunks,)),
        ],
        compiler_params=params,
        cost_estimate=cost(tm_count * half_snaps),
        name="last_half",
    )(place, left, right, acc, reg_rows, mine, other)
    return tuple(out.T for out in outs)


def solution(mesh):
    return jax.shard_map(
        local,
        mesh=mesh,
        in_specs=(P("tm", "space"), P("space", None), P()),
        out_specs=(P("tm", None), P("tm", None), P("tm", "space"), P("tm", None)),
        check_vma=False,
    )
```

```python
import functools

import jax
import jax.numpy as jnp
from jax import lax
from jax.experimental import pallas as pl
from jax.experimental.pallas import tpu as pltpu
from jax.sharding import PartitionSpec as P

NT = (((1,), (1,)), ((), ()))


def round_up(value, step):
    return (value + step - 1) // step * step


def tree_sum(terms):
    while len(terms) > 1:
        terms = [terms[i] + terms[i + 1] for i in range(0, len(terms), 2)]
    return terms[0]


def selectors(first, rows, modes, depth):
    feature = first + lax.broadcasted_iota(jnp.int32, (rows, 1), 0)
    mode = lax.broadcasted_iota(jnp.int32, (1, modes), 1)
    start = modes + mode * modes - (mode * (mode - 1)) // 2
    gap = feature - start
    holds = (gap >= 0) & (gap < modes - mode)
    left = jnp.sum(jnp.where(holds, mode, 0), axis=1, keepdims=True)
    right = left + jnp.sum(jnp.where(holds, gap, 0), axis=1, keepdims=True)
    linear = feature < modes
    left = jnp.where(linear, feature, left)
    right = jnp.where(linear, modes, right)
    lane = lax.broadcasted_iota(jnp.int32, (1, depth), 1)
    held = jnp.where(lane < 3 * modes, lax.rem(lane, modes), lane - 2 * modes)
    return (
        jnp.where(held == left, 1.0, 0.0).astype(jnp.bfloat16),
        jnp.where(held == right, 1.0, 0.0).astype(jnp.bfloat16),
    )


def parts_of(block, depth):
    modes, snaps = block.shape
    high = block.astype(jnp.bfloat16)
    rest = block - high.astype(jnp.float32)
    middle = rest.astype(jnp.bfloat16)
    low = (rest - middle.astype(jnp.float32)).astype(jnp.bfloat16)
    tail = depth - 3 * modes
    ones = jnp.where(lax.broadcasted_iota(jnp.int32, (tail, snaps), 0) == 0, 1.0, 0.0)
    return jnp.concatenate([high, middle, low, ones.astype(jnp.bfloat16)], axis=0)


def picked(left, right, parts):
    first = jnp.dot(left, parts, preferred_element_type=jnp.float32)
    second = jnp.dot(right, parts, preferred_element_type=jnp.float32)
    return (first * second).astype(jnp.bfloat16)


def project_kernel(place_ref, basis_ref, snaps_ref, keep_ref, give_ref, basis, held, basis_sem, sems):
    core = place_ref[1] % 2
    chunks, size, states = held.shape
    half = chunks // 2 * size
    basis_copy = pltpu.make_async_copy(basis_ref, basis, basis_sem)
    basis_copy.start()
    copies = []
    for chunk in range(chunks):
        side, at = divmod(chunk * size, half)
        first = pl.multiple_of((core if side else 1 - core) * half + at, size)
        copies.append(
            pltpu.make_async_copy(snaps_ref.at[pl.ds(first, size)], held.at[chunk], sems.at[chunk])
        )
        copies[-1].start()
    basis_copy.wait()
    pieces = 4
    step = states // pieces
    for chunk in range(chunks):
        copies[chunk].wait()
        terms = [
            lax.dot_general(
                basis[:, piece * step : (piece + 1) * step],
                held[chunk, :, piece * step : (piece + 1) * step],
                NT,
                preferred_element_type=jnp.float32,
            )
            for piece in range(pieces)
        ]
        side, at = divmod(chunk * size, half)
        (keep_ref if side else give_ref)[:, at : at + size] = tree_sum(terms)


def project(place, snapshots, basis):
    snaps, states = snapshots.shape
    modes = basis.shape[0]
    size = 128
    hbm = pl.BlockSpec(memory_space=pltpu.HBM)
    vmem = pl.BlockSpec(memory_space=pltpu.VMEM)
    block = jax.ShapeDtypeStruct((modes, snaps // 2), jnp.float32)
    return pl.pallas_call(
        project_kernel,
        out_shape=(block, block),
        in_specs=[pl.BlockSpec(memory_space=pltpu.SMEM), hbm, hbm],
        out_specs=(vmem, vmem),
        scratch_shapes=[
            pltpu.VMEM(basis.shape, basis.dtype),
            pltpu.VMEM((snaps // size, size, states), snapshots.dtype),
            pltpu.SemaphoreType.DMA,
            pltpu.SemaphoreType.DMA((snaps // size,)),
        ],
        compiler_params=pltpu.CompilerParams(vmem_limit_bytes=55000 * 1024),
        name="project",
    )(place, basis, snapshots)


def selector_kernel(row_block, col_block, modes, place_ref, left_ref, right_ref):
    cols = round_up(col_block, 16)
    rows = left_ref.shape[0] - cols
    depth = left_ref.shape[1]
    for at, size, first in (
        (0, cols, place_ref[1] * col_block),
        (cols, rows, place_ref[0] * row_block),
    ):
        left, right = selectors(first, size, modes, depth)
        left_ref[at : at + size] = left
        right_ref[at : at + size] = right


def inner_rates(block, half):
    snaps = block.shape[1]
    lane = lax.rem(lax.broadcasted_iota(jnp.int32, (1, snaps), 1), half)
    rates = (pltpu.roll(block, snaps - 1, 1) - pltpu.roll(block, 1, 1)) * 0.5
    return jnp.where((lane == 0) | (lane == half - 1), 0.0, rates)


def column_side(left_ref, right_ref, parts, rates, cols, col_scratch):
    col_scratch[:cols, : rates.shape[1]] = picked(left_ref[:cols], right_ref[:cols], parts)
    col_scratch[cols:, : rates.shape[1]] = rates.astype(jnp.bfloat16)


def terms_of(left_ref, right_ref, block, half, cols, col_scratch):
    parts = parts_of(block, left_ref.shape[1])
    column_side(left_ref, right_ref, parts, inner_rates(block, half), cols, col_scratch)
    row_features = picked(left_ref[cols:], right_ref[cols:], parts)
    return lax.dot_general(
        col_scratch[:, : block.shape[1]], row_features, NT, preferred_element_type=jnp.float32
    )


def joined(refs):
    halves = []
    for ref in refs:
        halves.extend([ref[...]] if len(ref.shape) == 2 else [ref[slot] for slot in range(ref.shape[0])])
    return jnp.concatenate(halves, axis=1)


def halves_kernel(cols, has_before, left_ref, right_ref, *refs):
    before_ref, refs = (refs[0], refs[1:]) if has_before else (None, refs)
    block_refs, acc_ref, col_scratch = refs[:-2], refs[-2], refs[-1]
    half = block_refs[0].shape[-1]
    block = joined(block_refs)
    term = terms_of(left_ref, right_ref, block, half, cols, col_scratch)
    acc_ref[...] = before_ref[...] + term if has_before else term


def edge_columns(time_idx, core, halves, starts, ends):
    count, modes, width = starts.shape
    for offset, side, load in halves:
        block = load()
        at = 2 * (time_idx ^ offset) + side
        starts[at] = block[:, :width]
        ends[at] = block[:, block.shape[1] - width :]
    lane = lax.broadcasted_iota(jnp.int32, (1, width), 1)
    heads = jnp.zeros((modes, width), jnp.float32)
    tails = jnp.zeros((modes, width), jnp.float32)
    for at in range(count):
        pair = (lane == 2 * at) | (lane == 2 * at + 1)
        heads = jnp.where(pair, pltpu.roll(starts[at], 2 * at, 1), heads)
        tails = jnp.where(pair, pltpu.roll(ends[at], (2 * at + 2) % width, 1), tails)
    after = pltpu.roll(heads, width - 1, 1)
    before = pltpu.roll(tails, 1, 1)
    rates = (after - before) * 0.5
    rates = jnp.where(lane == 0, after - heads, rates)
    rates = jnp.where(lane == 2 * count - 1, tails - before, rates)
    edge = jnp.where(lax.rem(lane, 2) == 0, heads, tails)
    inside = lane < 2 * count
    return jnp.where(inside, edge, 0.0), jnp.where(inside, rates, 0.0)


def last_kernel(
    row_block, col_block, row_chunk, offsets, place_ref, left_ref, right_ref, before_ref, reg_ref, early_ref,
    early_other_ref, late_ref, late_other_ref, reduced_ref, rates_ref, normal_ref, right_side_ref, starts,
    ends, col_scratch, reduced_out, rates_out, normal_out, right_side_out, sems,
):
    time_idx = place_ref[0]
    space_idx = place_ref[1]
    core = space_idx % 2
    early, modes, half = early_ref.shape
    groups = early + late_ref.shape[0]
    snaps = 2 * half
    cols = round_up(col_block, 16)
    depth = left_ref.shape[1]
    copies = []

    def send(source, target):
        copies.append(pltpu.make_async_copy(source, target, sems.at[len(copies)]))
        copies[-1].start()

    reduced_out[:, pl.ds(pl.multiple_of(core * half, half), half)] = early_ref[0]
    reduced_out[:, pl.ds(pl.multiple_of((1 - core) * half, half), half)] = early_other_ref[0]
    send(reduced_out, reduced_ref)
    halves = []
    for slot, offset in enumerate(offsets):
        for side, pair in ((core, (early_ref, late_ref)), (1 - core, (early_other_ref, late_other_ref))):
            ref, at = (pair[0], slot) if slot < early else (pair[1], slot - early)
            halves.append((offset, side, functools.partial(lambda ref, at: ref[at], ref, at)))
    edge, edge_rates = edge_columns(time_idx, core, halves, starts, ends)
    own = reduced_out[...]
    width = edge.shape[1]
    own_edges = pltpu.roll(edge_rates, lax.rem(width - 4 * time_idx, width), 1)
    lane = lax.broadcasted_iota(jnp.int32, (1, snaps), 1)
    rates = jnp.where(lane == 0, own_edges[:, 0:1], inner_rates(own, snaps))
    rates_out[...] = jnp.where(lane == snaps - 1, own_edges[:, 3:4], rates)
    send(rates_out, rates_ref)

    block = joined([late_other_ref])
    parts = parts_of(block, depth)
    column_side(left_ref, right_ref, parts, inner_rates(block, half), cols, col_scratch)
    scale = 1.0 / (groups * snaps)
    chunks = [(at, min(row_chunk, row_block - at)) for at in range(0, row_block, row_chunk)]
    edge_parts = parts_of(edge, depth)
    edge_rates = edge_rates.astype(jnp.bfloat16)
    for at, size in chunks:
        pick = slice(cols + at, cols + at + round_up(size, 16))
        features = picked(left_ref[pick], right_ref[pick], parts)
        edge_features = picked(left_ref[pick], right_ref[pick], edge_parts)
        total = before_ref[:, at : at + features.shape[0]] + lax.dot_general(
            col_scratch[...], features, NT, preferred_element_type=jnp.float32
        )
        edge_total = lax.dot_general(edge_rates, edge_features, NT, preferred_element_type=jnp.float32)
        col_ids = space_idx * col_block + lax.broadcasted_iota(jnp.int32, (col_block, size), 0)
        row_ids = time_idx * row_block + at + lax.broadcasted_iota(jnp.int32, (col_block, size), 1)
        diagonal = jnp.where(row_ids == col_ids, reg_ref[:, at : at + size], 0.0)
        normal_out[:, at : at + size] = total[:col_block, :size] * scale + diagonal
        right_side_out[:, at : at + size] = (total[cols:] + edge_total)[:, :size] * scale
        send(normal_out.at[:, at : at + size], normal_ref.at[:, at : at + size])
    send(right_side_out, right_side_ref)
    for copy in copies:
        copy.wait()


def swapped(value, axis, distance):
    return lax.ppermute(value, axis, [(i, i ^ distance) for i in range(lax.axis_size(axis))])


def local(snapshots, modes_basis, reg_weights):
    feature_count = reg_weights.shape[0]
    snaps_dev = snapshots.shape[0]
    modes = modes_basis.shape[1]
    tm_count = lax.axis_size("tm")
    space_count = lax.axis_size("space")
    row_block = feature_count // tm_count
    col_block = feature_count // space_count
    rows = round_up(row_block, 16)
    cols = round_up(col_block, 16)
    depth = round_up(3 * modes + 1, 128)
    time_idx = lax.axis_index("tm")
    space_idx = lax.axis_index("space")
    place = jnp.stack([time_idx, space_idx]).astype(jnp.int32)
    smem = pl.BlockSpec(memory_space=pltpu.SMEM)
    vmem = pl.BlockSpec(memory_space=pltpu.VMEM)
    params = pltpu.CompilerParams(vmem_limit_bytes=32 * 1024 * 1024)

    keep, give = project(place, snapshots, modes_basis.T)
    half = keep + swapped(give, "space", 1)
    after, half = lax.optimization_barrier((place, half))
    selector = jax.ShapeDtypeStruct((cols + rows, depth), jnp.bfloat16)
    left, right = pl.pallas_call(
        functools.partial(selector_kernel, row_block, col_block, modes),
        out_shape=(selector, selector),
        in_specs=[smem],
        out_specs=(vmem, vmem),
        compiler_params=params,
        cost_estimate=pl.CostEstimate(flops=10**6, bytes_accessed=10**6, transcendentals=0),
        name="selectors",
    )(after)
    first_row = after[0] * row_block
    reg_rows = lax.dynamic_slice_in_dim(reg_weights, first_row, row_block, 0)[None]

    terms = [half] + [swapped(half, "space", step) for step in range(2, space_count, 2)]
    while len(terms) > 1:
        terms = [terms[i] + terms[i + 1] for i in range(0, len(terms), 2)]
    mine, left, right, reg_rows = lax.optimization_barrier((terms[0], left, right, reg_rows))
    arriving = [(step, swapped(mine, "tm", step)) for step in range(tm_count - 1, 0, -1)]
    acc_shape = jax.ShapeDtypeStruct((cols + modes, rows), jnp.float32)

    def cost(count):
        flops = 2 * count * (2 * depth * (cols + rows) + (cols + modes) * rows)
        return pl.CostEstimate(flops=flops, bytes_accessed=2 * 10**6, transcendentals=0)

    def col_scratch(count):
        return pltpu.VMEM((cols + modes, count), jnp.bfloat16)

    half_snaps = snaps_dev // 2

    def add_terms(acc, blocks):
        count = sum(block.size for block in blocks) // modes
        before = [] if acc is None else [acc]
        return pl.pallas_call(
            functools.partial(halves_kernel, cols, len(before)),
            out_shape=acc_shape,
            in_specs=[vmem] * (2 + len(before) + len(blocks)),
            out_specs=vmem,
            scratch_shapes=[col_scratch(count)],
            input_output_aliases={2: 0} if before else {},
            compiler_params=params,
            cost_estimate=cost(count),
            name="halves",
        )(left, right, *before, *blocks)

    offsets = [0] + [offset for offset, _ in arriving]
    early = [mine, arriving[0][1]]
    late = [got for _, got in arriving[1:]]
    acc = add_terms(None, [mine])
    early_stack = jnp.stack(early)
    early_other = swapped(early_stack, "space", 1)
    acc = add_terms(acc, early[1:])
    acc, *late = lax.optimization_barrier((acc, *late))
    late_stack = jnp.stack(late)
    late_other = swapped(late_stack, "space", 1)
    acc = add_terms(acc, [early_other, late_stack])
    width = 128
    row_chunk = 256
    chunks = pl.cdiv(row_block, row_chunk)
    out_shapes = (
        jax.ShapeDtypeStruct((modes, snaps_dev), jnp.float32),
        jax.ShapeDtypeStruct((modes, snaps_dev), jnp.float32),
        jax.ShapeDtypeStruct((col_block, row_block), jnp.float32),
        jax.ShapeDtypeStruct((modes, row_block), jnp.float32),
    )
    outs = pl.pallas_call(
        functools.partial(last_kernel, row_block, col_block, row_chunk, offsets),
        out_shape=out_shapes,
        in_specs=[smem] + [vmem] * 8,
        out_specs=(pl.BlockSpec(memory_space=pltpu.HBM),) * 4,
        scratch_shapes=[
            pltpu.VMEM((2 * tm_count, modes, width), jnp.float32),
            pltpu.VMEM((2 * tm_count, modes, width), jnp.float32),
            col_scratch(len(late) * half_snaps),
            *[pltpu.VMEM(shape.shape, shape.dtype) for shape in out_shapes],
            pltpu.SemaphoreType.DMA((3 + chunks,)),
        ],
        compiler_params=params,
        cost_estimate=cost(len(late) * half_snaps),
        name="last_half",
    )(place, left, right, acc, reg_rows, early_stack, early_other, late_stack, late_other)
    return tuple(out.T for out in outs)


def solution(mesh):
    return jax.shard_map(
        local,
        mesh=mesh,
        in_specs=(P("tm", "space"), P("space", None), P()),
        out_specs=(P("tm", None), P("tm", None), P("tm", "space"), P("tm", None)),
        check_vma=False,
    )
```

```python
import functools

import jax
import jax.numpy as jnp
from jax import lax
from jax.experimental import pallas as pl
from jax.experimental.pallas import tpu as pltpu
from jax.sharding import PartitionSpec as P

NT = (((1,), (1,)), ((), ()))


def round_up(value, step):
    return (value + step - 1) // step * step


def tree_sum(terms):
    while len(terms) > 1:
        terms = [terms[i] + terms[i + 1] for i in range(0, len(terms), 2)]
    return terms[0]


def selectors(first, rows, modes, depth):
    feature = first + lax.broadcasted_iota(jnp.int32, (rows, 1), 0)
    mode = lax.broadcasted_iota(jnp.int32, (1, modes), 1)
    start = modes + mode * modes - (mode * (mode - 1)) // 2
    gap = feature - start
    holds = (gap >= 0) & (gap < modes - mode)
    left = jnp.sum(jnp.where(holds, mode, 0), axis=1, keepdims=True)
    right = left + jnp.sum(jnp.where(holds, gap, 0), axis=1, keepdims=True)
    linear = feature < modes
    left = jnp.where(linear, feature, left)
    right = jnp.where(linear, modes, right)
    lane = lax.broadcasted_iota(jnp.int32, (1, depth), 1)
    held = jnp.where(lane < 3 * modes, lax.rem(lane, modes), lane - 2 * modes)
    return (
        jnp.where(held == left, 1.0, 0.0).astype(jnp.bfloat16),
        jnp.where(held == right, 1.0, 0.0).astype(jnp.bfloat16),
    )


def parts_of(block, depth):
    modes, snaps = block.shape
    high = block.astype(jnp.bfloat16)
    rest = block - high.astype(jnp.float32)
    middle = rest.astype(jnp.bfloat16)
    low = (rest - middle.astype(jnp.float32)).astype(jnp.bfloat16)
    tail = depth - 3 * modes
    ones = jnp.where(lax.broadcasted_iota(jnp.int32, (tail, snaps), 0) == 0, 1.0, 0.0)
    return jnp.concatenate([high, middle, low, ones.astype(jnp.bfloat16)], axis=0)


def picked(left, right, parts):
    first = jnp.dot(left, parts, preferred_element_type=jnp.float32)
    second = jnp.dot(right, parts, preferred_element_type=jnp.float32)
    return (first * second).astype(jnp.bfloat16)


def project_kernel(place_ref, basis_ref, snaps_ref, keep_ref, give_ref, basis, held, basis_sem, sems):
    core = place_ref[1] % 2
    chunks, size, states = held.shape
    half = chunks // 2 * size
    parts = sems.shape[1]
    rows = size // parts
    basis_copy = pltpu.make_async_copy(basis_ref, basis, basis_sem)
    basis_copy.start(priority=1)
    copies = []
    for chunk in range(chunks):
        side, at = divmod(chunk * size, half)
        first = (core if side else 1 - core) * half + at
        for part in range(parts):
            copies.append(
                pltpu.make_async_copy(
                    snaps_ref.at[pl.ds(pl.multiple_of(first + part * rows, rows), rows)],
                    held.at[chunk, pl.ds(part * rows, rows)],
                    sems.at[chunk, part],
                )
            )
            copies[-1].start(priority=part % 2)
    basis_copy.wait()
    pieces = 4
    step = states // pieces
    for chunk in range(chunks):
        for copy in copies[chunk * parts : (chunk + 1) * parts]:
            copy.wait()
        terms = [
            lax.dot_general(
                basis[:, piece * step : (piece + 1) * step],
                held[chunk, :, piece * step : (piece + 1) * step],
                NT,
                preferred_element_type=jnp.float32,
            )
            for piece in range(pieces)
        ]
        side, at = divmod(chunk * size, half)
        (keep_ref if side else give_ref)[:, at : at + size] = tree_sum(terms)


def project(place, snapshots, basis):
    snaps, states = snapshots.shape
    modes = basis.shape[0]
    size = 128
    hbm = pl.BlockSpec(memory_space=pltpu.HBM)
    vmem = pl.BlockSpec(memory_space=pltpu.VMEM)
    block = jax.ShapeDtypeStruct((modes, snaps // 2), jnp.float32)
    return pl.pallas_call(
        project_kernel,
        out_shape=(block, block),
        in_specs=[pl.BlockSpec(memory_space=pltpu.SMEM), hbm, hbm],
        out_specs=(vmem, vmem),
        scratch_shapes=[
            pltpu.VMEM(basis.shape, basis.dtype),
            pltpu.VMEM((snaps // size, size, states), snapshots.dtype),
            pltpu.SemaphoreType.DMA,
            pltpu.SemaphoreType.DMA((snaps // size, 2)),
        ],
        compiler_params=pltpu.CompilerParams(vmem_limit_bytes=55000 * 1024),
        name="project",
    )(place, basis, snapshots)


def selector_kernel(row_block, col_block, modes, place_ref, left_ref, right_ref):
    cols = round_up(col_block, 16)
    rows = left_ref.shape[0] - cols
    depth = left_ref.shape[1]
    for at, size, first in (
        (0, cols, place_ref[1] * col_block),
        (cols, rows, place_ref[0] * row_block),
    ):
        left, right = selectors(first, size, modes, depth)
        left_ref[at : at + size] = left
        right_ref[at : at + size] = right


def inner_rates(block, half):
    snaps = block.shape[1]
    lane = lax.rem(lax.broadcasted_iota(jnp.int32, (1, snaps), 1), half)
    rates = (pltpu.roll(block, snaps - 1, 1) - pltpu.roll(block, 1, 1)) * 0.5
    return jnp.where((lane == 0) | (lane == half - 1), 0.0, rates)


def column_side(left_ref, right_ref, parts, rates, cols, col_scratch):
    col_scratch[:cols, : rates.shape[1]] = picked(left_ref[:cols], right_ref[:cols], parts)
    col_scratch[cols:, : rates.shape[1]] = rates.astype(jnp.bfloat16)


def terms_of(left_ref, right_ref, block, half, cols, col_scratch):
    parts = parts_of(block, left_ref.shape[1])
    column_side(left_ref, right_ref, parts, inner_rates(block, half), cols, col_scratch)
    row_features = picked(left_ref[cols:], right_ref[cols:], parts)
    return lax.dot_general(
        col_scratch[:, : block.shape[1]], row_features, NT, preferred_element_type=jnp.float32
    )


def joined(refs):
    halves = []
    for ref in refs:
        halves.extend([ref[...]] if len(ref.shape) == 2 else [ref[slot] for slot in range(ref.shape[0])])
    return jnp.concatenate(halves, axis=1)


def halves_kernel(cols, has_before, left_ref, right_ref, *refs):
    before_ref, refs = (refs[0], refs[1:]) if has_before else (None, refs)
    block_refs, acc_ref, col_scratch = refs[:-2], refs[-2], refs[-1]
    block = joined(block_refs)
    term = terms_of(left_ref, right_ref, block, block_refs[0].shape[-1], cols, col_scratch)
    acc_ref[...] = before_ref[...] + term if has_before else term


def own_kernel(
    cols, place_ref, left_ref, right_ref, before_ref, early_ref, other_ref, late_ref, acc_ref, reduced_ref,
    col_scratch, reduced_out, sem,
):
    core = place_ref[1] % 2
    half = early_ref.shape[-1]
    reduced_out[:, pl.ds(pl.multiple_of(core * half, half), half)] = early_ref[0]
    reduced_out[:, pl.ds(pl.multiple_of((1 - core) * half, half), half)] = other_ref[0]
    copy = pltpu.make_async_copy(reduced_out, reduced_ref, sem)
    copy.start()
    block = joined([other_ref, late_ref])
    acc_ref[...] = before_ref[...] + terms_of(left_ref, right_ref, block, half, cols, col_scratch)
    copy.wait()


def edge_columns(time_idx, core, halves, starts, ends):
    count, modes, width = starts.shape
    for offset, side, load in halves:
        block = load()
        at = 2 * (time_idx ^ offset) + side
        starts[at] = block[:, :width]
        ends[at] = block[:, block.shape[1] - width :]
    lane = lax.broadcasted_iota(jnp.int32, (1, width), 1)
    heads = jnp.zeros((modes, width), jnp.float32)
    tails = jnp.zeros((modes, width), jnp.float32)
    for at in range(count):
        pair = (lane == 2 * at) | (lane == 2 * at + 1)
        heads = jnp.where(pair, pltpu.roll(starts[at], 2 * at, 1), heads)
        tails = jnp.where(pair, pltpu.roll(ends[at], (2 * at + 2) % width, 1), tails)
    after = pltpu.roll(heads, width - 1, 1)
    before = pltpu.roll(tails, 1, 1)
    rates = (after - before) * 0.5
    rates = jnp.where(lane == 0, after - heads, rates)
    rates = jnp.where(lane == 2 * count - 1, tails - before, rates)
    edge = jnp.where(lax.rem(lane, 2) == 0, heads, tails)
    inside = lane < 2 * count
    return jnp.where(inside, edge, 0.0), jnp.where(inside, rates, 0.0)


def last_kernel(
    row_block, col_block, chunks, offsets, place_ref, left_ref, right_ref, before_ref, reg_ref, early_ref,
    early_other_ref, late_ref, late_other_ref, rates_ref, normal_ref, right_side_ref, starts, ends,
    col_scratch, rates_out, normal_out, right_side_out, sems,
):
    time_idx = place_ref[0]
    space_idx = place_ref[1]
    core = space_idx % 2
    early, modes, half = early_ref.shape
    groups = early + late_ref.shape[0]
    snaps = 2 * half
    cols = round_up(col_block, 16)
    depth = left_ref.shape[1]
    copies = []

    def send(source, target):
        copies.append(pltpu.make_async_copy(source, target, sems.at[len(copies)]))
        copies[-1].start()

    rates_out[:, pl.ds(pl.multiple_of(core * half, half), half)] = early_ref[0]
    rates_out[:, pl.ds(pl.multiple_of((1 - core) * half, half), half)] = early_other_ref[0]
    halves = []
    for slot, offset in enumerate(offsets):
        for side, pair in ((core, (early_ref, late_ref)), (1 - core, (early_other_ref, late_other_ref))):
            ref, at = (pair[0], slot) if slot < early else (pair[1], slot - early)
            halves.append((offset, side, functools.partial(lambda ref, at: ref[at], ref, at)))
    edge, edge_rates = edge_columns(time_idx, core, halves, starts, ends)
    own = rates_out[...]
    width = edge.shape[1]
    own_edges = pltpu.roll(edge_rates, lax.rem(width - 4 * time_idx, width), 1)
    lane = lax.broadcasted_iota(jnp.int32, (1, snaps), 1)
    rates = jnp.where(lane == 0, own_edges[:, 0:1], inner_rates(own, snaps))
    rates_out[...] = jnp.where(lane == snaps - 1, own_edges[:, 3:4], rates)
    send(rates_out, rates_ref)

    block = joined([late_other_ref])
    parts = parts_of(block, depth)
    column_side(left_ref, right_ref, parts, inner_rates(block, half), cols, col_scratch)
    scale = 1.0 / (groups * snaps)
    edge_parts = parts_of(edge, depth)
    edge_rates = edge_rates.astype(jnp.bfloat16)
    for at, size in chunks:
        pick = slice(cols + at, cols + at + round_up(size, 16))
        features = picked(left_ref[pick], right_ref[pick], parts)
        edge_features = picked(left_ref[pick], right_ref[pick], edge_parts)
        total = before_ref[:, at : at + features.shape[0]] + lax.dot_general(
            col_scratch[...], features, NT, preferred_element_type=jnp.float32
        )
        edge_total = lax.dot_general(edge_rates, edge_features, NT, preferred_element_type=jnp.float32)
        col_ids = space_idx * col_block + lax.broadcasted_iota(jnp.int32, (col_block, size), 0)
        row_ids = time_idx * row_block + at + lax.broadcasted_iota(jnp.int32, (col_block, size), 1)
        diagonal = jnp.where(row_ids == col_ids, reg_ref[:, at : at + size], 0.0)
        normal_out[:, at : at + size] = total[:col_block, :size] * scale + diagonal
        right_side_out[:, at : at + size] = (total[cols:] + edge_total)[:, :size] * scale
        send(normal_out.at[:, at : at + size], normal_ref.at[:, at : at + size])
        send(right_side_out.at[:, at : at + size], right_side_ref.at[:, at : at + size])
    for copy in copies:
        copy.wait()


def swapped(value, axis, distance):
    return lax.ppermute(value, axis, [(i, i ^ distance) for i in range(lax.axis_size(axis))])


def local(snapshots, modes_basis, reg_weights):
    feature_count = reg_weights.shape[0]
    snaps_dev = snapshots.shape[0]
    modes = modes_basis.shape[1]
    tm_count = lax.axis_size("tm")
    space_count = lax.axis_size("space")
    row_block = feature_count // tm_count
    col_block = feature_count // space_count
    rows = round_up(row_block, 16)
    cols = round_up(col_block, 16)
    depth = round_up(3 * modes + 1, 128)
    time_idx = lax.axis_index("tm")
    space_idx = lax.axis_index("space")
    place = jnp.stack([time_idx, space_idx]).astype(jnp.int32)
    smem = pl.BlockSpec(memory_space=pltpu.SMEM)
    vmem = pl.BlockSpec(memory_space=pltpu.VMEM)
    hbm = pl.BlockSpec(memory_space=pltpu.HBM)
    params = pltpu.CompilerParams(vmem_limit_bytes=32 * 1024 * 1024)

    keep, give = project(place, snapshots, modes_basis.T)
    half = keep + swapped(give, "space", 1)
    after, half = lax.optimization_barrier((place, half))
    selector = jax.ShapeDtypeStruct((cols + rows, depth), jnp.bfloat16)
    left, right = pl.pallas_call(
        functools.partial(selector_kernel, row_block, col_block, modes),
        out_shape=(selector, selector),
        in_specs=[smem],
        out_specs=(vmem, vmem),
        compiler_params=params,
        cost_estimate=pl.CostEstimate(flops=10**6, bytes_accessed=10**6, transcendentals=0),
        name="selectors",
    )(after)
    first_row = after[0] * row_block
    reg_rows = lax.dynamic_slice_in_dim(reg_weights, first_row, row_block, 0)[None]

    terms = [half] + [swapped(half, "space", step) for step in range(2, space_count, 2)]
    while len(terms) > 1:
        terms = [terms[i] + terms[i + 1] for i in range(0, len(terms), 2)]
    mine, left, right, reg_rows = lax.optimization_barrier((terms[0], left, right, reg_rows))
    arriving = [(step, swapped(mine, "tm", step)) for step in range(tm_count - 1, 0, -1)]
    acc_shape = jax.ShapeDtypeStruct((cols + modes, rows), jnp.float32)

    def cost(count):
        flops = 2 * count * (2 * depth * (cols + rows) + (cols + modes) * rows)
        return pl.CostEstimate(flops=flops, bytes_accessed=2 * 10**6, transcendentals=0)

    def col_scratch(count):
        return pltpu.VMEM((cols + modes, count), jnp.bfloat16)

    half_snaps = snaps_dev // 2

    def add_terms(acc, blocks):
        count = sum(block.size for block in blocks) // modes
        before = [] if acc is None else [acc]
        return pl.pallas_call(
            functools.partial(halves_kernel, cols, len(before)),
            out_shape=acc_shape,
            in_specs=[vmem] * (2 + len(before) + len(blocks)),
            out_specs=vmem,
            scratch_shapes=[col_scratch(count)],
            input_output_aliases={2: 0} if before else {},
            compiler_params=params,
            cost_estimate=cost(count),
            name="halves",
        )(left, right, *before, *blocks)

    offsets = [0] + [offset for offset, _ in arriving]
    early = [mine, arriving[0][1]]
    late = [got for _, got in arriving[1:]]
    acc = add_terms(None, [mine])
    early_stack = jnp.stack(early)
    early_other = swapped(early_stack, "space", 1)
    acc = add_terms(acc, early[1:])
    acc, *late = lax.optimization_barrier((acc, *late))
    late_stack = jnp.stack(late)
    late_other = swapped(late_stack, "space", 1)
    block_shape = jax.ShapeDtypeStruct((modes, snaps_dev), jnp.float32)
    count = tm_count * half_snaps
    acc, reduced = pl.pallas_call(
        functools.partial(own_kernel, cols),
        out_shape=(acc_shape, block_shape),
        in_specs=[smem] + [vmem] * 6,
        out_specs=(vmem, hbm),
        scratch_shapes=[
            col_scratch(count),
            pltpu.VMEM(block_shape.shape, block_shape.dtype),
            pltpu.SemaphoreType.DMA,
        ],
        input_output_aliases={3: 0},
        compiler_params=params,
        cost_estimate=cost(count),
        name="own_and_late",
    )(place, left, right, acc, early_stack, early_other, late_stack)
    width = 128
    starts = list(range(0, row_block - width, 2 * width))
    starts = [0] + [start - width for start in starts[1:]] if len(starts) > 1 else [0]
    ends = starts[1:] + [row_block]
    chunks = [(start, end - start) for start, end in zip(starts, ends)][::-1]
    out_shapes = (
        block_shape,
        jax.ShapeDtypeStruct((col_block, row_block), jnp.float32),
        jax.ShapeDtypeStruct((modes, row_block), jnp.float32),
    )
    outs = pl.pallas_call(
        functools.partial(last_kernel, row_block, col_block, chunks, offsets),
        out_shape=out_shapes,
        in_specs=[smem] + [vmem] * 8,
        out_specs=(hbm,) * 3,
        scratch_shapes=[
            pltpu.VMEM((2 * tm_count, modes, width), jnp.float32),
            pltpu.VMEM((2 * tm_count, modes, width), jnp.float32),
            col_scratch(len(late) * half_snaps),
            *[pltpu.VMEM(shape.shape, shape.dtype) for shape in out_shapes],
            pltpu.SemaphoreType.DMA((1 + 2 * len(chunks),)),
        ],
        compiler_params=params,
        cost_estimate=cost(len(late) * half_snaps),
        name="last_half",
    )(place, left, right, acc, reg_rows, early_stack, early_other, late_stack, late_other)
    return tuple(out.T for out in (reduced, *outs))


def solution(mesh):
    return jax.shard_map(
        local,
        mesh=mesh,
        in_specs=(P("tm", "space"), P("space", None), P()),
        out_specs=(P("tm", None), P("tm", None), P("tm", "space"), P("tm", None)),
        check_vma=False,
    )
```

```python
import functools

import jax
import jax.numpy as jnp
from jax import lax
from jax.experimental import pallas as pl
from jax.experimental.pallas import tpu as pltpu
from jax.sharding import PartitionSpec as P

NT = (((1,), (1,)), ((), ()))


def round_up(value, step):
    return (value + step - 1) // step * step


def tree_sum(terms):
    while len(terms) > 1:
        terms = [terms[i] + terms[i + 1] for i in range(0, len(terms), 2)]
    return terms[0]


def selectors(first, rows, modes, depth):
    feature = first + lax.broadcasted_iota(jnp.int32, (rows, 1), 0)
    mode = lax.broadcasted_iota(jnp.int32, (1, modes), 1)
    start = modes + mode * modes - (mode * (mode - 1)) // 2
    gap = feature - start
    holds = (gap >= 0) & (gap < modes - mode)
    left = jnp.sum(jnp.where(holds, mode, 0), axis=1, keepdims=True)
    right = left + jnp.sum(jnp.where(holds, gap, 0), axis=1, keepdims=True)
    linear = feature < modes
    left = jnp.where(linear, feature, left)
    right = jnp.where(linear, modes, right)
    lane = lax.broadcasted_iota(jnp.int32, (1, depth), 1)
    held = jnp.where(lane < 3 * modes, lax.rem(lane, modes), lane - 2 * modes)
    return (
        jnp.where(held == left, 1.0, 0.0).astype(jnp.bfloat16),
        jnp.where(held == right, 1.0, 0.0).astype(jnp.bfloat16),
    )


def parts_of(block, depth):
    modes, snaps = block.shape
    high = block.astype(jnp.bfloat16)
    rest = block - high.astype(jnp.float32)
    middle = rest.astype(jnp.bfloat16)
    low = (rest - middle.astype(jnp.float32)).astype(jnp.bfloat16)
    tail = depth - 3 * modes
    ones = jnp.where(lax.broadcasted_iota(jnp.int32, (tail, snaps), 0) == 0, 1.0, 0.0)
    return jnp.concatenate([high, middle, low, ones.astype(jnp.bfloat16)], axis=0)


def picked(left, right, parts):
    first = jnp.dot(left, parts, preferred_element_type=jnp.float32)
    second = jnp.dot(right, parts, preferred_element_type=jnp.float32)
    return (first * second).astype(jnp.bfloat16)


def project_kernel(basis_ref, snaps_ref, keep_ref, give_ref, basis, held, basis_sem, sems):
    core = lax.axis_index("space") % 2
    chunks, size, states = held.shape
    half = chunks // 2 * size
    basis_copy = pltpu.make_async_copy(basis_ref, basis, basis_sem)
    basis_copy.start()
    copies = []
    for chunk in range(chunks):
        side, at = divmod(chunk * size, half)
        first = pl.multiple_of((core if side else 1 - core) * half + at, size)
        copies.append(
            pltpu.make_async_copy(snaps_ref.at[pl.ds(first, size)], held.at[chunk], sems.at[chunk])
        )
        copies[-1].start()
    basis_copy.wait()
    pieces = 4
    step = states // pieces
    for chunk in range(chunks):
        copies[chunk].wait()
        terms = [
            lax.dot_general(
                held[chunk, :, piece * step : (piece + 1) * step],
                basis[:, piece * step : (piece + 1) * step],
                NT,
                preferred_element_type=jnp.float32,
            )
            for piece in range(pieces)
        ]
        side, at = divmod(chunk * size, half)
        (keep_ref if side else give_ref)[:, at : at + size] = tree_sum(terms).T


def project(snapshots, basis):
    snaps, states = snapshots.shape
    modes = basis.shape[0]
    size = 128
    hbm = pl.BlockSpec(memory_space=pltpu.HBM)
    vmem = pl.BlockSpec(memory_space=pltpu.VMEM)
    block = jax.ShapeDtypeStruct((modes, snaps // 2), jnp.float32)
    return pl.pallas_call(
        project_kernel,
        out_shape=(block, block),
        in_specs=[hbm, hbm],
        out_specs=(vmem, vmem),
        scratch_shapes=[
            pltpu.VMEM(basis.shape, basis.dtype),
            pltpu.VMEM((snaps // size, size, states), snapshots.dtype),
            pltpu.SemaphoreType.DMA,
            pltpu.SemaphoreType.DMA((snaps // size,)),
        ],
        compiler_params=pltpu.CompilerParams(vmem_limit_bytes=55000 * 1024),
        name="project",
    )(basis, snapshots)


def selector_kernel(row_block, col_block, after_ref, left_ref, right_ref):
    modes = after_ref.shape[0]
    cols = round_up(col_block, 16)
    rows = left_ref.shape[0] - cols
    depth = left_ref.shape[1]
    for at, size, first in (
        (0, cols, lax.axis_index("space") * col_block),
        (cols, rows, lax.axis_index("tm") * row_block),
    ):
        left, right = selectors(first, size, modes, depth)
        left_ref[at : at + size] = left
        right_ref[at : at + size] = right


def inner_rates(block, half):
    snaps = block.shape[1]
    lane = lax.rem(lax.broadcasted_iota(jnp.int32, (1, snaps), 1), half)
    rates = (pltpu.roll(block, snaps - 1, 1) - pltpu.roll(block, 1, 1)) * 0.5
    return jnp.where((lane == 0) | (lane == half - 1), 0.0, rates)


def column_side(left_ref, right_ref, parts, rates, cols, col_scratch):
    col_scratch[:cols, : rates.shape[1]] = picked(left_ref[:cols], right_ref[:cols], parts)
    col_scratch[cols:, : rates.shape[1]] = rates.astype(jnp.bfloat16)


def terms_of(left_ref, right_ref, block, half, cols, col_scratch):
    parts = parts_of(block, left_ref.shape[1])
    column_side(left_ref, right_ref, parts, inner_rates(block, half), cols, col_scratch)
    row_features = picked(left_ref[cols:], right_ref[cols:], parts)
    return lax.dot_general(
        col_scratch[:, : block.shape[1]], row_features, NT, preferred_element_type=jnp.float32
    )


def joined(refs):
    halves = []
    for ref in refs:
        halves.extend([ref[...]] if len(ref.shape) == 2 else [ref[slot] for slot in range(ref.shape[0])])
    return jnp.concatenate(halves, axis=1)


def halves_kernel(cols, has_before, left_ref, right_ref, *refs):
    before_ref, refs = (refs[0], refs[1:]) if has_before else (None, refs)
    block_refs, acc_ref, col_scratch = refs[:-2], refs[-2], refs[-1]
    block = joined(block_refs)
    term = terms_of(left_ref, right_ref, block, block_refs[0].shape[-1], cols, col_scratch)
    acc_ref[...] = before_ref[...] + term if has_before else term


def edge_columns(time_idx, core, halves, starts, ends):
    count, modes, width = starts.shape
    for offset, side, load in halves:
        block = load()
        at = 2 * (time_idx ^ offset) + side
        starts[at] = block[:, :width]
        ends[at] = block[:, block.shape[1] - width :]
    lane = lax.broadcasted_iota(jnp.int32, (1, width), 1)
    heads = jnp.zeros((modes, width), jnp.float32)
    tails = jnp.zeros((modes, width), jnp.float32)
    for at in range(count):
        pair = (lane == 2 * at) | (lane == 2 * at + 1)
        heads = jnp.where(pair, pltpu.roll(starts[at], 2 * at, 1), heads)
        tails = jnp.where(pair, pltpu.roll(ends[at], (2 * at + 2) % width, 1), tails)
    after = pltpu.roll(heads, width - 1, 1)
    before = pltpu.roll(tails, 1, 1)
    rates = (after - before) * 0.5
    rates = jnp.where(lane == 0, after - heads, rates)
    rates = jnp.where(lane == 2 * count - 1, tails - before, rates)
    edge = jnp.where(lax.rem(lane, 2) == 0, heads, tails)
    inside = lane < 2 * count
    return jnp.where(inside, edge, 0.0), jnp.where(inside, rates, 0.0)


def last_kernel(
    row_block, col_block, chunks, offsets, left_ref, right_ref, before_ref, reg_ref, early_ref,
    early_other_ref, late_ref, late_other_ref, reduced_ref, rates_ref, normal_ref, right_side_ref, starts,
    ends, col_scratch, reduced_out, rates_out, normal_out, right_side_out, sems,
):
    time_idx = lax.axis_index("tm")
    space_idx = lax.axis_index("space")
    core = space_idx % 2
    early, modes, half = early_ref.shape
    groups = early + late_ref.shape[0]
    snaps = 2 * half
    cols = round_up(col_block, 16)
    depth = left_ref.shape[1]
    copies = []

    def send(source, target):
        copies.append(pltpu.make_async_copy(source, target, sems.at[len(copies)]))
        copies[-1].start()

    reduced_out[:, pl.ds(pl.multiple_of(core * half, half), half)] = early_ref[0]
    reduced_out[:, pl.ds(pl.multiple_of((1 - core) * half, half), half)] = early_other_ref[0]
    send(reduced_out, reduced_ref)
    halves = []
    for slot, offset in enumerate(offsets):
        for side, pair in ((core, (early_ref, late_ref)), (1 - core, (early_other_ref, late_other_ref))):
            ref, at = (pair[0], slot) if slot < early else (pair[1], slot - early)
            halves.append((offset, side, functools.partial(lambda ref, at: ref[at], ref, at)))
    edge, edge_rates = edge_columns(time_idx, core, halves, starts, ends)
    own = reduced_out[...]
    width = edge.shape[1]
    own_edges = pltpu.roll(edge_rates, lax.rem(width - 4 * time_idx, width), 1)
    lane = lax.broadcasted_iota(jnp.int32, (1, snaps), 1)
    rates = jnp.where(lane == 0, own_edges[:, 0:1], inner_rates(own, snaps))
    rates_out[...] = jnp.where(lane == snaps - 1, own_edges[:, 3:4], rates)
    send(rates_out, rates_ref)

    block = joined([late_other_ref])
    parts = parts_of(block, depth)
    column_side(left_ref, right_ref, parts, inner_rates(block, half), cols, col_scratch)
    scale = 1.0 / (groups * snaps)
    edge_parts = parts_of(edge, depth)
    edge_rates = edge_rates.astype(jnp.bfloat16)
    for at, size in chunks:
        pick = slice(cols + at, cols + at + round_up(size, 16))
        features = picked(left_ref[pick], right_ref[pick], parts)
        edge_features = picked(left_ref[pick], right_ref[pick], edge_parts)
        total = before_ref[:, at : at + features.shape[0]] + lax.dot_general(
            col_scratch[...], features, NT, preferred_element_type=jnp.float32
        )
        edge_total = lax.dot_general(edge_rates, edge_features, NT, preferred_element_type=jnp.float32)
        col_ids = space_idx * col_block + lax.broadcasted_iota(jnp.int32, (col_block, size), 0)
        row_ids = time_idx * row_block + at + lax.broadcasted_iota(jnp.int32, (col_block, size), 1)
        diagonal = jnp.where(row_ids == col_ids, reg_ref[:, at : at + size], 0.0)
        normal_out[:, at : at + size] = total[:col_block, :size] * scale + diagonal
        right_side_out[:, at : at + size] = (total[cols:] + edge_total)[:, :size] * scale
        send(normal_out.at[:, at : at + size], normal_ref.at[:, at : at + size])
        send(right_side_out.at[:, at : at + size], right_side_ref.at[:, at : at + size])
    for copy in copies:
        copy.wait()


def swapped(value, axis, distance):
    return lax.ppermute(value, axis, [(i, i ^ distance) for i in range(lax.axis_size(axis))])


def local(snapshots, modes_basis, reg_weights):
    feature_count = reg_weights.shape[0]
    snaps_dev = snapshots.shape[0]
    modes = modes_basis.shape[1]
    tm_count = lax.axis_size("tm")
    space_count = lax.axis_size("space")
    row_block = feature_count // tm_count
    col_block = feature_count // space_count
    rows = round_up(row_block, 16)
    cols = round_up(col_block, 16)
    depth = round_up(3 * modes + 1, 128)
    time_idx = lax.axis_index("tm")
    vmem = pl.BlockSpec(memory_space=pltpu.VMEM)
    hbm = pl.BlockSpec(memory_space=pltpu.HBM)
    params = pltpu.CompilerParams(vmem_limit_bytes=32 * 1024 * 1024)

    keep, give = project(snapshots, modes_basis.T)
    half = keep + swapped(give, "space", 1)
    after, half = lax.optimization_barrier((time_idx, half))
    selector = jax.ShapeDtypeStruct((cols + rows, depth), jnp.bfloat16)
    left, right = pl.pallas_call(
        functools.partial(selector_kernel, row_block, col_block),
        out_shape=(selector, selector),
        in_specs=[vmem],
        out_specs=(vmem, vmem),
        compiler_params=params,
        cost_estimate=pl.CostEstimate(flops=10**6, bytes_accessed=10**6, transcendentals=0),
        name="selectors",
    )(half)
    first_row = after * row_block
    reg_rows = lax.dynamic_slice_in_dim(reg_weights, first_row, row_block, 0)[None]

    terms = [half] + [swapped(half, "space", step) for step in range(2, space_count, 2)]
    while len(terms) > 1:
        terms = [terms[i] + terms[i + 1] for i in range(0, len(terms), 2)]
    mine, left, right, reg_rows = lax.optimization_barrier((terms[0], left, right, reg_rows))
    arriving = [(step, swapped(mine, "tm", step)) for step in range(tm_count - 1, 0, -1)]
    acc_shape = jax.ShapeDtypeStruct((cols + modes, rows), jnp.float32)

    def cost(count):
        flops = 2 * count * (2 * depth * (cols + rows) + (cols + modes) * rows)
        return pl.CostEstimate(flops=flops, bytes_accessed=2 * 10**6, transcendentals=0)

    def col_scratch(count):
        return pltpu.VMEM((cols + modes, count), jnp.bfloat16)

    half_snaps = snaps_dev // 2

    def add_terms(acc, blocks):
        count = sum(block.size for block in blocks) // modes
        before = [] if acc is None else [acc]
        return pl.pallas_call(
            functools.partial(halves_kernel, cols, len(before)),
            out_shape=acc_shape,
            in_specs=[vmem] * (2 + len(before) + len(blocks)),
            out_specs=vmem,
            scratch_shapes=[col_scratch(count)],
            input_output_aliases={2: 0} if before else {},
            compiler_params=params,
            cost_estimate=cost(count),
            name="halves",
        )(left, right, *before, *blocks)

    offsets = [0] + [offset for offset, _ in arriving]
    early = [mine, arriving[0][1]]
    late = [got for _, got in arriving[1:]]
    acc = add_terms(None, [mine])
    early_stack = jnp.stack(early)
    early_other = swapped(early_stack, "space", 1)
    acc = add_terms(acc, early[1:])
    acc, *late = lax.optimization_barrier((acc, *late))
    late_stack = jnp.stack(late)
    late_other = swapped(late_stack, "space", 1)
    acc = add_terms(acc, [early_other, late_stack])
    width = 128
    starts = list(range(0, row_block - width, 2 * width))
    starts = [0] + [start - width for start in starts[1:]] if len(starts) > 1 else [0]
    ends = starts[1:] + [row_block]
    chunks = [(start, end - start) for start, end in zip(starts, ends)][::-1]
    out_shapes = (
        jax.ShapeDtypeStruct((modes, snaps_dev), jnp.float32),
        jax.ShapeDtypeStruct((modes, snaps_dev), jnp.float32),
        jax.ShapeDtypeStruct((col_block, row_block), jnp.float32),
        jax.ShapeDtypeStruct((modes, row_block), jnp.float32),
    )
    outs = pl.pallas_call(
        functools.partial(last_kernel, row_block, col_block, chunks, offsets),
        out_shape=out_shapes,
        in_specs=[vmem] * 8,
        out_specs=(hbm,) * 4,
        scratch_shapes=[
            pltpu.VMEM((2 * tm_count, modes, width), jnp.float32),
            pltpu.VMEM((2 * tm_count, modes, width), jnp.float32),
            col_scratch(len(late) * half_snaps),
            *[pltpu.VMEM(shape.shape, shape.dtype) for shape in out_shapes],
            pltpu.SemaphoreType.DMA((2 + 2 * len(chunks),)),
        ],
        compiler_params=params,
        cost_estimate=cost(len(late) * half_snaps),
        name="last_half",
    )(left, right, acc, reg_rows, early_stack, early_other, late_stack, late_other)
    return tuple(out.T for out in outs)


def solution(mesh):
    return jax.shard_map(
        local,
        mesh=mesh,
        in_specs=(P("tm", "space"), P("space", None), P()),
        out_specs=(P("tm", None), P("tm", None), P("tm", "space"), P("tm", None)),
        check_vma=False,
    )
```

```python
import functools

import jax
import jax.numpy as jnp
from jax import lax
from jax.experimental import pallas as pl
from jax.experimental.pallas import tpu as pltpu
from jax.sharding import PartitionSpec as P

NT = (((1,), (1,)), ((), ()))


def round_up(value, step):
    return (value + step - 1) // step * step


def tree_sum(terms):
    while len(terms) > 1:
        terms = [terms[i] + terms[i + 1] for i in range(0, len(terms), 2)]
    return terms[0]


def selectors(first, rows, modes, depth):
    feature = first + lax.broadcasted_iota(jnp.int32, (rows, 1), 0)
    mode = lax.broadcasted_iota(jnp.int32, (1, modes), 1)
    start = modes + mode * modes - (mode * (mode - 1)) // 2
    gap = feature - start
    holds = (gap >= 0) & (gap < modes - mode)
    left = jnp.sum(jnp.where(holds, mode, 0), axis=1, keepdims=True)
    right = left + jnp.sum(jnp.where(holds, gap, 0), axis=1, keepdims=True)
    linear = feature < modes
    left = jnp.where(linear, feature, left)
    right = jnp.where(linear, modes, right)
    lane = lax.broadcasted_iota(jnp.int32, (1, depth), 1)
    held = jnp.where(lane < 3 * modes, lax.rem(lane, modes), lane - 2 * modes)
    return (
        jnp.where(held == left, 1.0, 0.0).astype(jnp.bfloat16),
        jnp.where(held == right, 1.0, 0.0).astype(jnp.bfloat16),
    )


def parts_of(block, depth):
    modes, snaps = block.shape
    high = block.astype(jnp.bfloat16)
    rest = block - high.astype(jnp.float32)
    middle = rest.astype(jnp.bfloat16)
    low = (rest - middle.astype(jnp.float32)).astype(jnp.bfloat16)
    tail = depth - 3 * modes
    ones = jnp.where(lax.broadcasted_iota(jnp.int32, (tail, snaps), 0) == 0, 1.0, 0.0)
    return jnp.concatenate([high, middle, low, ones.astype(jnp.bfloat16)], axis=0)


def picked(left, right, parts):
    first = jnp.dot(left, parts, preferred_element_type=jnp.float32)
    second = jnp.dot(right, parts, preferred_element_type=jnp.float32)
    return (first * second).astype(jnp.bfloat16)


def project_kernel(basis_ref, snaps_ref, out_ref, basis, held, basis_sem, sems):
    chunks, size, states = held.shape
    basis_copy = pltpu.make_async_copy(basis_ref, basis, basis_sem)
    basis_copy.start()
    copies = []
    for chunk in range(chunks):
        rows = pl.ds(chunk * size, size)
        copies.append(pltpu.make_async_copy(snaps_ref.at[rows], held.at[chunk], sems.at[chunk]))
        copies[-1].start()
    basis_copy.wait()
    pieces = 4
    step = states // pieces
    for chunk in range(chunks):
        copies[chunk].wait()
        terms = [
            lax.dot_general(
                basis[:, piece * step : (piece + 1) * step],
                held[chunk, :, piece * step : (piece + 1) * step],
                NT,
                preferred_element_type=jnp.float32,
            )
            for piece in range(pieces)
        ]
        out_ref[:, chunk * size : (chunk + 1) * size] = tree_sum(terms)


def project(snapshots, basis):
    snaps, states = snapshots.shape
    modes = basis.shape[0]
    size = 128
    hbm = pl.BlockSpec(memory_space=pltpu.HBM)
    return pl.pallas_call(
        project_kernel,
        out_shape=jax.ShapeDtypeStruct((modes, snaps), jnp.float32),
        in_specs=[hbm, hbm],
        out_specs=pl.BlockSpec(memory_space=pltpu.VMEM),
        scratch_shapes=[
            pltpu.VMEM(basis.shape, basis.dtype),
            pltpu.VMEM((snaps // size, size, states), snapshots.dtype),
            pltpu.SemaphoreType.DMA,
            pltpu.SemaphoreType.DMA((snaps // size,)),
        ],
        compiler_params=pltpu.CompilerParams(vmem_limit_bytes=55000 * 1024),
        name="project",
    )(basis, snapshots)


def selector_kernel(row_block, col_block, after_ref, left_ref, right_ref):
    modes = after_ref.shape[0]
    cols = round_up(col_block, 16)
    rows = left_ref.shape[0] - cols
    depth = left_ref.shape[1]
    for at, size, first in (
        (0, cols, lax.axis_index("space") * col_block),
        (cols, rows, lax.axis_index("tm") * row_block),
    ):
        left, right = selectors(first, size, modes, depth)
        left_ref[at : at + size] = left
        right_ref[at : at + size] = right


def inner_rates(block, half):
    snaps = block.shape[1]
    lane = lax.rem(lax.broadcasted_iota(jnp.int32, (1, snaps), 1), half)
    rates = (pltpu.roll(block, snaps - 1, 1) - pltpu.roll(block, 1, 1)) * 0.5
    return jnp.where((lane == 0) | (lane == half - 1), 0.0, rates)


def column_side(left_ref, right_ref, parts, rates, cols, col_scratch):
    col_scratch[:cols, : rates.shape[1]] = picked(left_ref[:cols], right_ref[:cols], parts)
    col_scratch[cols:, : rates.shape[1]] = rates.astype(jnp.bfloat16)


def terms_of(left_ref, right_ref, block, half, cols, col_scratch):
    parts = parts_of(block, left_ref.shape[1])
    column_side(left_ref, right_ref, parts, inner_rates(block, half), cols, col_scratch)
    row_features = picked(left_ref[cols:], right_ref[cols:], parts)
    return lax.dot_general(
        col_scratch[:, : block.shape[1]], row_features, NT, preferred_element_type=jnp.float32
    )


def halves_kernel(cols, half, has_before, left_ref, right_ref, *refs):
    before_ref, refs = (refs[0], refs[1:]) if has_before else (None, refs)
    block_refs, acc_ref, col_scratch = refs[:-2], refs[-2], refs[-1]
    block = jnp.concatenate([ref[...] for ref in block_refs], axis=1)
    term = terms_of(left_ref, right_ref, block, half, cols, col_scratch)
    acc_ref[...] = before_ref[...] + term if has_before else term


def edge_columns(time_idx, core, halves, starts, ends):
    count, modes, width = starts.shape
    for offset, side, block in halves:
        at = 2 * (time_idx ^ offset) + side
        starts[at] = block[:, :width]
        ends[at] = block[:, block.shape[1] - width :]
    lane = lax.broadcasted_iota(jnp.int32, (1, width), 1)
    heads = jnp.zeros((modes, width), jnp.float32)
    tails = jnp.zeros((modes, width), jnp.float32)
    for at in range(count):
        pair = (lane == 2 * at) | (lane == 2 * at + 1)
        heads = jnp.where(pair, pltpu.roll(starts[at], 2 * at, 1), heads)
        tails = jnp.where(pair, pltpu.roll(ends[at], (2 * at + 2) % width, 1), tails)
    after = pltpu.roll(heads, width - 1, 1)
    before = pltpu.roll(tails, 1, 1)
    rates = (after - before) * 0.5
    rates = jnp.where(lane == 0, after - heads, rates)
    rates = jnp.where(lane == 2 * count - 1, tails - before, rates)
    edge = jnp.where(lax.rem(lane, 2) == 0, heads, tails)
    inside = lane < 2 * count
    return jnp.where(inside, edge, 0.0), jnp.where(inside, rates, 0.0)


def last_kernel(row_block, col_block, chunks, shares, left_ref, right_ref, before_ref, reg_ref, *refs):
    peers = shares.each
    own_ref = refs[0]
    got_refs, passed_refs = refs[1 : 1 + peers], refs[1 + peers : 1 + 2 * peers]
    got_half_ref, passed_half_ref = refs[1 + 2 * peers : 3 + 2 * peers]
    reduced_ref, rates_ref, normal_ref, right_side_ref = refs[3 + 2 * peers : 7 + 2 * peers]
    starts, ends, col_scratch, rates_out, normal_out, right_side_out, sems = refs[7 + 2 * peers :]
    time_idx = lax.axis_index("tm")
    space_idx = lax.axis_index("space")
    core = space_idx % 2
    modes, snaps = own_ref.shape
    half = snaps // 2
    groups = shares.count
    cols = round_up(col_block, 16)
    depth = left_ref.shape[1]
    copies = []

    def send(source, target):
        copies.append(pltpu.make_async_copy(source, target, sems.at[len(copies)]))
        copies[-1].start()

    send(own_ref, reduced_ref)
    wholes = [(0, own_ref)]
    for step in range(peers):
        first, second = shares.pair(step)
        wholes.append((jnp.where(core == 0, first, second), got_refs[step]))
        wholes.append((jnp.where(core == 0, second, first), passed_refs[step]))
    halves = [(shares.last, core, got_half_ref[...]), (shares.last, 1 - core, passed_half_ref[...])]
    for offset, ref in wholes:
        halves += [(offset, side, ref[:, side * half : (side + 1) * half]) for side in range(2)]
    edge, edge_rates = edge_columns(time_idx, core, halves, starts, ends)
    own = own_ref[...]
    width = edge.shape[1]
    own_edges = pltpu.roll(edge_rates, lax.rem(width - 4 * time_idx, width), 1)
    lane = lax.broadcasted_iota(jnp.int32, (1, snaps), 1)
    rates = jnp.where(lane == 0, own_edges[:, 0:1], inner_rates(own, snaps))
    rates_out[...] = jnp.where(lane == snaps - 1, own_edges[:, 3:4], rates)
    send(rates_out, rates_ref)

    block = passed_half_ref[...]
    parts = parts_of(block, depth)
    column_side(left_ref, right_ref, parts, inner_rates(block, half), cols, col_scratch)
    scale = 1.0 / (groups * snaps)
    edge_parts = parts_of(edge, depth)
    edge_rates = edge_rates.astype(jnp.bfloat16)
    for at, size in chunks:
        pick = slice(cols + at, cols + at + round_up(size, 16))
        features = picked(left_ref[pick], right_ref[pick], parts)
        edge_features = picked(left_ref[pick], right_ref[pick], edge_parts)
        total = before_ref[:, at : at + features.shape[0]] + lax.dot_general(
            col_scratch[...], features, NT, preferred_element_type=jnp.float32
        )
        edge_total = lax.dot_general(edge_rates, edge_features, NT, preferred_element_type=jnp.float32)
        col_ids = space_idx * col_block + lax.broadcasted_iota(jnp.int32, (col_block, size), 0)
        row_ids = time_idx * row_block + at + lax.broadcasted_iota(jnp.int32, (col_block, size), 1)
        diagonal = jnp.where(row_ids == col_ids, reg_ref[:, at : at + size], 0.0)
        normal_out[:, at : at + size] = total[:col_block, :size] * scale + diagonal
        right_side_out[:, at : at + size] = (total[cols:] + edge_total)[:, :size] * scale
        send(normal_out.at[:, at : at + size], normal_ref.at[:, at : at + size])
        send(right_side_out.at[:, at : at + size], right_side_ref.at[:, at : at + size])
    for copy in copies:
        copy.wait()


class Shares:
    def __init__(self, count):
        self.count = count
        self.each = (count - 2) // 2
        self.last = count - 1

    def pair(self, step):
        return 1 + step, 1 + self.each + step


def swapped(value):
    return lax.ppermute(value, "space", [(i, i ^ 1) for i in range(lax.axis_size("space"))])


def exchanged(value, axis, distances):
    space_count = lax.axis_size("space")
    perm = []
    for time in range(lax.axis_size("tm")):
        for space in range(space_count):
            distance = distances[space % 2]
            if axis == "tm":
                target = (time ^ distance) * space_count + space
            else:
                target = time * space_count + (space ^ (2 * distance))
            perm.append((time * space_count + space, target))
    return lax.ppermute(value, ("tm", "space"), perm)


def from_partners(value, axis, shares, core):
    half = value.shape[1] // 2
    wholes = [exchanged(value, axis, shares.pair(step)) for step in range(shares.each)]
    part = jnp.where(core == 0, value[:, :half], value[:, half:])
    return wholes, exchanged(part, axis, (shares.last, shares.last))


def local(snapshots, modes_basis, reg_weights):
    feature_count = reg_weights.shape[0]
    snaps_dev = snapshots.shape[0]
    modes = modes_basis.shape[1]
    tm_count = lax.axis_size("tm")
    space_count = lax.axis_size("space")
    row_block = feature_count // tm_count
    col_block = feature_count // space_count
    rows = round_up(row_block, 16)
    cols = round_up(col_block, 16)
    depth = round_up(3 * modes + 1, 128)
    time_idx = lax.axis_index("tm")
    vmem = pl.BlockSpec(memory_space=pltpu.VMEM)
    hbm = pl.BlockSpec(memory_space=pltpu.HBM)
    params = pltpu.CompilerParams(vmem_limit_bytes=32 * 1024 * 1024)

    core = lax.axis_index("space") % 2
    chip = project(snapshots, modes_basis.T)
    chip = chip + swapped(chip)
    after, chip = lax.optimization_barrier((time_idx, chip))
    selector = jax.ShapeDtypeStruct((cols + rows, depth), jnp.bfloat16)
    left, right = pl.pallas_call(
        functools.partial(selector_kernel, row_block, col_block),
        out_shape=(selector, selector),
        in_specs=[vmem],
        out_specs=(vmem, vmem),
        compiler_params=params,
        cost_estimate=pl.CostEstimate(flops=10**6, bytes_accessed=10**6, transcendentals=0),
        name="selectors",
    )(chip)
    first_row = after * row_block
    reg_rows = lax.dynamic_slice_in_dim(reg_weights, first_row, row_block, 0)[None]

    shares = Shares(space_count // 2)
    wholes, part = from_partners(chip, "space", shares, core)
    sent = jnp.concatenate(wholes + [part], axis=1)
    other = swapped(sent)
    low, high = [], []
    for step, whole in enumerate(wholes):
        passed = other[:, step * snaps_dev : (step + 1) * snaps_dev]
        low.append(jnp.where(core == 0, whole, passed))
        high.append(jnp.where(core == 0, passed, whole))
    passed = other[:, shares.each * snaps_dev :]
    last = [jnp.where(core == 0, part, passed), jnp.where(core == 0, passed, part)]
    own = tree_sum([chip] + low + high + [jnp.concatenate(last, axis=1)])
    own, left, right, reg_rows = lax.optimization_barrier((own, left, right, reg_rows))
    acc_shape = jax.ShapeDtypeStruct((cols + modes, rows), jnp.float32)

    def cost(count):
        flops = 8 * count * (2 * depth * (cols + rows) + (cols + modes) * rows)
        return pl.CostEstimate(flops=flops, bytes_accessed=2 * 10**6, transcendentals=0)

    def col_scratch(count):
        return pltpu.VMEM((cols + modes, count), jnp.bfloat16)

    half_snaps = snaps_dev // 2

    def add_terms(acc, blocks):
        count = sum(block.shape[1] for block in blocks)
        before = [] if acc is None else [acc]
        return pl.pallas_call(
            functools.partial(halves_kernel, cols, half_snaps, len(before)),
            out_shape=acc_shape,
            in_specs=[vmem] * (2 + len(before) + len(blocks)),
            out_specs=vmem,
            scratch_shapes=[col_scratch(count)],
            input_output_aliases={2: 0} if before else {},
            compiler_params=params,
            cost_estimate=cost(count),
            name="halves",
        )(left, right, *before, *blocks)

    shares = Shares(tm_count)
    got, got_half = from_partners(own, "tm", shares, core)
    acc = add_terms(None, [own])
    passed = [swapped(block) for block in got]
    acc = add_terms(acc, got)
    acc, got_half = lax.optimization_barrier((acc, got_half))
    passed_half = swapped(got_half)
    acc = add_terms(acc, passed + [got_half])
    width = 128
    starts = list(range(0, row_block - width, 2 * width))
    starts = [0] + [start - width for start in starts[1:]] if len(starts) > 1 else [0]
    ends = starts[1:] + [row_block]
    chunks = [(start, end - start) for start, end in zip(starts, ends)][::-1]
    out_shapes = (
        jax.ShapeDtypeStruct((modes, snaps_dev), jnp.float32),
        jax.ShapeDtypeStruct((modes, snaps_dev), jnp.float32),
        jax.ShapeDtypeStruct((col_block, row_block), jnp.float32),
        jax.ShapeDtypeStruct((modes, row_block), jnp.float32),
    )
    outs = pl.pallas_call(
        functools.partial(last_kernel, row_block, col_block, chunks, shares),
        out_shape=out_shapes,
        in_specs=[vmem] * (7 + 2 * shares.each),
        out_specs=(hbm,) * 4,
        scratch_shapes=[
            pltpu.VMEM((2 * tm_count, modes, width), jnp.float32),
            pltpu.VMEM((2 * tm_count, modes, width), jnp.float32),
            col_scratch(half_snaps),
            *[pltpu.VMEM(shape.shape, shape.dtype) for shape in out_shapes[1:]],
            pltpu.SemaphoreType.DMA((2 + 2 * len(chunks),)),
        ],
        compiler_params=params,
        cost_estimate=cost(half_snaps),
        name="last_half",
    )(left, right, acc, reg_rows, own, *got, *passed, got_half, passed_half)
    return tuple(out.T for out in outs)


def solution(mesh):
    return jax.shard_map(
        local,
        mesh=mesh,
        in_specs=(P("tm", "space"), P("space", None), P()),
        out_specs=(P("tm", None), P("tm", None), P("tm", "space"), P("tm", None)),
        check_vma=False,
    )
```

```python
import functools

import jax
import jax.numpy as jnp
from jax import lax
from jax.experimental import pallas as pl
from jax.experimental.pallas import tpu as pltpu
from jax.sharding import PartitionSpec as P

NT = (((1,), (1,)), ((), ()))


def round_up(value, step):
    return (value + step - 1) // step * step


def tree_sum(terms):
    while len(terms) > 1:
        terms = [terms[i] + terms[i + 1] for i in range(0, len(terms), 2)]
    return terms[0]


def selectors(first, rows, modes, depth):
    feature = first + lax.broadcasted_iota(jnp.int32, (rows, 1), 0)
    mode = lax.broadcasted_iota(jnp.int32, (1, modes), 1)
    start = modes + mode * modes - (mode * (mode - 1)) // 2
    gap = feature - start
    holds = (gap >= 0) & (gap < modes - mode)
    left = jnp.sum(jnp.where(holds, mode, 0), axis=1, keepdims=True)
    right = left + jnp.sum(jnp.where(holds, gap, 0), axis=1, keepdims=True)
    linear = feature < modes
    left = jnp.where(linear, feature, left)
    right = jnp.where(linear, modes, right)
    lane = lax.broadcasted_iota(jnp.int32, (1, depth), 1)
    held = jnp.where(lane < 3 * modes, lax.rem(lane, modes), lane - 2 * modes)
    return (
        jnp.where(held == left, 1.0, 0.0).astype(jnp.bfloat16),
        jnp.where(held == right, 1.0, 0.0).astype(jnp.bfloat16),
    )


def parts_of(block, depth):
    modes, snaps = block.shape
    high = block.astype(jnp.bfloat16)
    rest = block - high.astype(jnp.float32)
    middle = rest.astype(jnp.bfloat16)
    low = (rest - middle.astype(jnp.float32)).astype(jnp.bfloat16)
    tail = depth - 3 * modes
    ones = jnp.where(lax.broadcasted_iota(jnp.int32, (tail, snaps), 0) == 0, 1.0, 0.0)
    return jnp.concatenate([high, middle, low, ones.astype(jnp.bfloat16)], axis=0)


def picked(left, right, parts):
    first = jnp.dot(left, parts, preferred_element_type=jnp.float32)
    second = jnp.dot(right, parts, preferred_element_type=jnp.float32)
    return (first * second).astype(jnp.bfloat16)


def project_kernel(basis_ref, snaps_ref, keep_ref, give_ref, basis, held, basis_sem, sems):
    core = lax.axis_index("space") % 2
    chunks, size, states = held.shape
    half = chunks // 2 * size
    basis_copy = pltpu.make_async_copy(basis_ref, basis, basis_sem)
    basis_copy.start()
    copies = []
    for chunk in range(chunks):
        side, at = divmod(chunk * size, half)
        first = pl.multiple_of((core if side else 1 - core) * half + at, size)
        copies.append(
            pltpu.make_async_copy(snaps_ref.at[pl.ds(first, size)], held.at[chunk], sems.at[chunk])
        )
        copies[-1].start()
    basis_copy.wait()
    pieces = 4
    step = states // pieces
    for chunk in range(chunks):
        copies[chunk].wait()
        terms = [
            lax.dot_general(
                basis[:, piece * step : (piece + 1) * step],
                held[chunk, :, piece * step : (piece + 1) * step],
                NT,
                preferred_element_type=jnp.float32,
            )
            for piece in range(pieces)
        ]
        side, at = divmod(chunk * size, half)
        (keep_ref if side else give_ref)[:, at : at + size] = tree_sum(terms)


def project(snapshots, basis):
    snaps, states = snapshots.shape
    modes = basis.shape[0]
    size = 128
    hbm = pl.BlockSpec(memory_space=pltpu.HBM)
    vmem = pl.BlockSpec(memory_space=pltpu.VMEM)
    block = jax.ShapeDtypeStruct((modes, snaps // 2), jnp.float32)
    return pl.pallas_call(
        project_kernel,
        out_shape=(block, block),
        in_specs=[hbm, hbm],
        out_specs=(vmem, vmem),
        scratch_shapes=[
            pltpu.VMEM(basis.shape, basis.dtype),
            pltpu.VMEM((snaps // size, size, states), snapshots.dtype),
            pltpu.SemaphoreType.DMA,
            pltpu.SemaphoreType.DMA((snaps // size,)),
        ],
        compiler_params=pltpu.CompilerParams(vmem_limit_bytes=55000 * 1024),
        name="project",
    )(basis, snapshots)


def selector_kernel(row_block, col_block, after_ref, left_ref, right_ref):
    modes = after_ref.shape[0]
    cols = round_up(col_block, 16)
    rows = left_ref.shape[0] - cols
    depth = left_ref.shape[1]
    for at, size, first in (
        (0, cols, lax.axis_index("space") * col_block),
        (cols, rows, lax.axis_index("tm") * row_block),
    ):
        left, right = selectors(first, size, modes, depth)
        left_ref[at : at + size] = left
        right_ref[at : at + size] = right


def inner_rates(block, half):
    snaps = block.shape[1]
    lane = lax.rem(lax.broadcasted_iota(jnp.int32, (1, snaps), 1), half)
    rates = (pltpu.roll(block, snaps - 1, 1) - pltpu.roll(block, 1, 1)) * 0.5
    return jnp.where((lane == 0) | (lane == half - 1), 0.0, rates)


def column_side(left_ref, right_ref, parts, rates, cols, col_scratch):
    col_scratch[:cols, : rates.shape[1]] = picked(left_ref[:cols], right_ref[:cols], parts)
    col_scratch[cols:, : rates.shape[1]] = rates.astype(jnp.bfloat16)


def terms_of(left_ref, right_ref, block, half, cols, col_scratch):
    parts = parts_of(block, left_ref.shape[1])
    column_side(left_ref, right_ref, parts, inner_rates(block, half), cols, col_scratch)
    row_features = picked(left_ref[cols:], right_ref[cols:], parts)
    return lax.dot_general(
        col_scratch[:, : block.shape[1]], row_features, NT, preferred_element_type=jnp.float32
    )


def joined(refs):
    halves = []
    for ref in refs:
        halves.extend([ref[...]] if len(ref.shape) == 2 else [ref[slot] for slot in range(ref.shape[0])])
    return jnp.concatenate(halves, axis=1)


def halves_kernel(cols, has_before, left_ref, right_ref, *refs):
    before_ref, refs = (refs[0], refs[1:]) if has_before else (None, refs)
    block_refs, acc_ref, col_scratch = refs[:-2], refs[-2], refs[-1]
    block = joined(block_refs)
    term = terms_of(left_ref, right_ref, block, block_refs[0].shape[-1], cols, col_scratch)
    acc_ref[...] = before_ref[...] + term if has_before else term


def edge_columns(time_idx, core, halves, starts, ends):
    count, modes, width = starts.shape
    for offset, side, load in halves:
        block = load()
        at = 2 * (time_idx ^ offset) + side
        starts[at] = block[:, :width]
        ends[at] = block[:, block.shape[1] - width :]
    lane = lax.broadcasted_iota(jnp.int32, (1, width), 1)
    heads = jnp.zeros((modes, width), jnp.float32)
    tails = jnp.zeros((modes, width), jnp.float32)
    for at in range(count):
        pair = (lane == 2 * at) | (lane == 2 * at + 1)
        heads = jnp.where(pair, pltpu.roll(starts[at], 2 * at, 1), heads)
        tails = jnp.where(pair, pltpu.roll(ends[at], (2 * at + 2) % width, 1), tails)
    after = pltpu.roll(heads, width - 1, 1)
    before = pltpu.roll(tails, 1, 1)
    rates = (after - before) * 0.5
    rates = jnp.where(lane == 0, after - heads, rates)
    rates = jnp.where(lane == 2 * count - 1, tails - before, rates)
    edge = jnp.where(lax.rem(lane, 2) == 0, heads, tails)
    inside = lane < 2 * count
    return jnp.where(inside, edge, 0.0), jnp.where(inside, rates, 0.0)


def last_kernel(
    row_block, col_block, chunks, offsets, left_ref, right_ref, before_ref, reg_ref, early_ref,
    early_other_ref, late_ref, late_other_ref, reduced_ref, rates_ref, normal_ref, right_side_ref, starts,
    ends, col_scratch, reduced_out, rates_out, normal_out, right_side_out, sems,
):
    time_idx = lax.axis_index("tm")
    space_idx = lax.axis_index("space")
    core = space_idx % 2
    early, modes, half = early_ref.shape
    groups = early + late_ref.shape[0]
    snaps = 2 * half
    cols = round_up(col_block, 16)
    depth = left_ref.shape[1]
    copies = []

    def send(source, target):
        copies.append(pltpu.make_async_copy(source, target, sems.at[len(copies)]))
        copies[-1].start()

    reduced_out[:, pl.ds(pl.multiple_of(core * half, half), half)] = early_ref[0]
    reduced_out[:, pl.ds(pl.multiple_of((1 - core) * half, half), half)] = early_other_ref[0]
    send(reduced_out, reduced_ref)
    halves = []
    for slot, offset in enumerate(offsets):
        for side, pair in ((core, (early_ref, late_ref)), (1 - core, (early_other_ref, late_other_ref))):
            ref, at = (pair[0], slot) if slot < early else (pair[1], slot - early)
            halves.append((offset, side, functools.partial(lambda ref, at: ref[at], ref, at)))
    edge, edge_rates = edge_columns(time_idx, core, halves, starts, ends)
    own = reduced_out[...]
    width = edge.shape[1]
    own_edges = pltpu.roll(edge_rates, lax.rem(width - 4 * time_idx, width), 1)
    lane = lax.broadcasted_iota(jnp.int32, (1, snaps), 1)
    rates = jnp.where(lane == 0, own_edges[:, 0:1], inner_rates(own, snaps))
    rates_out[...] = jnp.where(lane == snaps - 1, own_edges[:, 3:4], rates)
    send(rates_out, rates_ref)

    block = joined([late_other_ref])
    parts = parts_of(block, depth)
    column_side(left_ref, right_ref, parts, inner_rates(block, half), cols, col_scratch)
    scale = 1.0 / (groups * snaps)
    edge_parts = parts_of(edge, depth)
    edge_rates = edge_rates.astype(jnp.bfloat16)
    for at, size in chunks:
        pick = slice(cols + at, cols + at + round_up(size, 16))
        features = picked(left_ref[pick], right_ref[pick], parts)
        edge_features = picked(left_ref[pick], right_ref[pick], edge_parts)
        total = before_ref[:, at : at + features.shape[0]] + lax.dot_general(
            col_scratch[...], features, NT, preferred_element_type=jnp.float32
        )
        edge_total = lax.dot_general(edge_rates, edge_features, NT, preferred_element_type=jnp.float32)
        col_ids = space_idx * col_block + lax.broadcasted_iota(jnp.int32, (col_block, size), 0)
        row_ids = time_idx * row_block + at + lax.broadcasted_iota(jnp.int32, (col_block, size), 1)
        diagonal = jnp.where(row_ids == col_ids, reg_ref[:, at : at + size], 0.0)
        normal_out[:, at : at + size] = total[:col_block, :size] * scale + diagonal
        right_side_out[:, at : at + size] = (total[cols:] + edge_total)[:, :size] * scale
        send(normal_out.at[:, at : at + size], normal_ref.at[:, at : at + size])
        send(right_side_out.at[:, at : at + size], right_side_ref.at[:, at : at + size])
    for copy in copies:
        copy.wait()


def swapped(value, axis, distance):
    return lax.ppermute(value, axis, [(i, i ^ distance) for i in range(lax.axis_size(axis))])


def local(snapshots, modes_basis, reg_weights):
    feature_count = reg_weights.shape[0]
    snaps_dev = snapshots.shape[0]
    modes = modes_basis.shape[1]
    tm_count = lax.axis_size("tm")
    space_count = lax.axis_size("space")
    row_block = feature_count // tm_count
    col_block = feature_count // space_count
    rows = round_up(row_block, 16)
    cols = round_up(col_block, 16)
    depth = round_up(3 * modes + 1, 128)
    time_idx = lax.axis_index("tm")
    vmem = pl.BlockSpec(memory_space=pltpu.VMEM)
    hbm = pl.BlockSpec(memory_space=pltpu.HBM)
    params = pltpu.CompilerParams(vmem_limit_bytes=32 * 1024 * 1024)

    keep, give = project(snapshots, modes_basis.T)
    half = keep + swapped(give, "space", 1)
    after, half = lax.optimization_barrier((time_idx, half))
    selector = jax.ShapeDtypeStruct((cols + rows, depth), jnp.bfloat16)
    left, right = pl.pallas_call(
        functools.partial(selector_kernel, row_block, col_block),
        out_shape=(selector, selector),
        in_specs=[vmem],
        out_specs=(vmem, vmem),
        compiler_params=params,
        cost_estimate=pl.CostEstimate(flops=10**6, bytes_accessed=10**6, transcendentals=0),
        name="selectors",
    )(half)
    first_row = after * row_block
    reg_rows = lax.dynamic_slice_in_dim(reg_weights, first_row, row_block, 0)[None]

    terms = [half] + [swapped(half, "space", step) for step in range(2, space_count, 2)]
    while len(terms) > 1:
        terms = [terms[i] + terms[i + 1] for i in range(0, len(terms), 2)]
    mine, left, right, reg_rows = lax.optimization_barrier((terms[0], left, right, reg_rows))
    arriving = [(step, swapped(mine, "tm", step)) for step in [1, *range(tm_count - 1, 1, -1)]]
    acc_shape = jax.ShapeDtypeStruct((cols + modes, rows), jnp.float32)

    def cost(count):
        flops = 2 * count * (2 * depth * (cols + rows) + (cols + modes) * rows)
        return pl.CostEstimate(flops=flops, bytes_accessed=2 * 10**6, transcendentals=0)

    def col_scratch(count):
        return pltpu.VMEM((cols + modes, count), jnp.bfloat16)

    half_snaps = snaps_dev // 2

    def add_terms(acc, blocks):
        count = sum(block.size for block in blocks) // modes
        before = [] if acc is None else [acc]
        return pl.pallas_call(
            functools.partial(halves_kernel, cols, len(before)),
            out_shape=acc_shape,
            in_specs=[vmem] * (2 + len(before) + len(blocks)),
            out_specs=vmem,
            scratch_shapes=[col_scratch(count)],
            input_output_aliases={2: 0} if before else {},
            compiler_params=params,
            cost_estimate=cost(count),
            name="halves",
        )(left, right, *before, *blocks)

    offsets = [0] + [offset for offset, _ in arriving]
    early = [mine, arriving[0][1]]
    late = [got for _, got in arriving[1:]]
    acc = add_terms(None, [mine])
    early_stack = jnp.stack(early)
    early_other = swapped(early_stack, "space", 1)
    acc = add_terms(acc, early[1:])
    acc, *late = lax.optimization_barrier((acc, *late))
    late_stack = jnp.stack(late)
    late_other = swapped(late_stack, "space", 1)
    acc = add_terms(acc, [early_other, late_stack])
    width = 128
    starts = list(range(0, row_block - width, 2 * width))
    starts = [0] + [start - width for start in starts[1:]] if len(starts) > 1 else [0]
    ends = starts[1:] + [row_block]
    chunks = [(start, end - start) for start, end in zip(starts, ends)][::-1]
    out_shapes = (
        jax.ShapeDtypeStruct((modes, snaps_dev), jnp.float32),
        jax.ShapeDtypeStruct((modes, snaps_dev), jnp.float32),
        jax.ShapeDtypeStruct((col_block, row_block), jnp.float32),
        jax.ShapeDtypeStruct((modes, row_block), jnp.float32),
    )
    outs = pl.pallas_call(
        functools.partial(last_kernel, row_block, col_block, chunks, offsets),
        out_shape=out_shapes,
        in_specs=[vmem] * 8,
        out_specs=(hbm,) * 4,
        scratch_shapes=[
            pltpu.VMEM((2 * tm_count, modes, width), jnp.float32),
            pltpu.VMEM((2 * tm_count, modes, width), jnp.float32),
            col_scratch(len(late) * half_snaps),
            *[pltpu.VMEM(shape.shape, shape.dtype) for shape in out_shapes],
            pltpu.SemaphoreType.DMA((2 + 2 * len(chunks),)),
        ],
        compiler_params=params,
        cost_estimate=cost(len(late) * half_snaps),
        name="last_half",
    )(left, right, acc, reg_rows, early_stack, early_other, late_stack, late_other)
    return tuple(out.T for out in outs)


def solution(mesh):
    return jax.shard_map(
        local,
        mesh=mesh,
        in_specs=(P("tm", "space"), P("space", None), P()),
        out_specs=(P("tm", None), P("tm", None), P("tm", "space"), P("tm", None)),
        check_vma=False,
    )
```

```python
import functools

import jax
import jax.numpy as jnp
from jax import lax
from jax.experimental import pallas as pl
from jax.experimental.pallas import tpu as pltpu
from jax.sharding import PartitionSpec as P

NT = (((1,), (1,)), ((), ()))


def round_up(value, step):
    return (value + step - 1) // step * step


def tree_sum(terms):
    while len(terms) > 1:
        terms = [terms[i] + terms[i + 1] for i in range(0, len(terms), 2)]
    return terms[0]


def selectors(first, rows, modes, depth):
    feature = first + lax.broadcasted_iota(jnp.int32, (rows, 1), 0)
    mode = lax.broadcasted_iota(jnp.int32, (1, modes), 1)
    start = modes + mode * modes - (mode * (mode - 1)) // 2
    gap = feature - start
    holds = (gap >= 0) & (gap < modes - mode)
    left = jnp.sum(jnp.where(holds, mode, 0), axis=1, keepdims=True)
    right = left + jnp.sum(jnp.where(holds, gap, 0), axis=1, keepdims=True)
    linear = feature < modes
    left = jnp.where(linear, feature, left)
    right = jnp.where(linear, modes, right)
    lane = lax.broadcasted_iota(jnp.int32, (1, depth), 1)
    held = jnp.where(lane < 3 * modes, lax.rem(lane, modes), lane - 2 * modes)
    return (
        jnp.where(held == left, 1.0, 0.0).astype(jnp.bfloat16),
        jnp.where(held == right, 1.0, 0.0).astype(jnp.bfloat16),
    )


def parts_of(block, depth):
    modes, snaps = block.shape
    high = block.astype(jnp.bfloat16)
    rest = block - high.astype(jnp.float32)
    middle = rest.astype(jnp.bfloat16)
    low = (rest - middle.astype(jnp.float32)).astype(jnp.bfloat16)
    tail = depth - 3 * modes
    ones = jnp.where(lax.broadcasted_iota(jnp.int32, (tail, snaps), 0) == 0, 1.0, 0.0)
    return jnp.concatenate([high, middle, low, ones.astype(jnp.bfloat16)], axis=0)


def picked(left, right, parts):
    first = jnp.dot(left, parts, preferred_element_type=jnp.float32)
    second = jnp.dot(right, parts, preferred_element_type=jnp.float32)
    return (first * second).astype(jnp.bfloat16)


def project_kernel(basis_ref, snaps_ref, keep_ref, give_ref, basis, held, basis_sem, sems):
    core = lax.axis_index("space") % 2
    chunks, size, states = held.shape
    half = chunks // 2 * size
    basis_copy = pltpu.make_async_copy(basis_ref, basis, basis_sem)
    basis_copy.start()
    copies = []
    for chunk in range(chunks):
        side, at = divmod(chunk * size, half)
        first = pl.multiple_of((core if side else 1 - core) * half + at, size)
        copies.append(
            pltpu.make_async_copy(snaps_ref.at[pl.ds(first, size)], held.at[chunk], sems.at[chunk])
        )
        copies[-1].start()
    basis_copy.wait()
    pieces = 4
    step = states // pieces
    for chunk in range(chunks):
        copies[chunk].wait()
        terms = [
            lax.dot_general(
                basis[:, piece * step : (piece + 1) * step],
                held[chunk, :, piece * step : (piece + 1) * step],
                NT,
                preferred_element_type=jnp.float32,
            )
            for piece in range(pieces)
        ]
        side, at = divmod(chunk * size, half)
        (keep_ref if side else give_ref)[:, at : at + size] = tree_sum(terms)


def project(snapshots, basis):
    snaps, states = snapshots.shape
    modes = basis.shape[0]
    size = 128
    hbm = pl.BlockSpec(memory_space=pltpu.HBM)
    vmem = pl.BlockSpec(memory_space=pltpu.VMEM)
    block = jax.ShapeDtypeStruct((modes, snaps // 2), jnp.float32)
    return pl.pallas_call(
        project_kernel,
        out_shape=(block, block),
        in_specs=[hbm, hbm],
        out_specs=(vmem, vmem),
        scratch_shapes=[
            pltpu.VMEM(basis.shape, basis.dtype),
            pltpu.VMEM((snaps // size, size, states), snapshots.dtype),
            pltpu.SemaphoreType.DMA,
            pltpu.SemaphoreType.DMA((snaps // size,)),
        ],
        compiler_params=pltpu.CompilerParams(vmem_limit_bytes=55000 * 1024),
        name="project",
    )(basis, snapshots)


def selector_kernel(row_block, col_block, after_ref, left_ref, right_ref):
    modes = after_ref.shape[0]
    cols = round_up(col_block, 16)
    rows = left_ref.shape[0] - cols
    depth = left_ref.shape[1]
    for at, size, first in (
        (0, cols, lax.axis_index("space") * col_block),
        (cols, rows, lax.axis_index("tm") * row_block),
    ):
        left, right = selectors(first, size, modes, depth)
        left_ref[at : at + size] = left
        right_ref[at : at + size] = right


def inner_rates(block, half):
    snaps = block.shape[1]
    lane = lax.rem(lax.broadcasted_iota(jnp.int32, (1, snaps), 1), half)
    rates = (pltpu.roll(block, snaps - 1, 1) - pltpu.roll(block, 1, 1)) * 0.5
    return jnp.where((lane == 0) | (lane == half - 1), 0.0, rates)


def column_side(left_ref, right_ref, parts, rates, cols, col_scratch):
    col_scratch[:cols, : rates.shape[1]] = picked(left_ref[:cols], right_ref[:cols], parts)
    col_scratch[cols:, : rates.shape[1]] = rates.astype(jnp.bfloat16)


def terms_of(left_ref, right_ref, block, half, cols, col_scratch):
    parts = parts_of(block, left_ref.shape[1])
    column_side(left_ref, right_ref, parts, inner_rates(block, half), cols, col_scratch)
    row_features = picked(left_ref[cols:], right_ref[cols:], parts)
    return lax.dot_general(
        col_scratch[:, : block.shape[1]], row_features, NT, preferred_element_type=jnp.float32
    )


def halves_of(refs):
    halves = []
    for ref in refs:
        halves.extend([ref[...]] if len(ref.shape) == 2 else [ref[slot] for slot in range(ref.shape[0])])
    return halves


def joined(refs):
    return jnp.concatenate(halves_of(refs), axis=1)


def halves_kernel(cols, has_before, left_ref, right_ref, *refs):
    before_ref, refs = (refs[0], refs[1:]) if has_before else (None, refs)
    block_refs, acc_ref, col_scratch = refs[:-2], refs[-2], refs[-1]
    block = joined(block_refs)
    term = terms_of(left_ref, right_ref, block, block_refs[0].shape[-1], cols, col_scratch)
    acc_ref[...] = before_ref[...] + term if has_before else term


def edge_columns(time_idx, core, halves, starts, ends):
    count, modes, width = starts.shape
    for offset, side, block in halves:
        at = 2 * (time_idx ^ offset) + side
        starts[at] = block[:, :width]
        ends[at] = block[:, block.shape[1] - width :]
    lane = lax.broadcasted_iota(jnp.int32, (1, width), 1)
    heads = jnp.zeros((modes, width), jnp.float32)
    tails = jnp.zeros((modes, width), jnp.float32)
    for at in range(count):
        pair = (lane == 2 * at) | (lane == 2 * at + 1)
        heads = jnp.where(pair, pltpu.roll(starts[at], 2 * at, 1), heads)
        tails = jnp.where(pair, pltpu.roll(ends[at], (2 * at + 2) % width, 1), tails)
    after = pltpu.roll(heads, width - 1, 1)
    before = pltpu.roll(tails, 1, 1)
    rates = (after - before) * 0.5
    rates = jnp.where(lane == 0, after - heads, rates)
    rates = jnp.where(lane == 2 * count - 1, tails - before, rates)
    edge = jnp.where(lax.rem(lane, 2) == 0, heads, tails)
    inside = lane < 2 * count
    return jnp.where(inside, edge, 0.0), jnp.where(inside, rates, 0.0)


def last_kernel(
    row_block, col_block, chunks, offsets, left_ref, right_ref, before_ref, reg_ref, own_ref, own_other_ref,
    first_ref, first_other_ref, late_ref, late_other_ref, reduced_ref, rates_ref, normal_ref, right_side_ref, starts,
    ends, col_scratch, reduced_out, rates_out, normal_out, right_side_out, sems,
):
    time_idx = lax.axis_index("tm")
    space_idx = lax.axis_index("space")
    core = space_idx % 2
    modes, half = own_ref.shape
    groups = 2 + late_ref.shape[0]
    snaps = 2 * half
    cols = round_up(col_block, 16)
    depth = left_ref.shape[1]
    copies = []

    def send(source, target):
        copies.append(pltpu.make_async_copy(source, target, sems.at[len(copies)]))
        copies[-1].start()

    reduced_out[:, pl.ds(pl.multiple_of(core * half, half), half)] = own_ref[...]
    reduced_out[:, pl.ds(pl.multiple_of((1 - core) * half, half), half)] = own_other_ref[...]
    send(reduced_out, reduced_ref)
    halves = []
    for side, refs in (
        (core, (own_ref, first_ref, late_ref)),
        (1 - core, (own_other_ref, first_other_ref, late_other_ref)),
    ):
        halves.extend((offset, side, half) for offset, half in zip(offsets, halves_of(refs)))
    edge, edge_rates = edge_columns(time_idx, core, halves, starts, ends)
    own = reduced_out[...]
    width = edge.shape[1]
    own_edges = pltpu.roll(edge_rates, lax.rem(width - 4 * time_idx, width), 1)
    lane = lax.broadcasted_iota(jnp.int32, (1, snaps), 1)
    rates = jnp.where(lane == 0, own_edges[:, 0:1], inner_rates(own, snaps))
    rates_out[...] = jnp.where(lane == snaps - 1, own_edges[:, 3:4], rates)
    send(rates_out, rates_ref)

    block = joined([late_other_ref])
    parts = parts_of(block, depth)
    column_side(left_ref, right_ref, parts, inner_rates(block, half), cols, col_scratch)
    scale = 1.0 / (groups * snaps)
    edge_parts = parts_of(edge, depth)
    edge_rates = edge_rates.astype(jnp.bfloat16)
    for at, size in chunks:
        pick = slice(cols + at, cols + at + round_up(size, 16))
        features = picked(left_ref[pick], right_ref[pick], parts)
        edge_features = picked(left_ref[pick], right_ref[pick], edge_parts)
        total = before_ref[:, at : at + features.shape[0]] + lax.dot_general(
            col_scratch[...], features, NT, preferred_element_type=jnp.float32
        )
        edge_total = lax.dot_general(edge_rates, edge_features, NT, preferred_element_type=jnp.float32)
        col_ids = space_idx * col_block + lax.broadcasted_iota(jnp.int32, (col_block, size), 0)
        row_ids = time_idx * row_block + at + lax.broadcasted_iota(jnp.int32, (col_block, size), 1)
        diagonal = jnp.where(row_ids == col_ids, reg_ref[:, at : at + size], 0.0)
        normal_out[:, at : at + size] = total[:col_block, :size] * scale + diagonal
        right_side_out[:, at : at + size] = (total[cols:] + edge_total)[:, :size] * scale
        send(normal_out.at[:, at : at + size], normal_ref.at[:, at : at + size])
        send(right_side_out.at[:, at : at + size], right_side_ref.at[:, at : at + size])
    for copy in copies:
        copy.wait()


def swapped(value, axis, distance):
    return lax.ppermute(value, axis, [(i, i ^ distance) for i in range(lax.axis_size(axis))])


def local(snapshots, modes_basis, reg_weights):
    feature_count = reg_weights.shape[0]
    snaps_dev = snapshots.shape[0]
    modes = modes_basis.shape[1]
    tm_count = lax.axis_size("tm")
    space_count = lax.axis_size("space")
    row_block = feature_count // tm_count
    col_block = feature_count // space_count
    rows = round_up(row_block, 16)
    cols = round_up(col_block, 16)
    depth = round_up(3 * modes + 1, 128)
    time_idx = lax.axis_index("tm")
    vmem = pl.BlockSpec(memory_space=pltpu.VMEM)
    hbm = pl.BlockSpec(memory_space=pltpu.HBM)
    params = pltpu.CompilerParams(vmem_limit_bytes=32 * 1024 * 1024)

    keep, give = project(snapshots, modes_basis.T)
    half = keep + swapped(give, "space", 1)
    after, half = lax.optimization_barrier((time_idx, half))
    selector = jax.ShapeDtypeStruct((cols + rows, depth), jnp.bfloat16)
    left, right = pl.pallas_call(
        functools.partial(selector_kernel, row_block, col_block),
        out_shape=(selector, selector),
        in_specs=[vmem],
        out_specs=(vmem, vmem),
        compiler_params=params,
        cost_estimate=pl.CostEstimate(flops=10**6, bytes_accessed=10**6, transcendentals=0),
        name="selectors",
    )(half)
    first_row = after * row_block
    reg_rows = lax.dynamic_slice_in_dim(reg_weights, first_row, row_block, 0)[None]

    terms = [half] + [swapped(half, "space", step) for step in range(2, space_count, 2)]
    while len(terms) > 1:
        terms = [terms[i] + terms[i + 1] for i in range(0, len(terms), 2)]
    mine, left, right, reg_rows = lax.optimization_barrier((terms[0], left, right, reg_rows))
    arriving = [(step, swapped(mine, "tm", step)) for step in range(tm_count - 1, 0, -1)]
    acc_shape = jax.ShapeDtypeStruct((cols + modes, rows), jnp.float32)

    def cost(count):
        flops = 2 * count * (2 * depth * (cols + rows) + (cols + modes) * rows)
        return pl.CostEstimate(flops=flops, bytes_accessed=2 * 10**6, transcendentals=0)

    def col_scratch(count):
        return pltpu.VMEM((cols + modes, count), jnp.bfloat16)

    half_snaps = snaps_dev // 2

    def add_terms(acc, blocks):
        count = sum(block.size for block in blocks) // modes
        before = [] if acc is None else [acc]
        return pl.pallas_call(
            functools.partial(halves_kernel, cols, len(before)),
            out_shape=acc_shape,
            in_specs=[vmem] * (2 + len(before) + len(blocks)),
            out_specs=vmem,
            scratch_shapes=[col_scratch(count)],
            input_output_aliases={2: 0} if before else {},
            compiler_params=params,
            cost_estimate=cost(count),
            name="halves",
        )(left, right, *before, *blocks)

    offsets = [0] + [offset for offset, _ in arriving]
    first = arriving[0][1]
    late = [got for _, got in arriving[1:]]
    own_other = swapped(mine, "space", 1)
    acc = add_terms(None, [mine, own_other])
    acc, first = lax.optimization_barrier((acc, first))
    first_other = swapped(jnp.stack([mine, first]), "space", 1)[1]
    acc = add_terms(acc, [first])
    acc, *late = lax.optimization_barrier((acc, *late))
    late_stack = jnp.stack(late)
    late_other = swapped(late_stack, "space", 1)
    acc = add_terms(acc, [first_other, late_stack])
    width = 128
    starts = list(range(0, row_block - width, 2 * width))
    starts = [0] + [start - width for start in starts[1:]] if len(starts) > 1 else [0]
    ends = starts[1:] + [row_block]
    chunks = [(start, end - start) for start, end in zip(starts, ends)][::-1]
    out_shapes = (
        jax.ShapeDtypeStruct((modes, snaps_dev), jnp.float32),
        jax.ShapeDtypeStruct((modes, snaps_dev), jnp.float32),
        jax.ShapeDtypeStruct((col_block, row_block), jnp.float32),
        jax.ShapeDtypeStruct((modes, row_block), jnp.float32),
    )
    outs = pl.pallas_call(
        functools.partial(last_kernel, row_block, col_block, chunks, offsets),
        out_shape=out_shapes,
        in_specs=[vmem] * 10,
        out_specs=(hbm,) * 4,
        scratch_shapes=[
            pltpu.VMEM((2 * tm_count, modes, width), jnp.float32),
            pltpu.VMEM((2 * tm_count, modes, width), jnp.float32),
            col_scratch(len(late) * half_snaps),
            *[pltpu.VMEM(shape.shape, shape.dtype) for shape in out_shapes],
            pltpu.SemaphoreType.DMA((2 + 2 * len(chunks),)),
        ],
        compiler_params=params,
        cost_estimate=cost(len(late) * half_snaps),
        name="last_half",
    )(left, right, acc, reg_rows, mine, own_other, first, first_other, late_stack, late_other)
    return tuple(out.T for out in outs)


def solution(mesh):
    return jax.shard_map(
        local,
        mesh=mesh,
        in_specs=(P("tm", "space"), P("space", None), P()),
        out_specs=(P("tm", None), P("tm", None), P("tm", "space"), P("tm", None)),
        check_vma=False,
    )
```

```python
import functools

import jax
import jax.numpy as jnp
from jax import lax
from jax.experimental import pallas as pl
from jax.experimental.pallas import tpu as pltpu
from jax.sharding import PartitionSpec as P

NT = (((1,), (1,)), ((), ()))


def round_up(value, step):
    return (value + step - 1) // step * step


def tree_sum(terms):
    while len(terms) > 1:
        terms = [terms[i] + terms[i + 1] for i in range(0, len(terms), 2)]
    return terms[0]


def selectors(first, rows, modes, depth):
    feature = first + lax.broadcasted_iota(jnp.int32, (rows, 1), 0)
    mode = lax.broadcasted_iota(jnp.int32, (1, modes), 1)
    start = modes + mode * modes - (mode * (mode - 1)) // 2
    gap = feature - start
    holds = (gap >= 0) & (gap < modes - mode)
    left = jnp.sum(jnp.where(holds, mode, 0), axis=1, keepdims=True)
    right = left + jnp.sum(jnp.where(holds, gap, 0), axis=1, keepdims=True)
    linear = feature < modes
    left = jnp.where(linear, feature, left)
    right = jnp.where(linear, modes, right)
    lane = lax.broadcasted_iota(jnp.int32, (1, depth), 1)
    held = jnp.where(lane < 3 * modes, lax.rem(lane, modes), lane - 2 * modes)
    return (
        jnp.where(held == left, 1.0, 0.0).astype(jnp.bfloat16),
        jnp.where(held == right, 1.0, 0.0).astype(jnp.bfloat16),
    )


def parts_of(block, depth):
    modes, snaps = block.shape
    high = block.astype(jnp.bfloat16)
    rest = block - high.astype(jnp.float32)
    middle = rest.astype(jnp.bfloat16)
    low = (rest - middle.astype(jnp.float32)).astype(jnp.bfloat16)
    tail = depth - 3 * modes
    ones = jnp.where(lax.broadcasted_iota(jnp.int32, (tail, snaps), 0) == 0, 1.0, 0.0)
    return jnp.concatenate([high, middle, low, ones.astype(jnp.bfloat16)], axis=0)


def picked(left, right, parts):
    first = jnp.dot(left, parts, preferred_element_type=jnp.float32)
    second = jnp.dot(right, parts, preferred_element_type=jnp.float32)
    return (first * second).astype(jnp.bfloat16)


def project_kernel(basis_ref, snaps_ref, keep_ref, give_ref, basis, held, basis_sem, sems):
    core = lax.axis_index("space") % 2
    chunks, size, states = held.shape
    half = chunks // 2 * size
    basis_copy = pltpu.make_async_copy(basis_ref, basis, basis_sem)
    basis_copy.start()
    copies = []
    for chunk in range(chunks):
        side, at = divmod(chunk * size, half)
        first = pl.multiple_of((core if side else 1 - core) * half + at, size)
        copies.append(
            pltpu.make_async_copy(snaps_ref.at[pl.ds(first, size)], held.at[chunk], sems.at[chunk])
        )
        copies[-1].start()
    basis_copy.wait()
    pieces = 4
    step = states // pieces
    for chunk in range(chunks):
        copies[chunk].wait()
        terms = [
            lax.dot_general(
                basis[:, piece * step : (piece + 1) * step],
                held[chunk, :, piece * step : (piece + 1) * step],
                NT,
                preferred_element_type=jnp.float32,
            )
            for piece in range(pieces)
        ]
        side, at = divmod(chunk * size, half)
        (keep_ref if side else give_ref)[:, at : at + size] = tree_sum(terms)


def project(snapshots, basis):
    snaps, states = snapshots.shape
    modes = basis.shape[0]
    size = 128
    hbm = pl.BlockSpec(memory_space=pltpu.HBM)
    vmem = pl.BlockSpec(memory_space=pltpu.VMEM)
    block = jax.ShapeDtypeStruct((modes, snaps // 2), jnp.float32)
    return pl.pallas_call(
        project_kernel,
        out_shape=(block, block),
        in_specs=[hbm, hbm],
        out_specs=(vmem, vmem),
        scratch_shapes=[
            pltpu.VMEM(basis.shape, basis.dtype),
            pltpu.VMEM((snaps // size, size, states), snapshots.dtype),
            pltpu.SemaphoreType.DMA,
            pltpu.SemaphoreType.DMA((snaps // size,)),
        ],
        compiler_params=pltpu.CompilerParams(vmem_limit_bytes=55000 * 1024),
        name="project",
    )(basis, snapshots)


def selector_kernel(row_block, col_block, after_ref, left_ref, right_ref):
    modes = after_ref.shape[0]
    cols = round_up(col_block, 16)
    rows = left_ref.shape[0] - cols
    depth = left_ref.shape[1]
    for at, size, first in (
        (0, cols, lax.axis_index("space") * col_block),
        (cols, rows, lax.axis_index("tm") * row_block),
    ):
        left, right = selectors(first, size, modes, depth)
        left_ref[at : at + size] = left
        right_ref[at : at + size] = right


def inner_rates(block, half):
    snaps = block.shape[1]
    lane = lax.rem(lax.broadcasted_iota(jnp.int32, (1, snaps), 1), half)
    rates = (pltpu.roll(block, snaps - 1, 1) - pltpu.roll(block, 1, 1)) * 0.5
    return jnp.where((lane == 0) | (lane == half - 1), 0.0, rates)


def column_side(left_ref, right_ref, parts, rates, cols, col_scratch):
    col_scratch[:cols, : rates.shape[1]] = picked(left_ref[:cols], right_ref[:cols], parts)
    col_scratch[cols:, : rates.shape[1]] = rates.astype(jnp.bfloat16)


def terms_of(left_ref, right_ref, block, half, cols, col_scratch):
    parts = parts_of(block, left_ref.shape[1])
    column_side(left_ref, right_ref, parts, inner_rates(block, half), cols, col_scratch)
    row_features = picked(left_ref[cols:], right_ref[cols:], parts)
    return lax.dot_general(
        col_scratch[:, : block.shape[1]], row_features, NT, preferred_element_type=jnp.float32
    )


def halves_of(refs):
    halves = []
    for ref in refs:
        halves.extend([ref[...]] if len(ref.shape) == 2 else [ref[slot] for slot in range(ref.shape[0])])
    return halves


def joined(refs):
    return jnp.concatenate(halves_of(refs), axis=1)


def halves_kernel(cols, has_before, left_ref, right_ref, *refs):
    before_ref, refs = (refs[0], refs[1:]) if has_before else (None, refs)
    block_refs, acc_ref, col_scratch = refs[:-2], refs[-2], refs[-1]
    block = joined(block_refs)
    term = terms_of(left_ref, right_ref, block, block_refs[0].shape[-1], cols, col_scratch)
    acc_ref[...] = before_ref[...] + term if has_before else term


def edge_columns(time_idx, core, halves, starts, ends):
    count, modes, width = starts.shape
    for offset, side, block in halves:
        at = 2 * (time_idx ^ offset) + side
        starts[at] = block[:, :width]
        ends[at] = block[:, block.shape[1] - width :]
    lane = lax.broadcasted_iota(jnp.int32, (1, width), 1)
    heads = jnp.zeros((modes, width), jnp.float32)
    tails = jnp.zeros((modes, width), jnp.float32)
    for at in range(count):
        pair = (lane == 2 * at) | (lane == 2 * at + 1)
        heads = jnp.where(pair, pltpu.roll(starts[at], 2 * at, 1), heads)
        tails = jnp.where(pair, pltpu.roll(ends[at], (2 * at + 2) % width, 1), tails)
    after = pltpu.roll(heads, width - 1, 1)
    before = pltpu.roll(tails, 1, 1)
    rates = (after - before) * 0.5
    rates = jnp.where(lane == 0, after - heads, rates)
    rates = jnp.where(lane == 2 * count - 1, tails - before, rates)
    edge = jnp.where(lax.rem(lane, 2) == 0, heads, tails)
    inside = lane < 2 * count
    return jnp.where(inside, edge, 0.0), jnp.where(inside, rates, 0.0)


def last_kernel(
    row_block, col_block, chunks, offsets, left_ref, right_ref, before_ref, reg_ref, own_ref, own_other_ref,
    first_ref, first_other_ref, late_ref, late_other_ref, reduced_ref, rates_ref, normal_ref, right_side_ref, starts,
    ends, col_scratch, reduced_out, rates_out, normal_out, right_side_out, sems,
):
    time_idx = lax.axis_index("tm")
    space_idx = lax.axis_index("space")
    core = space_idx % 2
    modes, half = own_ref.shape
    groups = 2 + late_ref.shape[0]
    snaps = 2 * half
    cols = round_up(col_block, 16)
    depth = left_ref.shape[1]
    copies = []

    def send(source, target):
        copies.append(pltpu.make_async_copy(source, target, sems.at[len(copies)]))
        copies[-1].start()

    reduced_out[:, pl.ds(pl.multiple_of(core * half, half), half)] = own_ref[...]
    reduced_out[:, pl.ds(pl.multiple_of((1 - core) * half, half), half)] = own_other_ref[...]
    send(reduced_out, reduced_ref)
    halves = []
    for side, refs in (
        (core, (own_ref, first_ref, late_ref)),
        (1 - core, (own_other_ref, first_other_ref, late_other_ref)),
    ):
        halves.extend((offset, side, half) for offset, half in zip(offsets, halves_of(refs)))
    edge, edge_rates = edge_columns(time_idx, core, halves, starts, ends)
    own = reduced_out[...]
    width = edge.shape[1]
    own_edges = pltpu.roll(edge_rates, lax.rem(width - 4 * time_idx, width), 1)
    lane = lax.broadcasted_iota(jnp.int32, (1, snaps), 1)
    rates = jnp.where(lane == 0, own_edges[:, 0:1], inner_rates(own, snaps))
    rates_out[...] = jnp.where(lane == snaps - 1, own_edges[:, 3:4], rates)
    send(rates_out, rates_ref)

    block = joined([late_other_ref])
    parts = parts_of(block, depth)
    column_side(left_ref, right_ref, parts, inner_rates(block, half), cols, col_scratch)
    scale = 1.0 / (groups * snaps)
    edge_parts = parts_of(edge, depth)
    edge_rates = edge_rates.astype(jnp.bfloat16)
    for at, size in chunks:
        pick = slice(cols + at, cols + at + round_up(size, 16))
        features = picked(left_ref[pick], right_ref[pick], parts)
        edge_features = picked(left_ref[pick], right_ref[pick], edge_parts)
        total = before_ref[:, at : at + features.shape[0]] + lax.dot_general(
            col_scratch[...], features, NT, preferred_element_type=jnp.float32
        )
        edge_total = lax.dot_general(edge_rates, edge_features, NT, preferred_element_type=jnp.float32)
        col_ids = space_idx * col_block + lax.broadcasted_iota(jnp.int32, (col_block, size), 0)
        row_ids = time_idx * row_block + at + lax.broadcasted_iota(jnp.int32, (col_block, size), 1)
        diagonal = jnp.where(row_ids == col_ids, reg_ref[:, at : at + size], 0.0)
        normal_out[:, at : at + size] = total[:col_block, :size] * scale + diagonal
        right_side_out[:, at : at + size] = (total[cols:] + edge_total)[:, :size] * scale
        send(normal_out.at[:, at : at + size], normal_ref.at[:, at : at + size])
        send(right_side_out.at[:, at : at + size], right_side_ref.at[:, at : at + size])
    for copy in copies:
        copy.wait()


def swapped(value, axis, distance):
    return lax.ppermute(value, axis, [(i, i ^ distance) for i in range(lax.axis_size(axis))])


def local(snapshots, modes_basis, reg_weights):
    feature_count = reg_weights.shape[0]
    snaps_dev = snapshots.shape[0]
    modes = modes_basis.shape[1]
    tm_count = lax.axis_size("tm")
    space_count = lax.axis_size("space")
    row_block = feature_count // tm_count
    col_block = feature_count // space_count
    rows = round_up(row_block, 16)
    cols = round_up(col_block, 16)
    depth = round_up(3 * modes + 1, 128)
    time_idx = lax.axis_index("tm")
    vmem = pl.BlockSpec(memory_space=pltpu.VMEM)
    hbm = pl.BlockSpec(memory_space=pltpu.HBM)
    params = pltpu.CompilerParams(vmem_limit_bytes=32 * 1024 * 1024)

    keep, give = project(snapshots, modes_basis.T)
    half = keep + swapped(give, "space", 1)
    after, half = lax.optimization_barrier((time_idx, half))
    selector = jax.ShapeDtypeStruct((cols + rows, depth), jnp.bfloat16)
    left, right = pl.pallas_call(
        functools.partial(selector_kernel, row_block, col_block),
        out_shape=(selector, selector),
        in_specs=[vmem],
        out_specs=(vmem, vmem),
        compiler_params=params,
        cost_estimate=pl.CostEstimate(flops=10**6, bytes_accessed=10**6, transcendentals=0),
        name="selectors",
    )(half)
    first_row = after * row_block
    reg_rows = lax.dynamic_slice_in_dim(reg_weights, first_row, row_block, 0)[None]

    steps = list(range(2, space_count, 2))
    steps = steps[:-2] + steps[-2:][::-1]
    terms = [half] + [swapped(half, "space", step) for step in steps]
    while len(terms) > 1:
        terms = [terms[i] + terms[i + 1] for i in range(0, len(terms), 2)]
    mine, left, right, reg_rows = lax.optimization_barrier((terms[0], left, right, reg_rows))
    arriving = [(step, swapped(mine, "tm", step)) for step in range(tm_count - 1, 0, -1)]
    acc_shape = jax.ShapeDtypeStruct((cols + modes, rows), jnp.float32)

    def cost(count):
        flops = 2 * count * (2 * depth * (cols + rows) + (cols + modes) * rows)
        return pl.CostEstimate(flops=flops, bytes_accessed=2 * 10**6, transcendentals=0)

    def col_scratch(count):
        return pltpu.VMEM((cols + modes, count), jnp.bfloat16)

    half_snaps = snaps_dev // 2

    def add_terms(acc, blocks):
        count = sum(block.size for block in blocks) // modes
        before = [] if acc is None else [acc]
        return pl.pallas_call(
            functools.partial(halves_kernel, cols, len(before)),
            out_shape=acc_shape,
            in_specs=[vmem] * (2 + len(before) + len(blocks)),
            out_specs=vmem,
            scratch_shapes=[col_scratch(count)],
            input_output_aliases={2: 0} if before else {},
            compiler_params=params,
            cost_estimate=cost(count),
            name="halves",
        )(left, right, *before, *blocks)

    offsets = [0] + [offset for offset, _ in arriving]
    first = arriving[0][1]
    late = [got for _, got in arriving[1:]]
    own_other = swapped(mine, "space", 1)
    acc = add_terms(None, [mine, own_other])
    acc, first = lax.optimization_barrier((acc, first))
    first_other = swapped(jnp.stack([mine, first]), "space", 1)[1]
    acc = add_terms(acc, [first])
    acc, *late = lax.optimization_barrier((acc, *late))
    late_stack = jnp.stack(late)
    late_other = swapped(late_stack, "space", 1)
    acc = add_terms(acc, [first_other, late_stack])
    width = 128
    starts = list(range(0, row_block - width, 2 * width))
    starts = [0] + [start - width for start in starts[1:]] if len(starts) > 1 else [0]
    ends = starts[1:] + [row_block]
    chunks = [(start, end - start) for start, end in zip(starts, ends)][::-1]
    out_shapes = (
        jax.ShapeDtypeStruct((modes, snaps_dev), jnp.float32),
        jax.ShapeDtypeStruct((modes, snaps_dev), jnp.float32),
        jax.ShapeDtypeStruct((col_block, row_block), jnp.float32),
        jax.ShapeDtypeStruct((modes, row_block), jnp.float32),
    )
    outs = pl.pallas_call(
        functools.partial(last_kernel, row_block, col_block, chunks, offsets),
        out_shape=out_shapes,
        in_specs=[vmem] * 10,
        out_specs=(hbm,) * 4,
        scratch_shapes=[
            pltpu.VMEM((2 * tm_count, modes, width), jnp.float32),
            pltpu.VMEM((2 * tm_count, modes, width), jnp.float32),
            col_scratch(len(late) * half_snaps),
            *[pltpu.VMEM(shape.shape, shape.dtype) for shape in out_shapes],
            pltpu.SemaphoreType.DMA((2 + 2 * len(chunks),)),
        ],
        compiler_params=params,
        cost_estimate=cost(len(late) * half_snaps),
        name="last_half",
    )(left, right, acc, reg_rows, mine, own_other, first, first_other, late_stack, late_other)
    return tuple(out.T for out in outs)


def solution(mesh):
    return jax.shard_map(
        local,
        mesh=mesh,
        in_specs=(P("tm", "space"), P("space", None), P()),
        out_specs=(P("tm", None), P("tm", None), P("tm", "space"), P("tm", None)),
        check_vma=False,
    )
```

```python
import functools

import jax
import jax.numpy as jnp
from jax import lax
from jax.experimental import pallas as pl
from jax.experimental.pallas import tpu as pltpu
from jax.sharding import PartitionSpec as P

NT = (((1,), (1,)), ((), ()))


def round_up(value, step):
    return (value + step - 1) // step * step


def tree_sum(terms):
    while len(terms) > 1:
        terms = [terms[i] + terms[i + 1] for i in range(0, len(terms), 2)]
    return terms[0]


def selectors(first, rows, modes, depth):
    feature = first + lax.broadcasted_iota(jnp.int32, (rows, 1), 0)
    mode = lax.broadcasted_iota(jnp.int32, (1, modes), 1)
    start = modes + mode * modes - (mode * (mode - 1)) // 2
    gap = feature - start
    holds = (gap >= 0) & (gap < modes - mode)
    left = jnp.sum(jnp.where(holds, mode, 0), axis=1, keepdims=True)
    right = left + jnp.sum(jnp.where(holds, gap, 0), axis=1, keepdims=True)
    linear = feature < modes
    left = jnp.where(linear, feature, left)
    right = jnp.where(linear, modes, right)
    lane = lax.broadcasted_iota(jnp.int32, (1, depth), 1)
    held = jnp.where(lane < 3 * modes, lax.rem(lane, modes), lane - 2 * modes)
    return (
        jnp.where(held == left, 1.0, 0.0).astype(jnp.bfloat16),
        jnp.where(held == right, 1.0, 0.0).astype(jnp.bfloat16),
    )


def parts_of(block, depth):
    modes, snaps = block.shape
    high = block.astype(jnp.bfloat16)
    rest = block - high.astype(jnp.float32)
    middle = rest.astype(jnp.bfloat16)
    low = (rest - middle.astype(jnp.float32)).astype(jnp.bfloat16)
    tail = depth - 3 * modes
    ones = jnp.where(lax.broadcasted_iota(jnp.int32, (tail, snaps), 0) == 0, 1.0, 0.0)
    return jnp.concatenate([high, middle, low, ones.astype(jnp.bfloat16)], axis=0)


def picked(left, right, parts):
    first = jnp.dot(left, parts, preferred_element_type=jnp.float32)
    second = jnp.dot(right, parts, preferred_element_type=jnp.float32)
    return (first * second).astype(jnp.bfloat16)


def project_kernel(basis_ref, snaps_ref, keep_ref, give_ref, basis, held, basis_sem, sems):
    core = lax.axis_index("space") % 2
    chunks, size, states = held.shape
    half = chunks // 2 * size
    basis_copy = pltpu.make_async_copy(basis_ref, basis, basis_sem)
    basis_copy.start()
    copies = []
    for chunk in range(chunks):
        side, at = divmod(chunk * size, half)
        first = pl.multiple_of((core if side else 1 - core) * half + at, size)
        copies.append(
            pltpu.make_async_copy(snaps_ref.at[pl.ds(first, size)], held.at[chunk], sems.at[chunk])
        )
        copies[-1].start()
    basis_copy.wait()
    pieces = 4
    step = states // pieces
    for chunk in range(chunks):
        copies[chunk].wait()
        terms = [
            lax.dot_general(
                basis[:, piece * step : (piece + 1) * step],
                held[chunk, :, piece * step : (piece + 1) * step],
                NT,
                preferred_element_type=jnp.float32,
            )
            for piece in range(pieces)
        ]
        side, at = divmod(chunk * size, half)
        (keep_ref if side else give_ref)[:, at : at + size] = tree_sum(terms)


def project(snapshots, basis):
    snaps, states = snapshots.shape
    modes = basis.shape[0]
    size = snaps // 2
    hbm = pl.BlockSpec(memory_space=pltpu.HBM)
    vmem = pl.BlockSpec(memory_space=pltpu.VMEM)
    block = jax.ShapeDtypeStruct((modes, snaps // 2), jnp.float32)
    return pl.pallas_call(
        project_kernel,
        out_shape=(block, block),
        in_specs=[hbm, hbm],
        out_specs=(vmem, vmem),
        scratch_shapes=[
            pltpu.VMEM(basis.shape, basis.dtype),
            pltpu.VMEM((snaps // size, size, states), snapshots.dtype),
            pltpu.SemaphoreType.DMA,
            pltpu.SemaphoreType.DMA((snaps // size,)),
        ],
        compiler_params=pltpu.CompilerParams(vmem_limit_bytes=55000 * 1024),
        name="project",
    )(basis, snapshots)


def selector_kernel(row_block, col_block, after_ref, left_ref, right_ref):
    modes = after_ref.shape[0]
    cols = round_up(col_block, 16)
    rows = left_ref.shape[0] - cols
    depth = left_ref.shape[1]
    for at, size, first in (
        (0, cols, lax.axis_index("space") * col_block),
        (cols, rows, lax.axis_index("tm") * row_block),
    ):
        left, right = selectors(first, size, modes, depth)
        left_ref[at : at + size] = left
        right_ref[at : at + size] = right


def inner_rates(block, half):
    snaps = block.shape[1]
    lane = lax.rem(lax.broadcasted_iota(jnp.int32, (1, snaps), 1), half)
    rates = (pltpu.roll(block, snaps - 1, 1) - pltpu.roll(block, 1, 1)) * 0.5
    return jnp.where((lane == 0) | (lane == half - 1), 0.0, rates)


def column_side(left_ref, right_ref, parts, rates, cols, col_scratch):
    col_scratch[:cols, : rates.shape[1]] = picked(left_ref[:cols], right_ref[:cols], parts)
    col_scratch[cols:, : rates.shape[1]] = rates.astype(jnp.bfloat16)


def terms_of(left_ref, right_ref, block, half, cols, col_scratch):
    parts = parts_of(block, left_ref.shape[1])
    column_side(left_ref, right_ref, parts, inner_rates(block, half), cols, col_scratch)
    row_features = picked(left_ref[cols:], right_ref[cols:], parts)
    return lax.dot_general(
        col_scratch[:, : block.shape[1]], row_features, NT, preferred_element_type=jnp.float32
    )


def halves_of(refs):
    halves = []
    for ref in refs:
        halves.extend([ref[...]] if len(ref.shape) == 2 else [ref[slot] for slot in range(ref.shape[0])])
    return halves


def joined(refs):
    return jnp.concatenate(halves_of(refs), axis=1)


def halves_kernel(cols, has_before, left_ref, right_ref, *refs):
    before_ref, refs = (refs[0], refs[1:]) if has_before else (None, refs)
    block_refs, acc_ref, col_scratch = refs[:-2], refs[-2], refs[-1]
    block = joined(block_refs)
    term = terms_of(left_ref, right_ref, block, block_refs[0].shape[-1], cols, col_scratch)
    acc_ref[...] = before_ref[...] + term if has_before else term


def edge_columns(time_idx, core, halves, starts, ends):
    count, modes, width = starts.shape
    for offset, side, block in halves:
        at = 2 * (time_idx ^ offset) + side
        starts[at] = block[:, :width]
        ends[at] = block[:, block.shape[1] - width :]
    lane = lax.broadcasted_iota(jnp.int32, (1, width), 1)
    heads = jnp.zeros((modes, width), jnp.float32)
    tails = jnp.zeros((modes, width), jnp.float32)
    for at in range(count):
        pair = (lane == 2 * at) | (lane == 2 * at + 1)
        heads = jnp.where(pair, pltpu.roll(starts[at], 2 * at, 1), heads)
        tails = jnp.where(pair, pltpu.roll(ends[at], (2 * at + 2) % width, 1), tails)
    after = pltpu.roll(heads, width - 1, 1)
    before = pltpu.roll(tails, 1, 1)
    rates = (after - before) * 0.5
    rates = jnp.where(lane == 0, after - heads, rates)
    rates = jnp.where(lane == 2 * count - 1, tails - before, rates)
    edge = jnp.where(lax.rem(lane, 2) == 0, heads, tails)
    inside = lane < 2 * count
    return jnp.where(inside, edge, 0.0), jnp.where(inside, rates, 0.0)


def last_kernel(
    row_block, col_block, chunks, offsets, left_ref, right_ref, before_ref, reg_ref, own_ref, own_other_ref,
    first_ref, first_other_ref, late_ref, late_other_ref, reduced_ref, rates_ref, normal_ref, right_side_ref, starts,
    ends, col_scratch, reduced_out, rates_out, normal_out, right_side_out, sems,
):
    time_idx = lax.axis_index("tm")
    space_idx = lax.axis_index("space")
    core = space_idx % 2
    modes, half = own_ref.shape
    groups = 2 + late_ref.shape[0]
    snaps = 2 * half
    cols = round_up(col_block, 16)
    depth = left_ref.shape[1]
    copies = []

    def send(source, target):
        copies.append(pltpu.make_async_copy(source, target, sems.at[len(copies)]))
        copies[-1].start()

    reduced_out[:, pl.ds(pl.multiple_of(core * half, half), half)] = own_ref[...]
    reduced_out[:, pl.ds(pl.multiple_of((1 - core) * half, half), half)] = own_other_ref[...]
    send(reduced_out, reduced_ref)
    halves = []
    for side, refs in (
        (core, (own_ref, first_ref, late_ref)),
        (1 - core, (own_other_ref, first_other_ref, late_other_ref)),
    ):
        halves.extend((offset, side, half) for offset, half in zip(offsets, halves_of(refs)))
    edge, edge_rates = edge_columns(time_idx, core, halves, starts, ends)
    own = reduced_out[...]
    width = edge.shape[1]
    own_edges = pltpu.roll(edge_rates, lax.rem(width - 4 * time_idx, width), 1)
    lane = lax.broadcasted_iota(jnp.int32, (1, snaps), 1)
    rates = jnp.where(lane == 0, own_edges[:, 0:1], inner_rates(own, snaps))
    rates_out[...] = jnp.where(lane == snaps - 1, own_edges[:, 3:4], rates)
    send(rates_out, rates_ref)

    block = joined([late_other_ref])
    parts = parts_of(block, depth)
    column_side(left_ref, right_ref, parts, inner_rates(block, half), cols, col_scratch)
    scale = 1.0 / (groups * snaps)
    edge_parts = parts_of(edge, depth)
    edge_rates = edge_rates.astype(jnp.bfloat16)
    for at, size in chunks:
        pick = slice(cols + at, cols + at + round_up(size, 16))
        features = picked(left_ref[pick], right_ref[pick], parts)
        edge_features = picked(left_ref[pick], right_ref[pick], edge_parts)
        total = before_ref[:, at : at + features.shape[0]] + lax.dot_general(
            col_scratch[...], features, NT, preferred_element_type=jnp.float32
        )
        edge_total = lax.dot_general(edge_rates, edge_features, NT, preferred_element_type=jnp.float32)
        col_ids = space_idx * col_block + lax.broadcasted_iota(jnp.int32, (col_block, size), 0)
        row_ids = time_idx * row_block + at + lax.broadcasted_iota(jnp.int32, (col_block, size), 1)
        diagonal = jnp.where(row_ids == col_ids, reg_ref[:, at : at + size], 0.0)
        normal_out[:, at : at + size] = total[:col_block, :size] * scale + diagonal
        right_side_out[:, at : at + size] = (total[cols:] + edge_total)[:, :size] * scale
        send(normal_out.at[:, at : at + size], normal_ref.at[:, at : at + size])
        send(right_side_out.at[:, at : at + size], right_side_ref.at[:, at : at + size])
    for copy in copies:
        copy.wait()


def swapped(value, axis, distance):
    return lax.ppermute(value, axis, [(i, i ^ distance) for i in range(lax.axis_size(axis))])


def local(snapshots, modes_basis, reg_weights):
    feature_count = reg_weights.shape[0]
    snaps_dev = snapshots.shape[0]
    modes = modes_basis.shape[1]
    tm_count = lax.axis_size("tm")
    space_count = lax.axis_size("space")
    row_block = feature_count // tm_count
    col_block = feature_count // space_count
    rows = round_up(row_block, 16)
    cols = round_up(col_block, 16)
    depth = round_up(3 * modes + 1, 128)
    time_idx = lax.axis_index("tm")
    vmem = pl.BlockSpec(memory_space=pltpu.VMEM)
    hbm = pl.BlockSpec(memory_space=pltpu.HBM)
    params = pltpu.CompilerParams(vmem_limit_bytes=32 * 1024 * 1024)

    keep, give = project(snapshots, modes_basis.T)
    half = keep + swapped(give, "space", 1)
    after, half = lax.optimization_barrier((time_idx, half))
    selector = jax.ShapeDtypeStruct((cols + rows, depth), jnp.bfloat16)
    left, right = pl.pallas_call(
        functools.partial(selector_kernel, row_block, col_block),
        out_shape=(selector, selector),
        in_specs=[vmem],
        out_specs=(vmem, vmem),
        compiler_params=params,
        cost_estimate=pl.CostEstimate(flops=10**6, bytes_accessed=10**6, transcendentals=0),
        name="selectors",
    )(half)
    first_row = after * row_block
    reg_rows = lax.dynamic_slice_in_dim(reg_weights, first_row, row_block, 0)[None]

    steps = list(range(2, space_count, 2))
    steps = steps[:-2] + steps[-2:][::-1]
    terms = [half] + [swapped(half, "space", step) for step in steps]
    while len(terms) > 1:
        terms = [terms[i] + terms[i + 1] for i in range(0, len(terms), 2)]
    mine, left, right, reg_rows = lax.optimization_barrier((terms[0], left, right, reg_rows))
    arriving = [(step, swapped(mine, "tm", step)) for step in [tm_count - 1, *range(1, tm_count - 1)]]
    acc_shape = jax.ShapeDtypeStruct((cols + modes, rows), jnp.float32)

    def cost(count):
        flops = 2 * count * (2 * depth * (cols + rows) + (cols + modes) * rows)
        return pl.CostEstimate(flops=flops, bytes_accessed=2 * 10**6, transcendentals=0)

    def col_scratch(count):
        return pltpu.VMEM((cols + modes, count), jnp.bfloat16)

    half_snaps = snaps_dev // 2

    def add_terms(acc, blocks):
        count = sum(block.size for block in blocks) // modes
        before = [] if acc is None else [acc]
        return pl.pallas_call(
            functools.partial(halves_kernel, cols, len(before)),
            out_shape=acc_shape,
            in_specs=[vmem] * (2 + len(before) + len(blocks)),
            out_specs=vmem,
            scratch_shapes=[col_scratch(count)],
            input_output_aliases={2: 0} if before else {},
            compiler_params=params,
            cost_estimate=cost(count),
            name="halves",
        )(left, right, *before, *blocks)

    offsets = [0] + [offset for offset, _ in arriving]
    first = arriving[0][1]
    late = [got for _, got in arriving[1:]]
    own_other = swapped(mine, "space", 1)
    acc = add_terms(None, [mine, own_other])
    acc, first = lax.optimization_barrier((acc, first))
    first_other = swapped(jnp.stack([mine, first]), "space", 1)[1]
    acc = add_terms(acc, [first])
    acc, *late = lax.optimization_barrier((acc, *late))
    late_stack = jnp.stack(late)
    late_other = swapped(late_stack, "space", 1)
    acc = add_terms(acc, [first_other, late_stack])
    width = 128
    starts = list(range(0, row_block - width, 2 * width))
    starts = [0] + [start - width for start in starts[1:]] if len(starts) > 1 else [0]
    ends = starts[1:] + [row_block]
    chunks = [(start, end - start) for start, end in zip(starts, ends)][::-1]
    out_shapes = (
        jax.ShapeDtypeStruct((modes, snaps_dev), jnp.float32),
        jax.ShapeDtypeStruct((modes, snaps_dev), jnp.float32),
        jax.ShapeDtypeStruct((col_block, row_block), jnp.float32),
        jax.ShapeDtypeStruct((modes, row_block), jnp.float32),
    )
    outs = pl.pallas_call(
        functools.partial(last_kernel, row_block, col_block, chunks, offsets),
        out_shape=out_shapes,
        in_specs=[vmem] * 10,
        out_specs=(hbm,) * 4,
        scratch_shapes=[
            pltpu.VMEM((2 * tm_count, modes, width), jnp.float32),
            pltpu.VMEM((2 * tm_count, modes, width), jnp.float32),
            col_scratch(len(late) * half_snaps),
            *[pltpu.VMEM(shape.shape, shape.dtype) for shape in out_shapes],
            pltpu.SemaphoreType.DMA((2 + 2 * len(chunks),)),
        ],
        compiler_params=params,
        cost_estimate=cost(len(late) * half_snaps),
        name="last_half",
    )(left, right, acc, reg_rows, mine, own_other, first, first_other, late_stack, late_other)
    return tuple(out.T for out in outs)


def solution(mesh):
    return jax.shard_map(
        local,
        mesh=mesh,
        in_specs=(P("tm", "space"), P("space", None), P()),
        out_specs=(P("tm", None), P("tm", None), P("tm", "space"), P("tm", None)),
        check_vma=False,
    )
```

```python
import functools

import jax
import jax.numpy as jnp
from jax import lax
from jax.experimental import pallas as pl
from jax.experimental.pallas import tpu as pltpu
from jax.sharding import PartitionSpec as P

NT = (((1,), (1,)), ((), ()))


def round_up(value, step):
    return (value + step - 1) // step * step


def tree_sum(terms):
    while len(terms) > 1:
        terms = [terms[i] + terms[i + 1] for i in range(0, len(terms), 2)]
    return terms[0]


def selectors(first, rows, modes, depth):
    feature = first + lax.broadcasted_iota(jnp.int32, (rows, 1), 0)
    mode = lax.broadcasted_iota(jnp.int32, (1, modes), 1)
    start = modes + mode * modes - (mode * (mode - 1)) // 2
    gap = feature - start
    holds = (gap >= 0) & (gap < modes - mode)
    left = jnp.sum(jnp.where(holds, mode, 0), axis=1, keepdims=True)
    right = left + jnp.sum(jnp.where(holds, gap, 0), axis=1, keepdims=True)
    linear = feature < modes
    left = jnp.where(linear, feature, left)
    right = jnp.where(linear, modes, right)
    lane = lax.broadcasted_iota(jnp.int32, (1, depth), 1)
    held = jnp.where(lane < 3 * modes, lax.rem(lane, modes), lane - 2 * modes)
    return (
        jnp.where(held == left, 1.0, 0.0).astype(jnp.bfloat16),
        jnp.where(held == right, 1.0, 0.0).astype(jnp.bfloat16),
    )


def parts_of(block, depth):
    modes, snaps = block.shape
    high = block.astype(jnp.bfloat16)
    rest = block - high.astype(jnp.float32)
    middle = rest.astype(jnp.bfloat16)
    low = (rest - middle.astype(jnp.float32)).astype(jnp.bfloat16)
    tail = depth - 3 * modes
    ones = jnp.where(lax.broadcasted_iota(jnp.int32, (tail, snaps), 0) == 0, 1.0, 0.0)
    return jnp.concatenate([high, middle, low, ones.astype(jnp.bfloat16)], axis=0)


def picked(left, right, parts):
    first = jnp.dot(left, parts, preferred_element_type=jnp.float32)
    second = jnp.dot(right, parts, preferred_element_type=jnp.float32)
    return (first * second).astype(jnp.bfloat16)


def project_kernel(basis_ref, snaps_ref, keep_ref, give_ref, basis, held, basis_sem, sems):
    core = lax.axis_index("space") % 2
    chunks, size, states = held.shape
    half = chunks // 2 * size
    basis_copy = pltpu.make_async_copy(basis_ref, basis, basis_sem)
    basis_copy.start()
    copies = []
    for chunk in range(chunks):
        side, at = divmod(chunk * size, half)
        first = pl.multiple_of((core if side else 1 - core) * half + at, size)
        copies.append(
            pltpu.make_async_copy(snaps_ref.at[pl.ds(first, size)], held.at[chunk], sems.at[chunk])
        )
        copies[-1].start()
    basis_copy.wait()
    pieces = 4
    step = states // pieces
    for chunk in range(chunks):
        copies[chunk].wait()
        terms = [
            lax.dot_general(
                basis[:, piece * step : (piece + 1) * step],
                held[chunk, :, piece * step : (piece + 1) * step],
                NT,
                preferred_element_type=jnp.float32,
            )
            for piece in range(pieces)
        ]
        side, at = divmod(chunk * size, half)
        (keep_ref if side else give_ref)[:, at : at + size] = tree_sum(terms)


def project(snapshots, basis):
    snaps, states = snapshots.shape
    modes = basis.shape[0]
    size = snaps // 2
    hbm = pl.BlockSpec(memory_space=pltpu.HBM)
    vmem = pl.BlockSpec(memory_space=pltpu.VMEM)
    block = jax.ShapeDtypeStruct((modes, snaps // 2), jnp.float32)
    return pl.pallas_call(
        project_kernel,
        out_shape=(block, block),
        in_specs=[hbm, hbm],
        out_specs=(vmem, vmem),
        scratch_shapes=[
            pltpu.VMEM(basis.shape, basis.dtype),
            pltpu.VMEM((snaps // size, size, states), snapshots.dtype),
            pltpu.SemaphoreType.DMA,
            pltpu.SemaphoreType.DMA((snaps // size,)),
        ],
        compiler_params=pltpu.CompilerParams(vmem_limit_bytes=55000 * 1024),
        name="project",
    )(basis, snapshots)


def selector_kernel(row_block, col_block, after_ref, left_ref, right_ref):
    modes = after_ref.shape[0]
    cols = round_up(col_block, 16)
    rows = left_ref.shape[0] - cols
    depth = left_ref.shape[1]
    for at, size, first in (
        (0, cols, lax.axis_index("space") * col_block),
        (cols, rows, lax.axis_index("tm") * row_block),
    ):
        left, right = selectors(first, size, modes, depth)
        left_ref[at : at + size] = left
        right_ref[at : at + size] = right


def inner_rates(block, half):
    snaps = block.shape[1]
    lane = lax.rem(lax.broadcasted_iota(jnp.int32, (1, snaps), 1), half)
    rates = (pltpu.roll(block, snaps - 1, 1) - pltpu.roll(block, 1, 1)) * 0.5
    return jnp.where((lane == 0) | (lane == half - 1), 0.0, rates)


def column_side(left_ref, right_ref, parts, rates, cols, col_scratch):
    col_scratch[:cols, : rates.shape[1]] = picked(left_ref[:cols], right_ref[:cols], parts)
    col_scratch[cols:, : rates.shape[1]] = rates.astype(jnp.bfloat16)


def terms_of(left_ref, right_ref, block, half, cols, col_scratch):
    parts = parts_of(block, left_ref.shape[1])
    column_side(left_ref, right_ref, parts, inner_rates(block, half), cols, col_scratch)
    row_features = picked(left_ref[cols:], right_ref[cols:], parts)
    return lax.dot_general(
        col_scratch[:, : block.shape[1]], row_features, NT, preferred_element_type=jnp.float32
    )


def halves_of(refs):
    halves = []
    for ref in refs:
        halves.extend([ref[...]] if len(ref.shape) == 2 else [ref[slot] for slot in range(ref.shape[0])])
    return halves


def joined(refs):
    return jnp.concatenate(halves_of(refs), axis=1)


def halves_kernel(cols, has_before, left_ref, right_ref, *refs):
    before_ref, refs = (refs[0], refs[1:]) if has_before else (None, refs)
    block_refs, acc_ref, col_scratch = refs[:-2], refs[-2], refs[-1]
    block = joined(block_refs)
    term = terms_of(left_ref, right_ref, block, block_refs[0].shape[-1], cols, col_scratch)
    acc_ref[...] = before_ref[...] + term if has_before else term


def edge_columns(time_idx, core, halves, starts, ends):
    count, modes, width = starts.shape
    for offset, side, block in halves:
        at = 2 * (time_idx ^ offset) + side
        starts[at] = block[:, :width]
        ends[at] = block[:, block.shape[1] - width :]
    lane = lax.broadcasted_iota(jnp.int32, (1, width), 1)
    heads = jnp.zeros((modes, width), jnp.float32)
    tails = jnp.zeros((modes, width), jnp.float32)
    for at in range(count):
        pair = (lane == 2 * at) | (lane == 2 * at + 1)
        heads = jnp.where(pair, pltpu.roll(starts[at], 2 * at, 1), heads)
        tails = jnp.where(pair, pltpu.roll(ends[at], (2 * at + 2) % width, 1), tails)
    after = pltpu.roll(heads, width - 1, 1)
    before = pltpu.roll(tails, 1, 1)
    rates = (after - before) * 0.5
    rates = jnp.where(lane == 0, after - heads, rates)
    rates = jnp.where(lane == 2 * count - 1, tails - before, rates)
    edge = jnp.where(lax.rem(lane, 2) == 0, heads, tails)
    inside = lane < 2 * count
    return jnp.where(inside, edge, 0.0), jnp.where(inside, rates, 0.0)


def last_kernel(
    row_block, col_block, chunks, offsets, left_ref, right_ref, before_ref, reg_ref, own_ref, own_other_ref,
    first_ref, first_other_ref, late_ref, late_other_ref, reduced_ref, rates_ref, normal_ref, right_side_ref, starts,
    ends, col_scratch, reduced_out, rates_out, normal_out, right_side_out, sems,
):
    time_idx = lax.axis_index("tm")
    space_idx = lax.axis_index("space")
    core = space_idx % 2
    modes, half = own_ref.shape
    groups = 2 + late_ref.shape[0]
    snaps = 2 * half
    cols = round_up(col_block, 16)
    depth = left_ref.shape[1]
    copies = []

    def send(source, target):
        copies.append(pltpu.make_async_copy(source, target, sems.at[len(copies)]))
        copies[-1].start()

    reduced_out[:, pl.ds(pl.multiple_of(core * half, half), half)] = own_ref[...]
    reduced_out[:, pl.ds(pl.multiple_of((1 - core) * half, half), half)] = own_other_ref[...]
    send(reduced_out, reduced_ref)
    halves = []
    for side, refs in (
        (core, (own_ref, first_ref, late_ref)),
        (1 - core, (own_other_ref, first_other_ref, late_other_ref)),
    ):
        halves.extend((offset, side, half) for offset, half in zip(offsets, halves_of(refs)))
    edge, edge_rates = edge_columns(time_idx, core, halves, starts, ends)
    own = reduced_out[...]
    width = edge.shape[1]
    own_edges = pltpu.roll(edge_rates, lax.rem(width - 4 * time_idx, width), 1)
    lane = lax.broadcasted_iota(jnp.int32, (1, snaps), 1)
    rates = jnp.where(lane == 0, own_edges[:, 0:1], inner_rates(own, snaps))
    rates_out[...] = jnp.where(lane == snaps - 1, own_edges[:, 3:4], rates)
    send(rates_out, rates_ref)

    block = joined([late_other_ref])
    parts = parts_of(block, depth)
    column_side(left_ref, right_ref, parts, inner_rates(block, half), cols, col_scratch)
    scale = 1.0 / (groups * snaps)
    edge_parts = parts_of(edge, depth)
    edge_rates = edge_rates.astype(jnp.bfloat16)
    for at, size in chunks:
        pick = slice(cols + at, cols + at + round_up(size, 16))
        features = picked(left_ref[pick], right_ref[pick], parts)
        edge_features = picked(left_ref[pick], right_ref[pick], edge_parts)
        total = before_ref[:, at : at + features.shape[0]] + lax.dot_general(
            col_scratch[...], features, NT, preferred_element_type=jnp.float32
        )
        edge_total = lax.dot_general(edge_rates, edge_features, NT, preferred_element_type=jnp.float32)
        col_ids = space_idx * col_block + lax.broadcasted_iota(jnp.int32, (col_block, size), 0)
        row_ids = time_idx * row_block + at + lax.broadcasted_iota(jnp.int32, (col_block, size), 1)
        diagonal = jnp.where(row_ids == col_ids, reg_ref[:, at : at + size], 0.0)
        normal_out[:, at : at + size] = total[:col_block, :size] * scale + diagonal
        right_side_out[:, at : at + size] = (total[cols:] + edge_total)[:, :size] * scale
        send(normal_out.at[:, at : at + size], normal_ref.at[:, at : at + size])
        send(right_side_out.at[:, at : at + size], right_side_ref.at[:, at : at + size])
    for copy in copies:
        copy.wait()


def swapped(value, axis, distance):
    return lax.ppermute(value, axis, [(i, i ^ distance) for i in range(lax.axis_size(axis))])


def shifted(value, distance):
    count = lax.axis_size("space")
    return lax.ppermute(value, "space", [(i, (i + distance) % count) for i in range(count)])


def local(snapshots, modes_basis, reg_weights):
    feature_count = reg_weights.shape[0]
    snaps_dev = snapshots.shape[0]
    modes = modes_basis.shape[1]
    tm_count = lax.axis_size("tm")
    space_count = lax.axis_size("space")
    row_block = feature_count // tm_count
    col_block = feature_count // space_count
    rows = round_up(row_block, 16)
    cols = round_up(col_block, 16)
    depth = round_up(3 * modes + 1, 128)
    time_idx = lax.axis_index("tm")
    vmem = pl.BlockSpec(memory_space=pltpu.VMEM)
    hbm = pl.BlockSpec(memory_space=pltpu.HBM)
    params = pltpu.CompilerParams(vmem_limit_bytes=32 * 1024 * 1024)

    keep, give = project(snapshots, modes_basis.T)
    half = keep + swapped(give, "space", 1)
    after, half = lax.optimization_barrier((time_idx, half))
    selector = jax.ShapeDtypeStruct((cols + rows, depth), jnp.bfloat16)
    left, right = pl.pallas_call(
        functools.partial(selector_kernel, row_block, col_block),
        out_shape=(selector, selector),
        in_specs=[vmem],
        out_specs=(vmem, vmem),
        compiler_params=params,
        cost_estimate=pl.CostEstimate(flops=10**6, bytes_accessed=10**6, transcendentals=0),
        name="selectors",
    )(half)
    first_row = after * row_block
    reg_rows = lax.dynamic_slice_in_dim(reg_weights, first_row, row_block, 0)[None]

    terms = [shifted(half, step) for step in range(2, space_count, 2)]
    terms = [half] + list(lax.optimization_barrier(tuple(terms[::-1]))[::-1])
    while len(terms) > 1:
        middle = len(terms) // 2
        terms = [terms[i] + terms[i + middle] for i in range(middle)]
    mine, left, right, reg_rows = lax.optimization_barrier((terms[0], left, right, reg_rows))
    arriving = [(step, swapped(mine, "tm", step)) for step in [tm_count - 1, *range(1, tm_count - 1)]]
    acc_shape = jax.ShapeDtypeStruct((cols + modes, rows), jnp.float32)

    def cost(count):
        flops = 2 * count * (2 * depth * (cols + rows) + (cols + modes) * rows)
        return pl.CostEstimate(flops=flops, bytes_accessed=2 * 10**6, transcendentals=0)

    def col_scratch(count):
        return pltpu.VMEM((cols + modes, count), jnp.bfloat16)

    half_snaps = snaps_dev // 2

    def add_terms(acc, blocks):
        count = sum(block.size for block in blocks) // modes
        before = [] if acc is None else [acc]
        return pl.pallas_call(
            functools.partial(halves_kernel, cols, len(before)),
            out_shape=acc_shape,
            in_specs=[vmem] * (2 + len(before) + len(blocks)),
            out_specs=vmem,
            scratch_shapes=[col_scratch(count)],
            input_output_aliases={2: 0} if before else {},
            compiler_params=params,
            cost_estimate=cost(count),
            name="halves",
        )(left, right, *before, *blocks)

    offsets = [0] + [offset for offset, _ in arriving]
    first = arriving[0][1]
    late = [got for _, got in arriving[1:]]
    own_other = swapped(mine, "space", 1)
    acc = add_terms(None, [mine, own_other])
    acc, first = lax.optimization_barrier((acc, first))
    first_other = swapped(jnp.stack([mine, first]), "space", 1)[1]
    acc = add_terms(acc, [first])
    acc, *late = lax.optimization_barrier((acc, *late))
    late_stack = jnp.stack(late)
    late_other = swapped(late_stack, "space", 1)
    acc = add_terms(acc, [first_other, late_stack])
    width = 128
    starts = list(range(0, row_block - width, 2 * width))
    starts = [0] + [start - width for start in starts[1:]] if len(starts) > 1 else [0]
    ends = starts[1:] + [row_block]
    chunks = [(start, end - start) for start, end in zip(starts, ends)][::-1]
    out_shapes = (
        jax.ShapeDtypeStruct((modes, snaps_dev), jnp.float32),
        jax.ShapeDtypeStruct((modes, snaps_dev), jnp.float32),
        jax.ShapeDtypeStruct((col_block, row_block), jnp.float32),
        jax.ShapeDtypeStruct((modes, row_block), jnp.float32),
    )
    outs = pl.pallas_call(
        functools.partial(last_kernel, row_block, col_block, chunks, offsets),
        out_shape=out_shapes,
        in_specs=[vmem] * 10,
        out_specs=(hbm,) * 4,
        scratch_shapes=[
            pltpu.VMEM((2 * tm_count, modes, width), jnp.float32),
            pltpu.VMEM((2 * tm_count, modes, width), jnp.float32),
            col_scratch(len(late) * half_snaps),
            *[pltpu.VMEM(shape.shape, shape.dtype) for shape in out_shapes],
            pltpu.SemaphoreType.DMA((2 + 2 * len(chunks),)),
        ],
        compiler_params=params,
        cost_estimate=cost(len(late) * half_snaps),
        name="last_half",
    )(left, right, acc, reg_rows, mine, own_other, first, first_other, late_stack, late_other)
    return tuple(out.T for out in outs)


def solution(mesh):
    return jax.shard_map(
        local,
        mesh=mesh,
        in_specs=(P("tm", "space"), P("space", None), P()),
        out_specs=(P("tm", None), P("tm", None), P("tm", "space"), P("tm", None)),
        check_vma=False,
    )
```

```python
import functools

import jax
import jax.numpy as jnp
from jax import lax
from jax.experimental import pallas as pl
from jax.experimental.pallas import tpu as pltpu
from jax.sharding import PartitionSpec as P

NT = (((1,), (1,)), ((), ()))


def round_up(value, step):
    return (value + step - 1) // step * step


def tree_sum(terms):
    while len(terms) > 1:
        terms = [terms[i] + terms[i + 1] for i in range(0, len(terms), 2)]
    return terms[0]


def selectors(first, rows, modes, depth):
    feature = first + lax.broadcasted_iota(jnp.int32, (rows, 1), 0)
    mode = lax.broadcasted_iota(jnp.int32, (1, modes), 1)
    start = modes + mode * modes - (mode * (mode - 1)) // 2
    gap = feature - start
    holds = (gap >= 0) & (gap < modes - mode)
    left = jnp.sum(jnp.where(holds, mode, 0), axis=1, keepdims=True)
    right = left + jnp.sum(jnp.where(holds, gap, 0), axis=1, keepdims=True)
    linear = feature < modes
    left = jnp.where(linear, feature, left)
    right = jnp.where(linear, modes, right)
    lane = lax.broadcasted_iota(jnp.int32, (1, depth), 1)
    held = jnp.where(lane < 3 * modes, lax.rem(lane, modes), lane - 2 * modes)
    return (
        jnp.where(held == left, 1.0, 0.0).astype(jnp.bfloat16),
        jnp.where(held == right, 1.0, 0.0).astype(jnp.bfloat16),
    )


def parts_of(block, depth):
    modes, snaps = block.shape
    high = block.astype(jnp.bfloat16)
    rest = block - high.astype(jnp.float32)
    middle = rest.astype(jnp.bfloat16)
    low = (rest - middle.astype(jnp.float32)).astype(jnp.bfloat16)
    tail = depth - 3 * modes
    ones = jnp.where(lax.broadcasted_iota(jnp.int32, (tail, snaps), 0) == 0, 1.0, 0.0)
    return jnp.concatenate([high, middle, low, ones.astype(jnp.bfloat16)], axis=0)


def picked(left, right, parts):
    first = jnp.dot(left, parts, preferred_element_type=jnp.float32)
    second = jnp.dot(right, parts, preferred_element_type=jnp.float32)
    return (first * second).astype(jnp.bfloat16)


def project_kernel(basis_ref, snaps_ref, keep_ref, give_ref, basis, held, basis_sem, sems):
    core = lax.axis_index("space") % 2
    chunks, size, states = held.shape
    half = chunks // 2 * size
    basis_copy = pltpu.make_async_copy(basis_ref, basis, basis_sem)
    basis_copy.start()
    copies = []
    for chunk in range(chunks):
        side, at = divmod(chunk * size, half)
        first = pl.multiple_of((core if side else 1 - core) * half + at, size)
        copies.append(
            pltpu.make_async_copy(snaps_ref.at[pl.ds(first, size)], held.at[chunk], sems.at[chunk])
        )
        copies[-1].start()
    basis_copy.wait()
    pieces = 4
    step = states // pieces
    for chunk in range(chunks):
        copies[chunk].wait()
        terms = [
            lax.dot_general(
                basis[:, piece * step : (piece + 1) * step],
                held[chunk, :, piece * step : (piece + 1) * step],
                NT,
                preferred_element_type=jnp.float32,
            )
            for piece in range(pieces)
        ]
        side, at = divmod(chunk * size, half)
        (keep_ref if side else give_ref)[:, at : at + size] = tree_sum(terms)


def project(snapshots, basis):
    snaps, states = snapshots.shape
    modes = basis.shape[0]
    size = snaps // 2
    hbm = pl.BlockSpec(memory_space=pltpu.HBM)
    vmem = pl.BlockSpec(memory_space=pltpu.VMEM)
    block = jax.ShapeDtypeStruct((modes, snaps // 2), jnp.float32)
    return pl.pallas_call(
        project_kernel,
        out_shape=(block, block),
        in_specs=[hbm, hbm],
        out_specs=(vmem, vmem),
        scratch_shapes=[
            pltpu.VMEM(basis.shape, basis.dtype),
            pltpu.VMEM((snaps // size, size, states), snapshots.dtype),
            pltpu.SemaphoreType.DMA,
            pltpu.SemaphoreType.DMA((snaps // size,)),
        ],
        compiler_params=pltpu.CompilerParams(vmem_limit_bytes=55000 * 1024),
        name="project",
    )(basis, snapshots)


def selector_kernel(row_block, col_block, after_ref, left_ref, right_ref):
    modes = after_ref.shape[0]
    cols = round_up(col_block, 16)
    rows = left_ref.shape[0] - cols
    depth = left_ref.shape[1]
    for at, size, first in (
        (0, cols, lax.axis_index("space") * col_block),
        (cols, rows, lax.axis_index("tm") * row_block),
    ):
        left, right = selectors(first, size, modes, depth)
        left_ref[at : at + size] = left
        right_ref[at : at + size] = right


def inner_rates(block, half):
    snaps = block.shape[1]
    lane = lax.rem(lax.broadcasted_iota(jnp.int32, (1, snaps), 1), half)
    rates = (pltpu.roll(block, snaps - 1, 1) - pltpu.roll(block, 1, 1)) * 0.5
    return jnp.where((lane == 0) | (lane == half - 1), 0.0, rates)


def column_side(left_ref, right_ref, parts, rates, cols, col_scratch):
    col_scratch[:cols, : rates.shape[1]] = picked(left_ref[:cols], right_ref[:cols], parts)
    col_scratch[cols:, : rates.shape[1]] = rates.astype(jnp.bfloat16)


def terms_of(left_ref, right_ref, block, half, cols, col_scratch):
    parts = parts_of(block, left_ref.shape[1])
    column_side(left_ref, right_ref, parts, inner_rates(block, half), cols, col_scratch)
    row_features = picked(left_ref[cols:], right_ref[cols:], parts)
    return lax.dot_general(
        col_scratch[:, : block.shape[1]], row_features, NT, preferred_element_type=jnp.float32
    )


def halves_of(refs):
    halves = []
    for ref in refs:
        halves.extend([ref[...]] if len(ref.shape) == 2 else [ref[slot] for slot in range(ref.shape[0])])
    return halves


def joined(refs):
    return jnp.concatenate(halves_of(refs), axis=1)


def halves_kernel(cols, has_before, left_ref, right_ref, *refs):
    before_ref, refs = (refs[0], refs[1:]) if has_before else (None, refs)
    block_refs, acc_ref, col_scratch = refs[:-2], refs[-2], refs[-1]
    block = joined(block_refs)
    term = terms_of(left_ref, right_ref, block, block_refs[0].shape[-1], cols, col_scratch)
    acc_ref[...] = before_ref[...] + term if has_before else term


def edge_columns(halves, starts, ends):
    count, modes, width = starts.shape
    for group, side, block in halves:
        at = 2 * group + side
        starts[at] = block[:, :width]
        ends[at] = block[:, block.shape[1] - width :]
    lane = lax.broadcasted_iota(jnp.int32, (1, width), 1)
    heads = jnp.zeros((modes, width), jnp.float32)
    tails = jnp.zeros((modes, width), jnp.float32)
    for at in range(count):
        pair = (lane == 2 * at) | (lane == 2 * at + 1)
        heads = jnp.where(pair, pltpu.roll(starts[at], 2 * at, 1), heads)
        tails = jnp.where(pair, pltpu.roll(ends[at], (2 * at + 2) % width, 1), tails)
    after = pltpu.roll(heads, width - 1, 1)
    before = pltpu.roll(tails, 1, 1)
    rates = (after - before) * 0.5
    rates = jnp.where(lane == 0, after - heads, rates)
    rates = jnp.where(lane == 2 * count - 1, tails - before, rates)
    edge = jnp.where(lax.rem(lane, 2) == 0, heads, tails)
    inside = lane < 2 * count
    return jnp.where(inside, edge, 0.0), jnp.where(inside, rates, 0.0)


def last_kernel(
    row_block, col_block, chunks, offsets, left_ref, right_ref, before_ref, reg_ref, own_ref, own_other_ref,
    first_ref, first_other_ref, late_ref, late_other_ref, reduced_ref, rates_ref, normal_ref, right_side_ref, starts,
    ends, col_scratch, reduced_out, rates_out, normal_out, right_side_out, sems,
):
    time_idx = lax.axis_index("tm")
    space_idx = lax.axis_index("space")
    core = space_idx % 2
    modes, half = own_ref.shape
    groups = 2 + late_ref.shape[0]
    snaps = 2 * half
    cols = round_up(col_block, 16)
    depth = left_ref.shape[1]
    copies = []

    def send(source, target):
        copies.append(pltpu.make_async_copy(source, target, sems.at[len(copies)]))
        copies[-1].start()

    reduced_out[:, pl.ds(pl.multiple_of(core * half, half), half)] = own_ref[...]
    reduced_out[:, pl.ds(pl.multiple_of((1 - core) * half, half), half)] = own_other_ref[...]
    send(reduced_out, reduced_ref)
    halves = []
    for side, refs in (
        (core, (own_ref, first_ref, late_ref)),
        (1 - core, (own_other_ref, first_other_ref, late_other_ref)),
    ):
        for (even, odd), half_block in zip(offsets, halves_of(refs)):
            group = lax.rem(time_idx + groups - jnp.where(side == 0, even, odd), groups)
            halves.append((group, side, half_block))
    edge, edge_rates = edge_columns(halves, starts, ends)
    own = reduced_out[...]
    width = edge.shape[1]
    own_edges = pltpu.roll(edge_rates, lax.rem(width - 4 * time_idx, width), 1)
    lane = lax.broadcasted_iota(jnp.int32, (1, snaps), 1)
    rates = jnp.where(lane == 0, own_edges[:, 0:1], inner_rates(own, snaps))
    rates_out[...] = jnp.where(lane == snaps - 1, own_edges[:, 3:4], rates)
    send(rates_out, rates_ref)

    block = joined([late_other_ref])
    parts = parts_of(block, depth)
    column_side(left_ref, right_ref, parts, inner_rates(block, half), cols, col_scratch)
    scale = 1.0 / (groups * snaps)
    edge_parts = parts_of(edge, depth)
    edge_rates = edge_rates.astype(jnp.bfloat16)
    for at, size in chunks:
        pick = slice(cols + at, cols + at + round_up(size, 16))
        features = picked(left_ref[pick], right_ref[pick], parts)
        edge_features = picked(left_ref[pick], right_ref[pick], edge_parts)
        total = before_ref[:, at : at + features.shape[0]] + lax.dot_general(
            col_scratch[...], features, NT, preferred_element_type=jnp.float32
        )
        edge_total = lax.dot_general(edge_rates, edge_features, NT, preferred_element_type=jnp.float32)
        col_ids = space_idx * col_block + lax.broadcasted_iota(jnp.int32, (col_block, size), 0)
        row_ids = time_idx * row_block + at + lax.broadcasted_iota(jnp.int32, (col_block, size), 1)
        diagonal = jnp.where(row_ids == col_ids, reg_ref[:, at : at + size], 0.0)
        normal_out[:, at : at + size] = total[:col_block, :size] * scale + diagonal
        right_side_out[:, at : at + size] = (total[cols:] + edge_total)[:, :size] * scale
        send(normal_out.at[:, at : at + size], normal_ref.at[:, at : at + size])
        send(right_side_out.at[:, at : at + size], right_side_ref.at[:, at : at + size])
    for copy in copies:
        copy.wait()


def swapped(value, axis, distance):
    return lax.ppermute(value, axis, [(i, i ^ distance) for i in range(lax.axis_size(axis))])


def shifted(value, distance):
    count = lax.axis_size("space")
    return lax.ppermute(value, "space", [(i, (i + distance) % count) for i in range(count)])


def turned(value, distances):
    tm_count = lax.axis_size("tm")
    space_count = lax.axis_size("space")
    perm = []
    for time in range(tm_count):
        for space in range(space_count):
            target = (time + distances[space % 2]) % tm_count
            perm.append((time * space_count + space, target * space_count + space))
    return lax.ppermute(value, ("tm", "space"), perm)


def local(snapshots, modes_basis, reg_weights):
    feature_count = reg_weights.shape[0]
    snaps_dev = snapshots.shape[0]
    modes = modes_basis.shape[1]
    tm_count = lax.axis_size("tm")
    space_count = lax.axis_size("space")
    row_block = feature_count // tm_count
    col_block = feature_count // space_count
    rows = round_up(row_block, 16)
    cols = round_up(col_block, 16)
    depth = round_up(3 * modes + 1, 128)
    time_idx = lax.axis_index("tm")
    vmem = pl.BlockSpec(memory_space=pltpu.VMEM)
    hbm = pl.BlockSpec(memory_space=pltpu.HBM)
    params = pltpu.CompilerParams(vmem_limit_bytes=32 * 1024 * 1024)

    keep, give = project(snapshots, modes_basis.T)
    half = keep + swapped(give, "space", 1)
    after, half = lax.optimization_barrier((time_idx, half))
    selector = jax.ShapeDtypeStruct((cols + rows, depth), jnp.bfloat16)
    left, right = pl.pallas_call(
        functools.partial(selector_kernel, row_block, col_block),
        out_shape=(selector, selector),
        in_specs=[vmem],
        out_specs=(vmem, vmem),
        compiler_params=params,
        cost_estimate=pl.CostEstimate(flops=10**6, bytes_accessed=10**6, transcendentals=0),
        name="selectors",
    )(half)
    first_row = after * row_block
    reg_rows = lax.dynamic_slice_in_dim(reg_weights, first_row, row_block, 0)[None]

    terms = [shifted(half, step) for step in range(2, space_count, 2)]
    terms = [half] + list(lax.optimization_barrier(tuple(terms[::-1]))[::-1])
    while len(terms) > 1:
        middle = len(terms) // 2
        terms = [terms[i] + terms[i + middle] for i in range(middle)]
    mine, left, right, reg_rows = lax.optimization_barrier((terms[0], left, right, reg_rows))
    orders = list(range(1, tm_count))
    orders = list(zip(orders[:-2] + orders[-2:][::-1], orders))
    arriving = [(orders[k], turned(mine, orders[k])) for k in (0, *range(tm_count - 2, 0, -1))]
    acc_shape = jax.ShapeDtypeStruct((cols + modes, rows), jnp.float32)

    def cost(count):
        flops = 2 * count * (2 * depth * (cols + rows) + (cols + modes) * rows)
        return pl.CostEstimate(flops=flops, bytes_accessed=2 * 10**6, transcendentals=0)

    def col_scratch(count):
        return pltpu.VMEM((cols + modes, count), jnp.bfloat16)

    half_snaps = snaps_dev // 2

    def add_terms(acc, blocks):
        count = sum(block.size for block in blocks) // modes
        before = [] if acc is None else [acc]
        return pl.pallas_call(
            functools.partial(halves_kernel, cols, len(before)),
            out_shape=acc_shape,
            in_specs=[vmem] * (2 + len(before) + len(blocks)),
            out_specs=vmem,
            scratch_shapes=[col_scratch(count)],
            input_output_aliases={2: 0} if before else {},
            compiler_params=params,
            cost_estimate=cost(count),
            name="halves",
        )(left, right, *before, *blocks)

    offsets = [(0, 0)] + [offset for offset, _ in arriving]
    first = arriving[0][1]
    late = [got for _, got in arriving[1:]]
    own_other = swapped(mine, "space", 1)
    acc = add_terms(None, [mine, own_other])
    acc, first = lax.optimization_barrier((acc, first))
    first_other = swapped(jnp.stack([mine, first]), "space", 1)[1]
    acc = add_terms(acc, [first])
    acc, *late = lax.optimization_barrier((acc, *late))
    late_stack = jnp.stack(late)
    late_other = swapped(late_stack, "space", 1)
    acc = add_terms(acc, [first_other, late_stack])
    width = 128
    starts = list(range(0, row_block - width, 2 * width))
    starts = [0] + [start - width for start in starts[1:]] if len(starts) > 1 else [0]
    ends = starts[1:] + [row_block]
    chunks = [(start, end - start) for start, end in zip(starts, ends)][::-1]
    out_shapes = (
        jax.ShapeDtypeStruct((modes, snaps_dev), jnp.float32),
        jax.ShapeDtypeStruct((modes, snaps_dev), jnp.float32),
        jax.ShapeDtypeStruct((col_block, row_block), jnp.float32),
        jax.ShapeDtypeStruct((modes, row_block), jnp.float32),
    )
    outs = pl.pallas_call(
        functools.partial(last_kernel, row_block, col_block, chunks, offsets),
        out_shape=out_shapes,
        in_specs=[vmem] * 10,
        out_specs=(hbm,) * 4,
        scratch_shapes=[
            pltpu.VMEM((2 * tm_count, modes, width), jnp.float32),
            pltpu.VMEM((2 * tm_count, modes, width), jnp.float32),
            col_scratch(len(late) * half_snaps),
            *[pltpu.VMEM(shape.shape, shape.dtype) for shape in out_shapes],
            pltpu.SemaphoreType.DMA((2 + 2 * len(chunks),)),
        ],
        compiler_params=params,
        cost_estimate=cost(len(late) * half_snaps),
        name="last_half",
    )(left, right, acc, reg_rows, mine, own_other, first, first_other, late_stack, late_other)
    return tuple(out.T for out in outs)


def solution(mesh):
    return jax.shard_map(
        local,
        mesh=mesh,
        in_specs=(P("tm", "space"), P("space", None), P()),
        out_specs=(P("tm", None), P("tm", None), P("tm", "space"), P("tm", None)),
        check_vma=False,
    )
```

```python
import functools

import jax
import jax.numpy as jnp
from jax import lax
from jax.experimental import pallas as pl
from jax.experimental.pallas import tpu as pltpu
from jax.sharding import PartitionSpec as P

NT = (((1,), (1,)), ((), ()))


def round_up(value, step):
    return (value + step - 1) // step * step


def tree_sum(terms):
    while len(terms) > 1:
        terms = [terms[i] + terms[i + 1] for i in range(0, len(terms), 2)]
    return terms[0]


def selectors(first, rows, modes, depth):
    feature = first + lax.broadcasted_iota(jnp.int32, (rows, 1), 0)
    mode = lax.broadcasted_iota(jnp.int32, (1, modes), 1)
    start = modes + mode * modes - (mode * (mode - 1)) // 2
    gap = feature - start
    holds = (gap >= 0) & (gap < modes - mode)
    left = jnp.sum(jnp.where(holds, mode, 0), axis=1, keepdims=True)
    right = left + jnp.sum(jnp.where(holds, gap, 0), axis=1, keepdims=True)
    linear = feature < modes
    left = jnp.where(linear, feature, left)
    right = jnp.where(linear, modes, right)
    lane = lax.broadcasted_iota(jnp.int32, (1, depth), 1)
    held = jnp.where(lane < 3 * modes, lax.rem(lane, modes), lane - 2 * modes)
    return (
        jnp.where(held == left, 1.0, 0.0).astype(jnp.bfloat16),
        jnp.where(held == right, 1.0, 0.0).astype(jnp.bfloat16),
    )


def parts_of(block, depth):
    modes, snaps = block.shape
    high = block.astype(jnp.bfloat16)
    rest = block - high.astype(jnp.float32)
    middle = rest.astype(jnp.bfloat16)
    low = (rest - middle.astype(jnp.float32)).astype(jnp.bfloat16)
    tail = depth - 3 * modes
    ones = jnp.where(lax.broadcasted_iota(jnp.int32, (tail, snaps), 0) == 0, 1.0, 0.0)
    return jnp.concatenate([high, middle, low, ones.astype(jnp.bfloat16)], axis=0)


def picked(left, right, parts):
    first = jnp.dot(left, parts, preferred_element_type=jnp.float32)
    second = jnp.dot(right, parts, preferred_element_type=jnp.float32)
    return (first * second).astype(jnp.bfloat16)


def project_kernel(basis_ref, snaps_ref, keep_ref, give_ref, basis, held, basis_sem, sems):
    core = lax.axis_index("space") % 2
    chunks, size, states = held.shape
    half = chunks // 2 * size
    basis_copy = pltpu.make_async_copy(basis_ref, basis, basis_sem)
    basis_copy.start()
    copies = []
    for chunk in range(chunks):
        side, at = divmod(chunk * size, half)
        first = pl.multiple_of((core if side else 1 - core) * half + at, size)
        copies.append(
            pltpu.make_async_copy(snaps_ref.at[pl.ds(first, size)], held.at[chunk], sems.at[chunk])
        )
        copies[-1].start()
    basis_copy.wait()
    pieces = 4
    step = states // pieces
    for chunk in range(chunks):
        copies[chunk].wait()
        terms = [
            lax.dot_general(
                basis[:, piece * step : (piece + 1) * step],
                held[chunk, :, piece * step : (piece + 1) * step],
                NT,
                preferred_element_type=jnp.float32,
            )
            for piece in range(pieces)
        ]
        side, at = divmod(chunk * size, half)
        (keep_ref if side else give_ref)[:, at : at + size] = tree_sum(terms)


def project(snapshots, basis):
    snaps, states = snapshots.shape
    modes = basis.shape[0]
    size = snaps // 2
    hbm = pl.BlockSpec(memory_space=pltpu.HBM)
    vmem = pl.BlockSpec(memory_space=pltpu.VMEM)
    block = jax.ShapeDtypeStruct((modes, snaps // 2), jnp.float32)
    return pl.pallas_call(
        project_kernel,
        out_shape=(block, block),
        in_specs=[hbm, hbm],
        out_specs=(vmem, vmem),
        scratch_shapes=[
            pltpu.VMEM(basis.shape, basis.dtype),
            pltpu.VMEM((snaps // size, size, states), snapshots.dtype),
            pltpu.SemaphoreType.DMA,
            pltpu.SemaphoreType.DMA((snaps // size,)),
        ],
        compiler_params=pltpu.CompilerParams(vmem_limit_bytes=55000 * 1024),
        name="project",
    )(basis, snapshots)


def selector_kernel(row_block, col_block, after_ref, left_ref, right_ref):
    modes = after_ref.shape[0]
    cols = round_up(col_block, 16)
    rows = left_ref.shape[0] - cols
    depth = left_ref.shape[1]
    for at, size, first in (
        (0, cols, lax.axis_index("space") * col_block),
        (cols, rows, lax.axis_index("tm") * row_block),
    ):
        left, right = selectors(first, size, modes, depth)
        left_ref[at : at + size] = left
        right_ref[at : at + size] = right


def inner_rates(block, half):
    snaps = block.shape[1]
    lane = lax.rem(lax.broadcasted_iota(jnp.int32, (1, snaps), 1), half)
    rates = (pltpu.roll(block, snaps - 1, 1) - pltpu.roll(block, 1, 1)) * 0.5
    return jnp.where((lane == 0) | (lane == half - 1), 0.0, rates)


def column_side(left_ref, right_ref, parts, rates, cols, col_scratch):
    col_scratch[:cols, : rates.shape[1]] = picked(left_ref[:cols], right_ref[:cols], parts)
    col_scratch[cols:, : rates.shape[1]] = rates.astype(jnp.bfloat16)


def terms_of(left_ref, right_ref, block, half, cols, col_scratch):
    parts = parts_of(block, left_ref.shape[1])
    column_side(left_ref, right_ref, parts, inner_rates(block, half), cols, col_scratch)
    row_features = picked(left_ref[cols:], right_ref[cols:], parts)
    return lax.dot_general(
        col_scratch[:, : block.shape[1]], row_features, NT, preferred_element_type=jnp.float32
    )


def halves_kernel(cols, half, has_before, left_ref, right_ref, *refs):
    before_ref, refs = (refs[0], refs[1:]) if has_before else (None, refs)
    block_refs, acc_ref, col_scratch = refs[:-2], refs[-2], refs[-1]
    block = jnp.concatenate([ref[...] for ref in block_refs], axis=1)
    term = terms_of(left_ref, right_ref, block, half, cols, col_scratch)
    acc_ref[...] = before_ref[...] + term if has_before else term


def edge_columns(halves, starts, ends):
    count, modes, width = starts.shape
    for group, side, block in halves:
        at = 2 * group + side
        starts[at] = block[:, :width]
        ends[at] = block[:, block.shape[1] - width :]
    lane = lax.broadcasted_iota(jnp.int32, (1, width), 1)
    heads = jnp.zeros((modes, width), jnp.float32)
    tails = jnp.zeros((modes, width), jnp.float32)
    for at in range(count):
        pair = (lane == 2 * at) | (lane == 2 * at + 1)
        heads = jnp.where(pair, pltpu.roll(starts[at], 2 * at, 1), heads)
        tails = jnp.where(pair, pltpu.roll(ends[at], (2 * at + 2) % width, 1), tails)
    after = pltpu.roll(heads, width - 1, 1)
    before = pltpu.roll(tails, 1, 1)
    rates = (after - before) * 0.5
    rates = jnp.where(lane == 0, after - heads, rates)
    rates = jnp.where(lane == 2 * count - 1, tails - before, rates)
    edge = jnp.where(lax.rem(lane, 2) == 0, heads, tails)
    inside = lane < 2 * count
    return jnp.where(inside, edge, 0.0), jnp.where(inside, rates, 0.0)


def last_kernel(row_block, col_block, chunks, wholes, left_ref, right_ref, before_ref, reg_ref, *refs):
    each = len(wholes)
    own_ref, got_half_ref, passed_half_ref = refs[:3]
    got_refs, passed_refs, refs = refs[3 : 3 + each], refs[3 + each : 3 + 2 * each], refs[3 + 2 * each :]
    reduced_ref, rates_ref, normal_ref, right_side_ref = refs[:4]
    starts, ends, col_scratch, rates_out, normal_out, right_side_out, sems = refs[4:]
    time_idx = lax.axis_index("tm")
    space_idx = lax.axis_index("space")
    core = space_idx % 2
    modes, snaps = own_ref.shape
    half = snaps // 2
    groups = 2 + 2 * each
    cols = round_up(col_block, 16)
    depth = left_ref.shape[1]
    copies = []

    def send(source, target):
        copies.append(pltpu.make_async_copy(source, target, sems.at[len(copies)]))
        copies[-1].start()

    send(own_ref, reduced_ref)

    def group_at(steps, side):
        return lax.rem(time_idx + groups - jnp.where(side == 0, steps[0], steps[1]), groups)

    halves = [
        (group_at((1, 1), 0), core, got_half_ref[...]),
        (group_at((1, 1), 0), 1 - core, passed_half_ref[...]),
    ]
    blocks = [(time_idx, own_ref)]
    blocks += [(group_at(steps, core), ref) for steps, ref in zip(wholes, got_refs)]
    blocks += [(group_at(steps, 1 - core), ref) for steps, ref in zip(wholes, passed_refs)]
    for group, ref in blocks:
        halves += [(group, side, ref[:, side * half : (side + 1) * half]) for side in range(2)]
    edge, edge_rates = edge_columns(halves, starts, ends)
    own = own_ref[...]
    width = edge.shape[1]
    own_edges = pltpu.roll(edge_rates, lax.rem(width - 4 * time_idx, width), 1)
    lane = lax.broadcasted_iota(jnp.int32, (1, snaps), 1)
    rates = jnp.where(lane == 0, own_edges[:, 0:1], inner_rates(own, snaps))
    rates_out[...] = jnp.where(lane == snaps - 1, own_edges[:, 3:4], rates)
    send(rates_out, rates_ref)

    block = jnp.concatenate([ref[...] for ref in passed_refs], axis=1)
    parts = parts_of(block, depth)
    column_side(left_ref, right_ref, parts, inner_rates(block, half), cols, col_scratch)
    scale = 1.0 / (groups * snaps)
    edge_parts = parts_of(edge, depth)
    edge_rates = edge_rates.astype(jnp.bfloat16)
    for at, size in chunks:
        pick = slice(cols + at, cols + at + round_up(size, 16))
        features = picked(left_ref[pick], right_ref[pick], parts)
        edge_features = picked(left_ref[pick], right_ref[pick], edge_parts)
        total = before_ref[:, at : at + features.shape[0]] + lax.dot_general(
            col_scratch[...], features, NT, preferred_element_type=jnp.float32
        )
        edge_total = lax.dot_general(edge_rates, edge_features, NT, preferred_element_type=jnp.float32)
        col_ids = space_idx * col_block + lax.broadcasted_iota(jnp.int32, (col_block, size), 0)
        row_ids = time_idx * row_block + at + lax.broadcasted_iota(jnp.int32, (col_block, size), 1)
        diagonal = jnp.where(row_ids == col_ids, reg_ref[:, at : at + size], 0.0)
        normal_out[:, at : at + size] = total[:col_block, :size] * scale + diagonal
        right_side_out[:, at : at + size] = (total[cols:] + edge_total)[:, :size] * scale
        send(normal_out.at[:, at : at + size], normal_ref.at[:, at : at + size])
        send(right_side_out.at[:, at : at + size], right_side_ref.at[:, at : at + size])
    for copy in copies:
        copy.wait()


def swapped(value, axis, distance):
    return lax.ppermute(value, axis, [(i, i ^ distance) for i in range(lax.axis_size(axis))])


def shifted(value, distance):
    count = lax.axis_size("space")
    return lax.ppermute(value, "space", [(i, (i + distance) % count) for i in range(count)])


def turned(value, distances):
    tm_count = lax.axis_size("tm")
    space_count = lax.axis_size("space")
    perm = []
    for time in range(tm_count):
        for space in range(space_count):
            target = (time + distances[space % 2]) % tm_count
            perm.append((time * space_count + space, target * space_count + space))
    return lax.ppermute(value, ("tm", "space"), perm)


def local(snapshots, modes_basis, reg_weights):
    feature_count = reg_weights.shape[0]
    snaps_dev = snapshots.shape[0]
    modes = modes_basis.shape[1]
    tm_count = lax.axis_size("tm")
    space_count = lax.axis_size("space")
    row_block = feature_count // tm_count
    col_block = feature_count // space_count
    rows = round_up(row_block, 16)
    cols = round_up(col_block, 16)
    depth = round_up(3 * modes + 1, 128)
    time_idx = lax.axis_index("tm")
    vmem = pl.BlockSpec(memory_space=pltpu.VMEM)
    hbm = pl.BlockSpec(memory_space=pltpu.HBM)
    params = pltpu.CompilerParams(vmem_limit_bytes=32 * 1024 * 1024)

    keep, give = project(snapshots, modes_basis.T)
    half = keep + swapped(give, "space", 1)
    after, half = lax.optimization_barrier((time_idx, half))
    selector = jax.ShapeDtypeStruct((cols + rows, depth), jnp.bfloat16)
    left, right = pl.pallas_call(
        functools.partial(selector_kernel, row_block, col_block),
        out_shape=(selector, selector),
        in_specs=[vmem],
        out_specs=(vmem, vmem),
        compiler_params=params,
        cost_estimate=pl.CostEstimate(flops=10**6, bytes_accessed=10**6, transcendentals=0),
        name="selectors",
    )(half)
    first_row = after * row_block
    reg_rows = lax.dynamic_slice_in_dim(reg_weights, first_row, row_block, 0)[None]

    terms = [shifted(half, step) for step in range(2, space_count, 2)]
    terms = [half] + list(lax.optimization_barrier(tuple(terms[::-1]))[::-1])
    while len(terms) > 1:
        middle = len(terms) // 2
        terms = [terms[i] + terms[i + middle] for i in range(middle)]
    mine, left, right, reg_rows = lax.optimization_barrier((terms[0], left, right, reg_rows))
    core = lax.axis_index("space") % 2
    own_other = swapped(mine, "space", 1)
    got_half = turned(mine, (1, 1))
    own = jnp.concatenate(
        [jnp.where(core == 0, mine, own_other), jnp.where(core == 0, own_other, mine)], axis=1
    )
    wholes = [(tm_count - 1 - k, 2 + k) for k in range((tm_count - 2) // 2)]
    got = [turned(own, steps) for steps in wholes]
    acc_shape = jax.ShapeDtypeStruct((cols + modes, rows), jnp.float32)

    def cost(count):
        flops = 2 * count * (2 * depth * (cols + rows) + (cols + modes) * rows)
        return pl.CostEstimate(flops=flops, bytes_accessed=2 * 10**6, transcendentals=0)

    def col_scratch(count):
        return pltpu.VMEM((cols + modes, count), jnp.bfloat16)

    half_snaps = snaps_dev // 2

    def add_terms(acc, blocks):
        count = sum(block.size for block in blocks) // modes
        before = [] if acc is None else [acc]
        return pl.pallas_call(
            functools.partial(halves_kernel, cols, half_snaps, len(before)),
            out_shape=acc_shape,
            in_specs=[vmem] * (2 + len(before) + len(blocks)),
            out_specs=vmem,
            scratch_shapes=[col_scratch(count)],
            input_output_aliases={2: 0} if before else {},
            compiler_params=params,
            cost_estimate=cost(count),
            name="halves",
        )(left, right, *before, *blocks)

    acc = add_terms(None, [own])
    acc, got_half = lax.optimization_barrier((acc, got_half))
    passed_half = swapped(got_half, "space", 1)
    acc = add_terms(acc, [got_half, passed_half])
    acc, *got = lax.optimization_barrier((acc, *got))
    passed = [swapped(block, "space", 1) for block in got]
    acc = add_terms(acc, got)
    width = 128
    starts = list(range(0, row_block - width, 2 * width))
    starts = [0] + [start - width for start in starts[1:]] if len(starts) > 1 else [0]
    ends = starts[1:] + [row_block]
    chunks = [(start, end - start) for start, end in zip(starts, ends)][::-1]
    out_shapes = (
        jax.ShapeDtypeStruct((modes, snaps_dev), jnp.float32),
        jax.ShapeDtypeStruct((modes, snaps_dev), jnp.float32),
        jax.ShapeDtypeStruct((col_block, row_block), jnp.float32),
        jax.ShapeDtypeStruct((modes, row_block), jnp.float32),
    )
    outs = pl.pallas_call(
        functools.partial(last_kernel, row_block, col_block, chunks, wholes),
        out_shape=out_shapes,
        in_specs=[vmem] * (7 + 2 * len(wholes)),
        out_specs=(hbm,) * 4,
        scratch_shapes=[
            pltpu.VMEM((2 * tm_count, modes, width), jnp.float32),
            pltpu.VMEM((2 * tm_count, modes, width), jnp.float32),
            col_scratch(len(wholes) * snaps_dev),
            *[pltpu.VMEM(shape.shape, shape.dtype) for shape in out_shapes[1:]],
            pltpu.SemaphoreType.DMA((2 + 2 * len(chunks),)),
        ],
        compiler_params=params,
        cost_estimate=cost(len(wholes) * snaps_dev),
        name="last_half",
    )(left, right, acc, reg_rows, own, got_half, passed_half, *got, *passed)
    return tuple(out.T for out in outs)


def solution(mesh):
    return jax.shard_map(
        local,
        mesh=mesh,
        in_specs=(P("tm", "space"), P("space", None), P()),
        out_specs=(P("tm", None), P("tm", None), P("tm", "space"), P("tm", None)),
        check_vma=False,
    )
```

```python
import functools

import jax
import jax.numpy as jnp
from jax import lax
from jax.experimental import pallas as pl
from jax.experimental.pallas import tpu as pltpu
from jax.sharding import PartitionSpec as P

NT = (((1,), (1,)), ((), ()))


def round_up(value, step):
    return (value + step - 1) // step * step


def tree_sum(terms):
    while len(terms) > 1:
        terms = [terms[i] + terms[i + 1] for i in range(0, len(terms), 2)]
    return terms[0]


def selectors(first, rows, modes, depth):
    feature = first + lax.broadcasted_iota(jnp.int32, (rows, 1), 0)
    mode = lax.broadcasted_iota(jnp.int32, (1, modes), 1)
    start = modes + mode * modes - (mode * (mode - 1)) // 2
    gap = feature - start
    holds = (gap >= 0) & (gap < modes - mode)
    left = jnp.sum(jnp.where(holds, mode, 0), axis=1, keepdims=True)
    right = left + jnp.sum(jnp.where(holds, gap, 0), axis=1, keepdims=True)
    linear = feature < modes
    left = jnp.where(linear, feature, left)
    right = jnp.where(linear, modes, right)
    lane = lax.broadcasted_iota(jnp.int32, (1, depth), 1)
    held = jnp.where(lane < 3 * modes, lax.rem(lane, modes), lane - 2 * modes)
    return (
        jnp.where(held == left, 1.0, 0.0).astype(jnp.bfloat16),
        jnp.where(held == right, 1.0, 0.0).astype(jnp.bfloat16),
    )


def parts_of(block, depth):
    modes, snaps = block.shape
    high = block.astype(jnp.bfloat16)
    rest = block - high.astype(jnp.float32)
    middle = rest.astype(jnp.bfloat16)
    low = (rest - middle.astype(jnp.float32)).astype(jnp.bfloat16)
    tail = depth - 3 * modes
    ones = jnp.where(lax.broadcasted_iota(jnp.int32, (tail, snaps), 0) == 0, 1.0, 0.0)
    return jnp.concatenate([high, middle, low, ones.astype(jnp.bfloat16)], axis=0)


def picked(left, right, parts):
    first = jnp.dot(left, parts, preferred_element_type=jnp.float32)
    second = jnp.dot(right, parts, preferred_element_type=jnp.float32)
    return (first * second).astype(jnp.bfloat16)


def project_kernel(basis_ref, snaps_ref, keep_ref, give_ref, basis, held, basis_sem, sems):
    core = lax.axis_index("space") % 2
    chunks, size, states = held.shape
    half = chunks // 2 * size
    basis_copy = pltpu.make_async_copy(basis_ref, basis, basis_sem)
    basis_copy.start()
    copies = []
    for chunk in range(chunks):
        side, at = divmod(chunk * size, half)
        first = pl.multiple_of((core if side else 1 - core) * half + at, size)
        copies.append(
            pltpu.make_async_copy(snaps_ref.at[pl.ds(first, size)], held.at[chunk], sems.at[chunk])
        )
        copies[-1].start()
    basis_copy.wait()
    pieces = 4
    step = states // pieces
    for chunk in range(chunks):
        copies[chunk].wait()
        terms = [
            lax.dot_general(
                basis[:, piece * step : (piece + 1) * step],
                held[chunk, :, piece * step : (piece + 1) * step],
                NT,
                preferred_element_type=jnp.float32,
            )
            for piece in range(pieces)
        ]
        side, at = divmod(chunk * size, half)
        (keep_ref if side else give_ref)[:, at : at + size] = tree_sum(terms)


def project(snapshots, basis):
    snaps, states = snapshots.shape
    modes = basis.shape[0]
    size = snaps // 2
    hbm = pl.BlockSpec(memory_space=pltpu.HBM)
    vmem = pl.BlockSpec(memory_space=pltpu.VMEM)
    block = jax.ShapeDtypeStruct((modes, snaps // 2), jnp.float32)
    return pl.pallas_call(
        project_kernel,
        out_shape=(block, block),
        in_specs=[hbm, hbm],
        out_specs=(vmem, vmem),
        scratch_shapes=[
            pltpu.VMEM(basis.shape, basis.dtype),
            pltpu.VMEM((snaps // size, size, states), snapshots.dtype),
            pltpu.SemaphoreType.DMA,
            pltpu.SemaphoreType.DMA((snaps // size,)),
        ],
        compiler_params=pltpu.CompilerParams(vmem_limit_bytes=55000 * 1024),
        name="project",
    )(basis, snapshots)


def selector_kernel(row_block, col_block, after_ref, left_ref, right_ref):
    modes = after_ref.shape[0]
    cols = round_up(col_block, 16)
    rows = left_ref.shape[0] - cols
    depth = left_ref.shape[1]
    for at, size, first in (
        (0, cols, lax.axis_index("space") * col_block),
        (cols, rows, lax.axis_index("tm") * row_block),
    ):
        left, right = selectors(first, size, modes, depth)
        left_ref[at : at + size] = left
        right_ref[at : at + size] = right


def inner_rates(block, half):
    snaps = block.shape[1]
    lane = lax.rem(lax.broadcasted_iota(jnp.int32, (1, snaps), 1), half)
    rates = (pltpu.roll(block, snaps - 1, 1) - pltpu.roll(block, 1, 1)) * 0.5
    return jnp.where((lane == 0) | (lane == half - 1), 0.0, rates)


def column_side(left_ref, right_ref, parts, rates, cols, col_scratch):
    col_scratch[:cols, : rates.shape[1]] = picked(left_ref[:cols], right_ref[:cols], parts)
    col_scratch[cols:, : rates.shape[1]] = rates.astype(jnp.bfloat16)


def terms_of(left_ref, right_ref, block, half, cols, col_scratch):
    parts = parts_of(block, left_ref.shape[1])
    column_side(left_ref, right_ref, parts, inner_rates(block, half), cols, col_scratch)
    row_features = picked(left_ref[cols:], right_ref[cols:], parts)
    return lax.dot_general(
        col_scratch[:, : block.shape[1]], row_features, NT, preferred_element_type=jnp.float32
    )


def halves_kernel(cols, half, has_before, left_ref, right_ref, *refs):
    before_ref, refs = (refs[0], refs[1:]) if has_before else (None, refs)
    block_refs, acc_ref, col_scratch = refs[:-2], refs[-2], refs[-1]
    block = jnp.concatenate([ref[...] for ref in block_refs], axis=1)
    term = terms_of(left_ref, right_ref, block, half, cols, col_scratch)
    acc_ref[...] = before_ref[...] + term if has_before else term


def edge_columns(halves, starts, ends):
    count, modes, width = starts.shape
    for group, side, block in halves:
        at = 2 * group + side
        starts[at] = block[:, :width]
        ends[at] = block[:, block.shape[1] - width :]
    lane = lax.broadcasted_iota(jnp.int32, (1, width), 1)
    heads = jnp.zeros((modes, width), jnp.float32)
    tails = jnp.zeros((modes, width), jnp.float32)
    for at in range(count):
        pair = (lane == 2 * at) | (lane == 2 * at + 1)
        heads = jnp.where(pair, pltpu.roll(starts[at], 2 * at, 1), heads)
        tails = jnp.where(pair, pltpu.roll(ends[at], (2 * at + 2) % width, 1), tails)
    after = pltpu.roll(heads, width - 1, 1)
    before = pltpu.roll(tails, 1, 1)
    rates = (after - before) * 0.5
    rates = jnp.where(lane == 0, after - heads, rates)
    rates = jnp.where(lane == 2 * count - 1, tails - before, rates)
    edge = jnp.where(lax.rem(lane, 2) == 0, heads, tails)
    inside = lane < 2 * count
    return jnp.where(inside, edge, 0.0), jnp.where(inside, rates, 0.0)


def last_kernel(row_block, col_block, chunks, wholes, left_ref, right_ref, before_ref, reg_ref, *refs):
    each = len(wholes)
    own_ref, got_half_ref, passed_half_ref = refs[:3]
    got_refs, passed_refs, refs = refs[3 : 3 + each], refs[3 + each : 3 + 2 * each], refs[3 + 2 * each :]
    reduced_ref, rates_ref, normal_ref, right_side_ref = refs[:4]
    starts, ends, col_scratch, rates_out, normal_out, right_side_out, sems = refs[4:]
    time_idx = lax.axis_index("tm")
    space_idx = lax.axis_index("space")
    core = space_idx % 2
    modes, snaps = own_ref.shape
    half = snaps // 2
    groups = 2 + 2 * each
    cols = round_up(col_block, 16)
    depth = left_ref.shape[1]
    copies = []

    def send(source, target):
        copies.append(pltpu.make_async_copy(source, target, sems.at[len(copies)]))
        copies[-1].start()

    send(own_ref, reduced_ref)

    def group_at(steps, side):
        return lax.rem(time_idx + groups - jnp.where(side == 0, steps[0], steps[1]), groups)

    halves = [
        (group_at((1, 1), 0), core, got_half_ref[...]),
        (group_at((1, 1), 0), 1 - core, passed_half_ref[...]),
    ]
    blocks = [(time_idx, own_ref)]
    blocks += [(group_at(steps, core), ref) for steps, ref in zip(wholes, got_refs)]
    blocks += [(group_at(steps, 1 - core), ref) for steps, ref in zip(wholes, passed_refs)]
    for group, ref in blocks:
        halves += [(group, side, ref[:, side * half : (side + 1) * half]) for side in range(2)]
    edge, edge_rates = edge_columns(halves, starts, ends)
    own = own_ref[...]
    width = edge.shape[1]
    own_edges = pltpu.roll(edge_rates, lax.rem(width - 4 * time_idx, width), 1)
    lane = lax.broadcasted_iota(jnp.int32, (1, snaps), 1)
    rates = jnp.where(lane == 0, own_edges[:, 0:1], inner_rates(own, snaps))
    rates_out[...] = jnp.where(lane == snaps - 1, own_edges[:, 3:4], rates)
    send(rates_out, rates_ref)

    block = jnp.concatenate([ref[...] for ref in passed_refs], axis=1)
    parts = parts_of(block, depth)
    column_side(left_ref, right_ref, parts, inner_rates(block, half), cols, col_scratch)
    scale = 1.0 / (groups * snaps)
    edge_parts = parts_of(edge, depth)
    edge_rates = edge_rates.astype(jnp.bfloat16)
    for at, size in chunks:
        pick = slice(cols + at, cols + at + round_up(size, 16))
        features = picked(left_ref[pick], right_ref[pick], parts)
        edge_features = picked(left_ref[pick], right_ref[pick], edge_parts)
        total = before_ref[:, at : at + features.shape[0]] + lax.dot_general(
            col_scratch[...], features, NT, preferred_element_type=jnp.float32
        )
        edge_total = lax.dot_general(edge_rates, edge_features, NT, preferred_element_type=jnp.float32)
        col_ids = space_idx * col_block + lax.broadcasted_iota(jnp.int32, (col_block, size), 0)
        row_ids = time_idx * row_block + at + lax.broadcasted_iota(jnp.int32, (col_block, size), 1)
        diagonal = jnp.where(row_ids == col_ids, reg_ref[:, at : at + size], 0.0)
        normal_out[:, at : at + size] = total[:col_block, :size] * scale + diagonal
        right_side_out[:, at : at + size] = (total[cols:] + edge_total)[:, :size] * scale
        send(normal_out.at[:, at : at + size], normal_ref.at[:, at : at + size])
        send(right_side_out.at[:, at : at + size], right_side_ref.at[:, at : at + size])
    for copy in copies:
        copy.wait()


def swapped(value, axis, distance):
    return lax.ppermute(value, axis, [(i, i ^ distance) for i in range(lax.axis_size(axis))])


def shifted(value, distance):
    count = lax.axis_size("space")
    return lax.ppermute(value, "space", [(i, (i + distance) % count) for i in range(count)])


def turned(value, distances):
    tm_count = lax.axis_size("tm")
    space_count = lax.axis_size("space")
    perm = []
    for time in range(tm_count):
        for space in range(space_count):
            target = (time + distances[space % 2]) % tm_count
            perm.append((time * space_count + space, target * space_count + space))
    return lax.ppermute(value, ("tm", "space"), perm)


def local(snapshots, modes_basis, reg_weights):
    feature_count = reg_weights.shape[0]
    snaps_dev = snapshots.shape[0]
    modes = modes_basis.shape[1]
    tm_count = lax.axis_size("tm")
    space_count = lax.axis_size("space")
    row_block = feature_count // tm_count
    col_block = feature_count // space_count
    rows = round_up(row_block, 16)
    cols = round_up(col_block, 16)
    depth = round_up(3 * modes + 1, 128)
    time_idx = lax.axis_index("tm")
    vmem = pl.BlockSpec(memory_space=pltpu.VMEM)
    hbm = pl.BlockSpec(memory_space=pltpu.HBM)
    params = pltpu.CompilerParams(vmem_limit_bytes=32 * 1024 * 1024)

    keep, give = project(snapshots, modes_basis.T)
    half = keep + swapped(give, "space", 1)
    after, half = lax.optimization_barrier((time_idx, half))
    selector = jax.ShapeDtypeStruct((cols + rows, depth), jnp.bfloat16)
    left, right = pl.pallas_call(
        functools.partial(selector_kernel, row_block, col_block),
        out_shape=(selector, selector),
        in_specs=[vmem],
        out_specs=(vmem, vmem),
        compiler_params=params,
        cost_estimate=pl.CostEstimate(flops=10**6, bytes_accessed=10**6, transcendentals=0),
        name="selectors",
    )(half)
    first_row = after * row_block
    reg_rows = lax.dynamic_slice_in_dim(reg_weights, first_row, row_block, 0)[None]

    terms = [shifted(half, step) for step in range(2, space_count, 2)]
    terms = [half] + list(lax.optimization_barrier(tuple(terms[::-1]))[::-1])
    while len(terms) > 1:
        middle = len(terms) // 2
        terms = [terms[i] + terms[i + middle] for i in range(middle)]
    mine, left, right, reg_rows = lax.optimization_barrier((terms[0], left, right, reg_rows))
    core = lax.axis_index("space") % 2
    own_other = swapped(mine, "space", 1)
    got_half = turned(mine, (1, 1))
    own = jnp.concatenate(
        [jnp.where(core == 0, mine, own_other), jnp.where(core == 0, own_other, mine)], axis=1
    )
    wholes = [(tm_count - 1 - k, 2 + k) for k in range((tm_count - 2) // 2)]
    got = [turned(own, steps) for steps in wholes]
    acc_shape = jax.ShapeDtypeStruct((cols + modes, rows), jnp.float32)

    def cost(count):
        flops = 4 * count * (2 * depth * (cols + rows) + (cols + modes) * rows)
        return pl.CostEstimate(flops=flops, bytes_accessed=2 * 10**6, transcendentals=0)

    def col_scratch(count):
        return pltpu.VMEM((cols + modes, count), jnp.bfloat16)

    half_snaps = snaps_dev // 2

    def add_terms(acc, blocks):
        count = sum(block.size for block in blocks) // modes
        before = [] if acc is None else [acc]
        return pl.pallas_call(
            functools.partial(halves_kernel, cols, half_snaps, len(before)),
            out_shape=acc_shape,
            in_specs=[vmem] * (2 + len(before) + len(blocks)),
            out_specs=vmem,
            scratch_shapes=[col_scratch(count)],
            input_output_aliases={2: 0} if before else {},
            compiler_params=params,
            cost_estimate=cost(count),
            name="halves",
        )(left, right, *before, *blocks)

    acc = add_terms(None, [own])
    acc, got_half = lax.optimization_barrier((acc, got_half))
    passed_half = swapped(got_half, "space", 1)
    acc = add_terms(acc, [got_half])
    acc, *got = lax.optimization_barrier((acc, *got))
    passed = [swapped(block, "space", 1) for block in got]
    acc = add_terms(acc, [passed_half] + got)
    width = 128
    starts = list(range(0, row_block - width, 2 * width))
    starts = [0] + [start - width for start in starts[1:]] if len(starts) > 1 else [0]
    ends = starts[1:] + [row_block]
    chunks = [(start, end - start) for start, end in zip(starts, ends)][::-1]
    out_shapes = (
        jax.ShapeDtypeStruct((modes, snaps_dev), jnp.float32),
        jax.ShapeDtypeStruct((modes, snaps_dev), jnp.float32),
        jax.ShapeDtypeStruct((col_block, row_block), jnp.float32),
        jax.ShapeDtypeStruct((modes, row_block), jnp.float32),
    )
    outs = pl.pallas_call(
        functools.partial(last_kernel, row_block, col_block, chunks, wholes),
        out_shape=out_shapes,
        in_specs=[vmem] * (7 + 2 * len(wholes)),
        out_specs=(hbm,) * 4,
        scratch_shapes=[
            pltpu.VMEM((2 * tm_count, modes, width), jnp.float32),
            pltpu.VMEM((2 * tm_count, modes, width), jnp.float32),
            col_scratch(len(wholes) * snaps_dev),
            *[pltpu.VMEM(shape.shape, shape.dtype) for shape in out_shapes[1:]],
            pltpu.SemaphoreType.DMA((2 + 2 * len(chunks),)),
        ],
        compiler_params=params,
        cost_estimate=cost(len(wholes) * snaps_dev),
        name="last_half",
    )(left, right, acc, reg_rows, own, got_half, passed_half, *got, *passed)
    return tuple(out.T for out in outs)


def solution(mesh):
    return jax.shard_map(
        local,
        mesh=mesh,
        in_specs=(P("tm", "space"), P("space", None), P()),
        out_specs=(P("tm", None), P("tm", None), P("tm", "space"), P("tm", None)),
        check_vma=False,
    )
```

```python
import functools

import jax
import jax.numpy as jnp
from jax import lax
from jax.experimental import pallas as pl
from jax.experimental.pallas import tpu as pltpu
from jax.sharding import PartitionSpec as P

NT = (((1,), (1,)), ((), ()))


def round_up(value, step):
    return (value + step - 1) // step * step


def tree_sum(terms):
    while len(terms) > 1:
        terms = [terms[i] + terms[i + 1] for i in range(0, len(terms), 2)]
    return terms[0]


def selectors(first, rows, modes, depth):
    feature = first + lax.broadcasted_iota(jnp.int32, (rows, 1), 0)
    mode = lax.broadcasted_iota(jnp.int32, (1, modes), 1)
    start = modes + mode * modes - (mode * (mode - 1)) // 2
    gap = feature - start
    holds = (gap >= 0) & (gap < modes - mode)
    left = jnp.sum(jnp.where(holds, mode, 0), axis=1, keepdims=True)
    right = left + jnp.sum(jnp.where(holds, gap, 0), axis=1, keepdims=True)
    linear = feature < modes
    left = jnp.where(linear, feature, left)
    right = jnp.where(linear, modes, right)
    lane = lax.broadcasted_iota(jnp.int32, (1, depth), 1)
    held = jnp.where(lane < 3 * modes, lax.rem(lane, modes), lane - 2 * modes)
    return (
        jnp.where(held == left, 1.0, 0.0).astype(jnp.bfloat16),
        jnp.where(held == right, 1.0, 0.0).astype(jnp.bfloat16),
    )


def parts_of(block, depth):
    modes, snaps = block.shape
    high = block.astype(jnp.bfloat16)
    rest = block - high.astype(jnp.float32)
    middle = rest.astype(jnp.bfloat16)
    low = (rest - middle.astype(jnp.float32)).astype(jnp.bfloat16)
    tail = depth - 3 * modes
    ones = jnp.where(lax.broadcasted_iota(jnp.int32, (tail, snaps), 0) == 0, 1.0, 0.0)
    return jnp.concatenate([high, middle, low, ones.astype(jnp.bfloat16)], axis=0)


def picked(left, right, parts):
    first = jnp.dot(left, parts, preferred_element_type=jnp.float32)
    second = jnp.dot(right, parts, preferred_element_type=jnp.float32)
    return (first * second).astype(jnp.bfloat16)


def project_kernel(basis_ref, snaps_ref, keep_ref, give_ref, basis, held, basis_sem, sems):
    core = lax.axis_index("space") % 2
    half = held.shape[0] // 2
    states = held.shape[1]
    basis_copy = pltpu.make_async_copy(basis_ref, basis, basis_sem)
    basis_copy.start()
    copies = []
    for slot, (side, at, size) in enumerate(((0, 0, half), (1, 0, half // 2), (1, half // 2, half // 2))):
        first = pl.multiple_of((core if side else 1 - core) * half + at, size)
        rows = held.at[pl.ds(side * half + at, size)]
        copies.append(
            (side, at, size, pltpu.make_async_copy(snaps_ref.at[pl.ds(first, size)], rows, sems.at[slot]))
        )
        copies[-1][-1].start()
    basis_copy.wait()
    pieces = 4
    step = states // pieces
    for side, at, size, copy in copies:
        copy.wait()
        rows = slice(side * half + at, side * half + at + size)
        terms = [
            lax.dot_general(
                basis[:, piece * step : (piece + 1) * step],
                held[rows, piece * step : (piece + 1) * step],
                NT,
                preferred_element_type=jnp.float32,
            )
            for piece in range(pieces)
        ]
        (keep_ref if side else give_ref)[:, at : at + size] = tree_sum(terms)


def project(snapshots, basis):
    snaps, states = snapshots.shape
    modes = basis.shape[0]
    hbm = pl.BlockSpec(memory_space=pltpu.HBM)
    vmem = pl.BlockSpec(memory_space=pltpu.VMEM)
    block = jax.ShapeDtypeStruct((modes, snaps // 2), jnp.float32)
    return pl.pallas_call(
        project_kernel,
        out_shape=(block, block),
        in_specs=[hbm, hbm],
        out_specs=(vmem, vmem),
        scratch_shapes=[
            pltpu.VMEM(basis.shape, basis.dtype),
            pltpu.VMEM((snaps, states), snapshots.dtype),
            pltpu.SemaphoreType.DMA,
            pltpu.SemaphoreType.DMA((3,)),
        ],
        compiler_params=pltpu.CompilerParams(vmem_limit_bytes=55000 * 1024),
        name="project",
    )(basis, snapshots)


def selector_kernel(row_block, col_block, after_ref, left_ref, right_ref):
    modes = after_ref.shape[0]
    cols = round_up(col_block, 16)
    rows = left_ref.shape[0] - cols
    depth = left_ref.shape[1]
    for at, size, first in (
        (0, cols, lax.axis_index("space") * col_block),
        (cols, rows, lax.axis_index("tm") * row_block),
    ):
        left, right = selectors(first, size, modes, depth)
        left_ref[at : at + size] = left
        right_ref[at : at + size] = right


def inner_rates(block, half):
    snaps = block.shape[1]
    lane = lax.rem(lax.broadcasted_iota(jnp.int32, (1, snaps), 1), half)
    rates = (pltpu.roll(block, snaps - 1, 1) - pltpu.roll(block, 1, 1)) * 0.5
    return jnp.where((lane == 0) | (lane == half - 1), 0.0, rates)


def column_side(left_ref, right_ref, parts, rates, cols, col_scratch):
    col_scratch[:cols, : rates.shape[1]] = picked(left_ref[:cols], right_ref[:cols], parts)
    col_scratch[cols:, : rates.shape[1]] = rates.astype(jnp.bfloat16)


def terms_of(left_ref, right_ref, block, half, cols, col_scratch):
    parts = parts_of(block, left_ref.shape[1])
    column_side(left_ref, right_ref, parts, inner_rates(block, half), cols, col_scratch)
    row_features = picked(left_ref[cols:], right_ref[cols:], parts)
    return lax.dot_general(
        col_scratch[:, : block.shape[1]], row_features, NT, preferred_element_type=jnp.float32
    )


def halves_kernel(cols, half, has_before, left_ref, right_ref, *refs):
    before_ref, refs = (refs[0], refs[1:]) if has_before else (None, refs)
    block_refs, acc_ref, col_scratch = refs[:-2], refs[-2], refs[-1]
    block = jnp.concatenate([ref[...] for ref in block_refs], axis=1)
    term = terms_of(left_ref, right_ref, block, half, cols, col_scratch)
    acc_ref[...] = before_ref[...] + term if has_before else term


def own_kernel(cols, half, left_ref, right_ref, own_ref, acc_ref, reduced_ref, col_scratch, sem):
    copy = pltpu.make_async_copy(own_ref, reduced_ref, sem)
    copy.start()
    acc_ref[...] = terms_of(left_ref, right_ref, own_ref[...], half, cols, col_scratch)
    copy.wait()


def edge_columns(halves, starts, ends):
    count, modes, width = starts.shape
    for group, side, block in halves:
        at = 2 * group + side
        starts[at] = block[:, :width]
        ends[at] = block[:, block.shape[1] - width :]
    lane = lax.broadcasted_iota(jnp.int32, (1, width), 1)
    heads = jnp.zeros((modes, width), jnp.float32)
    tails = jnp.zeros((modes, width), jnp.float32)
    for at in range(count):
        pair = (lane == 2 * at) | (lane == 2 * at + 1)
        heads = jnp.where(pair, pltpu.roll(starts[at], 2 * at, 1), heads)
        tails = jnp.where(pair, pltpu.roll(ends[at], (2 * at + 2) % width, 1), tails)
    after = pltpu.roll(heads, width - 1, 1)
    before = pltpu.roll(tails, 1, 1)
    rates = (after - before) * 0.5
    rates = jnp.where(lane == 0, after - heads, rates)
    rates = jnp.where(lane == 2 * count - 1, tails - before, rates)
    edge = jnp.where(lax.rem(lane, 2) == 0, heads, tails)
    inside = lane < 2 * count
    return jnp.where(inside, edge, 0.0), jnp.where(inside, rates, 0.0)


def last_kernel(row_block, col_block, chunks, wholes, left_ref, right_ref, before_ref, reg_ref, *refs):
    each = len(wholes)
    own_ref, got_half_ref, passed_half_ref = refs[:3]
    got_refs, passed_refs, refs = refs[3 : 3 + each], refs[3 + each : 3 + 2 * each], refs[3 + 2 * each :]
    rates_ref, normal_ref, right_side_ref = refs[:3]
    starts, ends, col_scratch, rates_out, normal_out, right_side_out, sems = refs[3:]
    time_idx = lax.axis_index("tm")
    space_idx = lax.axis_index("space")
    core = space_idx % 2
    modes, snaps = own_ref.shape
    half = snaps // 2
    groups = 2 + 2 * each
    cols = round_up(col_block, 16)
    depth = left_ref.shape[1]
    copies = []

    def send(source, target):
        copies.append(pltpu.make_async_copy(source, target, sems.at[len(copies)]))
        copies[-1].start()

    def group_at(steps, side):
        return lax.rem(time_idx + groups - jnp.where(side == 0, steps[0], steps[1]), groups)

    halves = [
        (group_at((1, 1), 0), core, got_half_ref[...]),
        (group_at((1, 1), 0), 1 - core, passed_half_ref[...]),
    ]
    blocks = [(time_idx, own_ref)]
    blocks += [(group_at(steps, core), ref) for steps, ref in zip(wholes, got_refs)]
    blocks += [(group_at(steps, 1 - core), ref) for steps, ref in zip(wholes, passed_refs)]
    for group, ref in blocks:
        halves += [(group, side, ref[:, side * half : (side + 1) * half]) for side in range(2)]
    edge, edge_rates = edge_columns(halves, starts, ends)
    own = own_ref[...]
    width = edge.shape[1]
    own_edges = pltpu.roll(edge_rates, lax.rem(width - 4 * time_idx, width), 1)
    lane = lax.broadcasted_iota(jnp.int32, (1, snaps), 1)
    rates = jnp.where(lane == 0, own_edges[:, 0:1], inner_rates(own, snaps))
    rates_out[...] = jnp.where(lane == snaps - 1, own_edges[:, 3:4], rates)
    send(rates_out, rates_ref)

    block = jnp.concatenate([ref[...] for ref in passed_refs], axis=1)
    parts = parts_of(block, depth)
    column_side(left_ref, right_ref, parts, inner_rates(block, half), cols, col_scratch)
    scale = 1.0 / (groups * snaps)
    edge_parts = parts_of(edge, depth)
    edge_rates = edge_rates.astype(jnp.bfloat16)
    for at, size in chunks:
        pick = slice(cols + at, cols + at + round_up(size, 16))
        features = picked(left_ref[pick], right_ref[pick], parts)
        edge_features = picked(left_ref[pick], right_ref[pick], edge_parts)
        total = before_ref[:, at : at + features.shape[0]] + lax.dot_general(
            col_scratch[...], features, NT, preferred_element_type=jnp.float32
        )
        edge_total = lax.dot_general(edge_rates, edge_features, NT, preferred_element_type=jnp.float32)
        col_ids = space_idx * col_block + lax.broadcasted_iota(jnp.int32, (col_block, size), 0)
        row_ids = time_idx * row_block + at + lax.broadcasted_iota(jnp.int32, (col_block, size), 1)
        diagonal = jnp.where(row_ids == col_ids, reg_ref[:, at : at + size], 0.0)
        normal_out[:, at : at + size] = total[:col_block, :size] * scale + diagonal
        right_side_out[:, at : at + size] = (total[cols:] + edge_total)[:, :size] * scale
        send(normal_out.at[:, at : at + size], normal_ref.at[:, at : at + size])
        send(right_side_out.at[:, at : at + size], right_side_ref.at[:, at : at + size])
    for copy in copies:
        copy.wait()


def swapped(value, axis, distance):
    return lax.ppermute(value, axis, [(i, i ^ distance) for i in range(lax.axis_size(axis))])


def shifted(value, distance):
    count = lax.axis_size("space")
    return lax.ppermute(value, "space", [(i, (i + distance) % count) for i in range(count)])


def turned(value, distances):
    tm_count = lax.axis_size("tm")
    space_count = lax.axis_size("space")
    perm = []
    for time in range(tm_count):
        for space in range(space_count):
            target = (time + distances[space % 2]) % tm_count
            perm.append((time * space_count + space, target * space_count + space))
    return lax.ppermute(value, ("tm", "space"), perm)


def local(snapshots, modes_basis, reg_weights):
    feature_count = reg_weights.shape[0]
    snaps_dev = snapshots.shape[0]
    modes = modes_basis.shape[1]
    tm_count = lax.axis_size("tm")
    space_count = lax.axis_size("space")
    row_block = feature_count // tm_count
    col_block = feature_count // space_count
    rows = round_up(row_block, 16)
    cols = round_up(col_block, 16)
    depth = round_up(3 * modes + 1, 128)
    time_idx = lax.axis_index("tm")
    vmem = pl.BlockSpec(memory_space=pltpu.VMEM)
    hbm = pl.BlockSpec(memory_space=pltpu.HBM)
    params = pltpu.CompilerParams(vmem_limit_bytes=32 * 1024 * 1024)

    keep, give = project(snapshots, modes_basis.T)
    half = keep + swapped(give, "space", 1)
    after, half = lax.optimization_barrier((time_idx, half))
    selector = jax.ShapeDtypeStruct((cols + rows, depth), jnp.bfloat16)
    left, right = pl.pallas_call(
        functools.partial(selector_kernel, row_block, col_block),
        out_shape=(selector, selector),
        in_specs=[vmem],
        out_specs=(vmem, vmem),
        compiler_params=params,
        cost_estimate=pl.CostEstimate(flops=10**6, bytes_accessed=10**6, transcendentals=0),
        name="selectors",
    )(half)
    first_row = after * row_block
    reg_rows = lax.dynamic_slice_in_dim(reg_weights, first_row, row_block, 0)[None]

    terms = [shifted(half, step) for step in range(2, space_count, 2)]
    terms = [half] + list(lax.optimization_barrier(tuple(terms[::-1]))[::-1])
    while len(terms) > 1:
        middle = len(terms) // 2
        terms = [terms[i] + terms[i + middle] for i in range(middle)]
    mine, left, right, reg_rows = lax.optimization_barrier((terms[0], left, right, reg_rows))
    core = lax.axis_index("space") % 2
    own_other = swapped(mine, "space", 1)
    got_half = turned(mine, (1, 1))
    own = jnp.concatenate(
        [jnp.where(core == 0, mine, own_other), jnp.where(core == 0, own_other, mine)], axis=1
    )
    wholes = [(tm_count - 1 - k, 2 + k) for k in range((tm_count - 2) // 2)]
    got = [turned(own, steps) for steps in wholes]
    acc_shape = jax.ShapeDtypeStruct((cols + modes, rows), jnp.float32)

    def cost(count):
        flops = 4 * count * (2 * depth * (cols + rows) + (cols + modes) * rows)
        return pl.CostEstimate(flops=flops, bytes_accessed=2 * 10**6, transcendentals=0)

    def col_scratch(count):
        return pltpu.VMEM((cols + modes, count), jnp.bfloat16)

    half_snaps = snaps_dev // 2

    def add_terms(acc, blocks):
        count = sum(block.size for block in blocks) // modes
        before = [] if acc is None else [acc]
        return pl.pallas_call(
            functools.partial(halves_kernel, cols, half_snaps, len(before)),
            out_shape=acc_shape,
            in_specs=[vmem] * (2 + len(before) + len(blocks)),
            out_specs=vmem,
            scratch_shapes=[col_scratch(count)],
            input_output_aliases={2: 0} if before else {},
            compiler_params=params,
            cost_estimate=cost(count),
            name="halves",
        )(left, right, *before, *blocks)

    block_shape = jax.ShapeDtypeStruct((modes, snaps_dev), jnp.float32)
    acc, reduced = pl.pallas_call(
        functools.partial(own_kernel, cols, half_snaps),
        out_shape=(acc_shape, block_shape),
        in_specs=[vmem] * 3,
        out_specs=(vmem, hbm),
        scratch_shapes=[col_scratch(snaps_dev), pltpu.SemaphoreType.DMA],
        compiler_params=params,
        cost_estimate=cost(snaps_dev),
        name="own_group",
    )(left, right, own)
    acc, got_half = lax.optimization_barrier((acc, got_half))
    passed_half = swapped(got_half, "space", 1)
    acc = add_terms(acc, [got_half])
    acc, *got = lax.optimization_barrier((acc, *got))
    passed = [swapped(block, "space", 1) for block in got]
    acc = add_terms(acc, [passed_half] + got)
    width = 128
    starts = list(range(0, row_block - width, 2 * width))
    starts = [0] + [start - width for start in starts[1:]] if len(starts) > 1 else [0]
    ends = starts[1:] + [row_block]
    chunks = [(start, end - start) for start, end in zip(starts, ends)][::-1]
    out_shapes = (
        block_shape,
        jax.ShapeDtypeStruct((col_block, row_block), jnp.float32),
        jax.ShapeDtypeStruct((modes, row_block), jnp.float32),
    )
    outs = pl.pallas_call(
        functools.partial(last_kernel, row_block, col_block, chunks, wholes),
        out_shape=out_shapes,
        in_specs=[vmem] * (7 + 2 * len(wholes)),
        out_specs=(hbm,) * 3,
        scratch_shapes=[
            pltpu.VMEM((2 * tm_count, modes, width), jnp.float32),
            pltpu.VMEM((2 * tm_count, modes, width), jnp.float32),
            col_scratch(len(wholes) * snaps_dev),
            *[pltpu.VMEM(shape.shape, shape.dtype) for shape in out_shapes],
            pltpu.SemaphoreType.DMA((1 + 2 * len(chunks),)),
        ],
        compiler_params=params,
        cost_estimate=cost(len(wholes) * snaps_dev),
        name="last_half",
    )(left, right, acc, reg_rows, own, got_half, passed_half, *got, *passed)
    return tuple(out.T for out in (reduced, *outs))


def solution(mesh):
    return jax.shard_map(
        local,
        mesh=mesh,
        in_specs=(P("tm", "space"), P("space", None), P()),
        out_specs=(P("tm", None), P("tm", None), P("tm", "space"), P("tm", None)),
        check_vma=False,
    )
```

```python
import functools

import jax
import jax.numpy as jnp
from jax import lax
from jax.experimental import pallas as pl
from jax.experimental.pallas import tpu as pltpu
from jax.sharding import PartitionSpec as P

NT = (((1,), (1,)), ((), ()))


def round_up(value, step):
    return (value + step - 1) // step * step


def tree_sum(terms):
    while len(terms) > 1:
        terms = [terms[i] + terms[i + 1] for i in range(0, len(terms), 2)]
    return terms[0]


def selectors(first, rows, modes, depth):
    feature = first + lax.broadcasted_iota(jnp.int32, (rows, 1), 0)
    mode = lax.broadcasted_iota(jnp.int32, (1, modes), 1)
    start = modes + mode * modes - (mode * (mode - 1)) // 2
    gap = feature - start
    holds = (gap >= 0) & (gap < modes - mode)
    left = jnp.sum(jnp.where(holds, mode, 0), axis=1, keepdims=True)
    right = left + jnp.sum(jnp.where(holds, gap, 0), axis=1, keepdims=True)
    linear = feature < modes
    left = jnp.where(linear, feature, left)
    right = jnp.where(linear, modes, right)
    lane = lax.broadcasted_iota(jnp.int32, (1, depth), 1)
    held = jnp.where(lane < 3 * modes, lax.rem(lane, modes), lane - 2 * modes)
    return (
        jnp.where(held == left, 1.0, 0.0).astype(jnp.bfloat16),
        jnp.where(held == right, 1.0, 0.0).astype(jnp.bfloat16),
    )


def parts_of(block, depth):
    modes, snaps = block.shape
    high = block.astype(jnp.bfloat16)
    rest = block - high.astype(jnp.float32)
    middle = rest.astype(jnp.bfloat16)
    low = (rest - middle.astype(jnp.float32)).astype(jnp.bfloat16)
    tail = depth - 3 * modes
    ones = jnp.where(lax.broadcasted_iota(jnp.int32, (tail, snaps), 0) == 0, 1.0, 0.0)
    return jnp.concatenate([high, middle, low, ones.astype(jnp.bfloat16)], axis=0)


def picked(left, right, parts):
    first = jnp.dot(left, parts, preferred_element_type=jnp.float32)
    second = jnp.dot(right, parts, preferred_element_type=jnp.float32)
    return (first * second).astype(jnp.bfloat16)


def project_kernel(basis_ref, snaps_ref, keep_ref, give_ref, basis, held, basis_sem, sems):
    core = lax.axis_index("space") % 2
    half = held.shape[0] // 2
    states = held.shape[1]
    basis_copy = pltpu.make_async_copy(basis_ref, basis, basis_sem)
    basis_copy.start()
    copies = []
    for slot, (side, at, size) in enumerate(((0, 0, half), (1, 0, half))):
        first = pl.multiple_of((core if side else 1 - core) * half + at, size)
        rows = held.at[pl.ds(side * half + at, size)]
        copies.append(
            (side, at, size, pltpu.make_async_copy(snaps_ref.at[pl.ds(first, size)], rows, sems.at[slot]))
        )
        copies[-1][-1].start()
    basis_copy.wait()
    pieces = 4
    step = states // pieces
    for side, at, size, copy in copies:
        copy.wait()
        rows = slice(side * half + at, side * half + at + size)
        terms = [
            lax.dot_general(
                basis[:, piece * step : (piece + 1) * step],
                held[rows, piece * step : (piece + 1) * step],
                NT,
                preferred_element_type=jnp.float32,
            )
            for piece in range(pieces)
        ]
        (keep_ref if side else give_ref)[:, at : at + size] = tree_sum(terms)


def project(snapshots, basis):
    snaps, states = snapshots.shape
    modes = basis.shape[0]
    hbm = pl.BlockSpec(memory_space=pltpu.HBM)
    vmem = pl.BlockSpec(memory_space=pltpu.VMEM)
    block = jax.ShapeDtypeStruct((modes, snaps // 2), jnp.float32)
    return pl.pallas_call(
        project_kernel,
        out_shape=(block, block),
        in_specs=[hbm, hbm],
        out_specs=(vmem, vmem),
        scratch_shapes=[
            pltpu.VMEM(basis.shape, basis.dtype),
            pltpu.VMEM((snaps, states), snapshots.dtype),
            pltpu.SemaphoreType.DMA,
            pltpu.SemaphoreType.DMA((2,)),
        ],
        compiler_params=pltpu.CompilerParams(vmem_limit_bytes=55000 * 1024),
        name="project",
    )(basis, snapshots)


def selector_kernel(row_block, col_block, after_ref, left_ref, right_ref):
    modes = after_ref.shape[0]
    cols = round_up(col_block, 16)
    rows = left_ref.shape[0] - cols
    depth = left_ref.shape[1]
    for at, size, first in (
        (0, cols, lax.axis_index("space") * col_block),
        (cols, rows, lax.axis_index("tm") * row_block),
    ):
        left, right = selectors(first, size, modes, depth)
        left_ref[at : at + size] = left
        right_ref[at : at + size] = right


def inner_rates(block, half):
    snaps = block.shape[1]
    lane = lax.rem(lax.broadcasted_iota(jnp.int32, (1, snaps), 1), half)
    rates = (pltpu.roll(block, snaps - 1, 1) - pltpu.roll(block, 1, 1)) * 0.5
    return jnp.where((lane == 0) | (lane == half - 1), 0.0, rates)


def column_side(left_ref, right_ref, parts, rates, cols, col_scratch):
    col_scratch[:cols, : rates.shape[1]] = picked(left_ref[:cols], right_ref[:cols], parts)
    col_scratch[cols:, : rates.shape[1]] = rates.astype(jnp.bfloat16)


def terms_of(left_ref, right_ref, block, half, cols, col_scratch):
    parts = parts_of(block, left_ref.shape[1])
    column_side(left_ref, right_ref, parts, inner_rates(block, half), cols, col_scratch)
    row_features = picked(left_ref[cols:], right_ref[cols:], parts)
    return lax.dot_general(
        col_scratch[:, : block.shape[1]], row_features, NT, preferred_element_type=jnp.float32
    )


def halves_kernel(cols, half, has_before, left_ref, right_ref, *refs):
    before_ref, refs = (refs[0], refs[1:]) if has_before else (None, refs)
    block_refs, acc_ref, col_scratch = refs[:-2], refs[-2], refs[-1]
    block = jnp.concatenate([ref[...] for ref in block_refs], axis=1)
    term = terms_of(left_ref, right_ref, block, half, cols, col_scratch)
    acc_ref[...] = before_ref[...] + term if has_before else term


def own_kernel(cols, half, left_ref, right_ref, own_ref, acc_ref, reduced_ref, col_scratch, sem):
    copy = pltpu.make_async_copy(own_ref, reduced_ref, sem)
    copy.start()
    acc_ref[...] = terms_of(left_ref, right_ref, own_ref[...], half, cols, col_scratch)
    copy.wait()


def edge_columns(halves, starts, ends):
    count, modes, width = starts.shape
    for group, side, block in halves:
        at = 2 * group + side
        starts[at] = block[:, :width]
        ends[at] = block[:, block.shape[1] - width :]
    lane = lax.broadcasted_iota(jnp.int32, (1, width), 1)
    heads = jnp.zeros((modes, width), jnp.float32)
    tails = jnp.zeros((modes, width), jnp.float32)
    for at in range(count):
        pair = (lane == 2 * at) | (lane == 2 * at + 1)
        heads = jnp.where(pair, pltpu.roll(starts[at], 2 * at, 1), heads)
        tails = jnp.where(pair, pltpu.roll(ends[at], (2 * at + 2) % width, 1), tails)
    after = pltpu.roll(heads, width - 1, 1)
    before = pltpu.roll(tails, 1, 1)
    rates = (after - before) * 0.5
    rates = jnp.where(lane == 0, after - heads, rates)
    rates = jnp.where(lane == 2 * count - 1, tails - before, rates)
    edge = jnp.where(lax.rem(lane, 2) == 0, heads, tails)
    inside = lane < 2 * count
    return jnp.where(inside, edge, 0.0), jnp.where(inside, rates, 0.0)


def last_kernel(row_block, col_block, chunks, wholes, left_ref, right_ref, before_ref, reg_ref, *refs):
    each = len(wholes)
    own_ref, got_half_ref, passed_half_ref = refs[:3]
    got_refs, passed_refs, refs = refs[3 : 3 + each], refs[3 + each : 3 + 2 * each], refs[3 + 2 * each :]
    rates_ref, normal_ref, right_side_ref = refs[:3]
    starts, ends, col_scratch, rates_out, normal_out, right_side_out, sems = refs[3:]
    time_idx = lax.axis_index("tm")
    space_idx = lax.axis_index("space")
    core = space_idx % 2
    modes, snaps = own_ref.shape
    half = snaps // 2
    groups = 2 + 2 * each
    cols = round_up(col_block, 16)
    depth = left_ref.shape[1]
    copies = []

    def send(source, target):
        copies.append(pltpu.make_async_copy(source, target, sems.at[len(copies)]))
        copies[-1].start()

    def group_at(steps, side):
        return lax.rem(time_idx + groups - jnp.where(side == 0, steps[0], steps[1]), groups)

    halves = [
        (group_at((1, 1), 0), core, got_half_ref[...]),
        (group_at((1, 1), 0), 1 - core, passed_half_ref[...]),
    ]
    blocks = [(time_idx, own_ref)]
    blocks += [(group_at(steps, core), ref) for steps, ref in zip(wholes, got_refs)]
    blocks += [(group_at(steps, 1 - core), ref) for steps, ref in zip(wholes, passed_refs)]
    for group, ref in blocks:
        halves += [(group, side, ref[:, side * half : (side + 1) * half]) for side in range(2)]
    edge, edge_rates = edge_columns(halves, starts, ends)
    own = own_ref[...]
    width = edge.shape[1]
    own_edges = pltpu.roll(edge_rates, lax.rem(width - 4 * time_idx, width), 1)
    lane = lax.broadcasted_iota(jnp.int32, (1, snaps), 1)
    rates = jnp.where(lane == 0, own_edges[:, 0:1], inner_rates(own, snaps))
    rates_out[...] = jnp.where(lane == snaps - 1, own_edges[:, 3:4], rates)
    send(rates_out, rates_ref)

    block = jnp.concatenate([ref[...] for ref in passed_refs], axis=1)
    parts = parts_of(block, depth)
    column_side(left_ref, right_ref, parts, inner_rates(block, half), cols, col_scratch)
    scale = 1.0 / (groups * snaps)
    edge_parts = parts_of(edge, depth)
    edge_rates = edge_rates.astype(jnp.bfloat16)
    for at, size in chunks:
        pick = slice(cols + at, cols + at + round_up(size, 16))
        features = picked(left_ref[pick], right_ref[pick], parts)
        edge_features = picked(left_ref[pick], right_ref[pick], edge_parts)
        total = before_ref[:, at : at + features.shape[0]] + lax.dot_general(
            col_scratch[...], features, NT, preferred_element_type=jnp.float32
        )
        edge_total = lax.dot_general(edge_rates, edge_features, NT, preferred_element_type=jnp.float32)
        col_ids = space_idx * col_block + lax.broadcasted_iota(jnp.int32, (col_block, size), 0)
        row_ids = time_idx * row_block + at + lax.broadcasted_iota(jnp.int32, (col_block, size), 1)
        diagonal = jnp.where(row_ids == col_ids, reg_ref[:, at : at + size], 0.0)
        normal_out[:, at : at + size] = total[:col_block, :size] * scale + diagonal
        right_side_out[:, at : at + size] = (total[cols:] + edge_total)[:, :size] * scale
        send(normal_out.at[:, at : at + size], normal_ref.at[:, at : at + size])
        send(right_side_out.at[:, at : at + size], right_side_ref.at[:, at : at + size])
    for copy in copies:
        copy.wait()


def swapped(value, axis, distance):
    return lax.ppermute(value, axis, [(i, i ^ distance) for i in range(lax.axis_size(axis))])


def shifted(value, distance):
    count = lax.axis_size("space")
    return lax.ppermute(value, "space", [(i, (i + distance) % count) for i in range(count)])


def turned(value, distances):
    tm_count = lax.axis_size("tm")
    space_count = lax.axis_size("space")
    perm = []
    for time in range(tm_count):
        for space in range(space_count):
            target = (time + distances[space % 2]) % tm_count
            perm.append((time * space_count + space, target * space_count + space))
    return lax.ppermute(value, ("tm", "space"), perm)


def local(snapshots, modes_basis, reg_weights):
    feature_count = reg_weights.shape[0]
    snaps_dev = snapshots.shape[0]
    modes = modes_basis.shape[1]
    tm_count = lax.axis_size("tm")
    space_count = lax.axis_size("space")
    row_block = feature_count // tm_count
    col_block = feature_count // space_count
    rows = round_up(row_block, 16)
    cols = round_up(col_block, 16)
    depth = round_up(3 * modes + 1, 128)
    time_idx = lax.axis_index("tm")
    vmem = pl.BlockSpec(memory_space=pltpu.VMEM)
    hbm = pl.BlockSpec(memory_space=pltpu.HBM)
    params = pltpu.CompilerParams(vmem_limit_bytes=32 * 1024 * 1024)

    keep, give = project(snapshots, modes_basis.T)
    half = keep + swapped(give, "space", 1)
    after, half = lax.optimization_barrier((time_idx, half))
    selector = jax.ShapeDtypeStruct((cols + rows, depth), jnp.bfloat16)
    left, right = pl.pallas_call(
        functools.partial(selector_kernel, row_block, col_block),
        out_shape=(selector, selector),
        in_specs=[vmem],
        out_specs=(vmem, vmem),
        compiler_params=params,
        cost_estimate=pl.CostEstimate(flops=10**6, bytes_accessed=10**6, transcendentals=0),
        name="selectors",
    )(half)
    first_row = after * row_block
    reg_rows = lax.dynamic_slice_in_dim(reg_weights, first_row, row_block, 0)[None]

    terms = [shifted(half, step) for step in range(2, space_count, 2)]
    terms = [half] + list(lax.optimization_barrier(tuple(terms[::-1]))[::-1])
    while len(terms) > 1:
        middle = len(terms) // 2
        terms = [terms[i] + terms[i + middle] for i in range(middle)]
    mine, left, right, reg_rows = lax.optimization_barrier((terms[0], left, right, reg_rows))
    core = lax.axis_index("space") % 2
    own_other = swapped(mine, "space", 1)
    got_half = turned(mine, (1, 1))
    own = jnp.concatenate(
        [jnp.where(core == 0, mine, own_other), jnp.where(core == 0, own_other, mine)], axis=1
    )
    wholes = [(tm_count - 1 - k, 2 + k) for k in range((tm_count - 2) // 2)]
    got = [turned(own, steps) for steps in wholes]
    acc_shape = jax.ShapeDtypeStruct((cols + modes, rows), jnp.float32)

    def cost(count):
        flops = 4 * count * (2 * depth * (cols + rows) + (cols + modes) * rows)
        return pl.CostEstimate(flops=flops, bytes_accessed=2 * 10**6, transcendentals=0)

    def col_scratch(count):
        return pltpu.VMEM((cols + modes, count), jnp.bfloat16)

    half_snaps = snaps_dev // 2

    def add_terms(acc, blocks):
        count = sum(block.size for block in blocks) // modes
        before = [] if acc is None else [acc]
        return pl.pallas_call(
            functools.partial(halves_kernel, cols, half_snaps, len(before)),
            out_shape=acc_shape,
            in_specs=[vmem] * (2 + len(before) + len(blocks)),
            out_specs=vmem,
            scratch_shapes=[col_scratch(count)],
            input_output_aliases={2: 0} if before else {},
            compiler_params=params,
            cost_estimate=cost(count),
            name="halves",
        )(left, right, *before, *blocks)

    block_shape = jax.ShapeDtypeStruct((modes, snaps_dev), jnp.float32)
    acc, reduced = pl.pallas_call(
        functools.partial(own_kernel, cols, half_snaps),
        out_shape=(acc_shape, block_shape),
        in_specs=[vmem] * 3,
        out_specs=(vmem, hbm),
        scratch_shapes=[col_scratch(snaps_dev), pltpu.SemaphoreType.DMA],
        compiler_params=params,
        cost_estimate=cost(snaps_dev),
        name="own_group",
    )(left, right, own)
    acc, got_half = lax.optimization_barrier((acc, got_half))
    passed_half = swapped(got_half, "space", 1)
    acc = add_terms(acc, [got_half])
    acc, *got = lax.optimization_barrier((acc, *got))
    passed = [swapped(block, "space", 1) for block in got]
    acc = add_terms(acc, [passed_half] + got)
    width = 128
    chunks = [(0, row_block)]
    out_shapes = (
        block_shape,
        jax.ShapeDtypeStruct((col_block, row_block), jnp.float32),
        jax.ShapeDtypeStruct((modes, row_block), jnp.float32),
    )
    outs = pl.pallas_call(
        functools.partial(last_kernel, row_block, col_block, chunks, wholes),
        out_shape=out_shapes,
        in_specs=[vmem] * (7 + 2 * len(wholes)),
        out_specs=(hbm,) * 3,
        scratch_shapes=[
            pltpu.VMEM((2 * tm_count, modes, width), jnp.float32),
            pltpu.VMEM((2 * tm_count, modes, width), jnp.float32),
            col_scratch(len(wholes) * snaps_dev),
            *[pltpu.VMEM(shape.shape, shape.dtype) for shape in out_shapes],
            pltpu.SemaphoreType.DMA((1 + 2 * len(chunks),)),
        ],
        compiler_params=params,
        cost_estimate=cost(len(wholes) * snaps_dev),
        name="last_half",
    )(left, right, acc, reg_rows, own, got_half, passed_half, *got, *passed)
    return tuple(out.T for out in (reduced, *outs))


def solution(mesh):
    return jax.shard_map(
        local,
        mesh=mesh,
        in_specs=(P("tm", "space"), P("space", None), P()),
        out_specs=(P("tm", None), P("tm", None), P("tm", "space"), P("tm", None)),
        check_vma=False,
    )
```

```python
import functools

import jax
import jax.numpy as jnp
from jax import lax
from jax.experimental import pallas as pl
from jax.experimental.pallas import tpu as pltpu
from jax.sharding import PartitionSpec as P

NT = (((1,), (1,)), ((), ()))


def round_up(value, step):
    return (value + step - 1) // step * step


def tree_sum(terms):
    while len(terms) > 1:
        terms = [terms[i] + terms[i + 1] for i in range(0, len(terms), 2)]
    return terms[0]


def selectors(first, rows, modes, depth):
    feature = first + lax.broadcasted_iota(jnp.int32, (rows, 1), 0)
    mode = lax.broadcasted_iota(jnp.int32, (1, modes), 1)
    start = modes + mode * modes - (mode * (mode - 1)) // 2
    gap = feature - start
    holds = (gap >= 0) & (gap < modes - mode)
    left = jnp.sum(jnp.where(holds, mode, 0), axis=1, keepdims=True)
    right = left + jnp.sum(jnp.where(holds, gap, 0), axis=1, keepdims=True)
    linear = feature < modes
    left = jnp.where(linear, feature, left)
    right = jnp.where(linear, modes, right)
    lane = lax.broadcasted_iota(jnp.int32, (1, depth), 1)
    held = jnp.where(lane < 3 * modes, lax.rem(lane, modes), lane - 2 * modes)
    return (
        jnp.where(held == left, 1.0, 0.0).astype(jnp.bfloat16),
        jnp.where(held == right, 1.0, 0.0).astype(jnp.bfloat16),
    )


def parts_of(block, depth):
    modes, snaps = block.shape
    high = block.astype(jnp.bfloat16)
    rest = block - high.astype(jnp.float32)
    middle = rest.astype(jnp.bfloat16)
    low = (rest - middle.astype(jnp.float32)).astype(jnp.bfloat16)
    tail = depth - 3 * modes
    ones = jnp.where(lax.broadcasted_iota(jnp.int32, (tail, snaps), 0) == 0, 1.0, 0.0)
    return jnp.concatenate([high, middle, low, ones.astype(jnp.bfloat16)], axis=0)


def picked(left, right, parts):
    first = jnp.dot(left, parts, preferred_element_type=jnp.float32)
    second = jnp.dot(right, parts, preferred_element_type=jnp.float32)
    return (first * second).astype(jnp.bfloat16)


def project_kernel(basis_ref, snaps_ref, keep_ref, give_ref, basis, held, basis_sem, sems):
    core = lax.axis_index("space") % 2
    chunks, size, states = held.shape
    half = chunks // 2 * size
    basis_copy = pltpu.make_async_copy(basis_ref, basis, basis_sem)
    basis_copy.start()
    copies = []
    for chunk in range(chunks):
        side, at = divmod(chunk * size, half)
        first = pl.multiple_of((core if side else 1 - core) * half + at, size)
        copies.append(
            pltpu.make_async_copy(snaps_ref.at[pl.ds(first, size)], held.at[chunk], sems.at[chunk])
        )
        copies[-1].start()
    basis_copy.wait()
    pieces = 4
    step = states // pieces
    for chunk in range(chunks):
        copies[chunk].wait()
        terms = [
            lax.dot_general(
                basis[:, piece * step : (piece + 1) * step],
                held[chunk, :, piece * step : (piece + 1) * step],
                NT,
                preferred_element_type=jnp.float32,
            )
            for piece in range(pieces)
        ]
        side, at = divmod(chunk * size, half)
        (keep_ref if side else give_ref)[:, at : at + size] = tree_sum(terms)


def project(snapshots, basis):
    snaps, states = snapshots.shape
    modes = basis.shape[0]
    size = snaps // 2
    hbm = pl.BlockSpec(memory_space=pltpu.HBM)
    vmem = pl.BlockSpec(memory_space=pltpu.VMEM)
    block = jax.ShapeDtypeStruct((modes, snaps // 2), jnp.float32)
    return pl.pallas_call(
        project_kernel,
        out_shape=(block, block),
        in_specs=[hbm, hbm],
        out_specs=(vmem, vmem),
        scratch_shapes=[
            pltpu.VMEM(basis.shape, basis.dtype),
            pltpu.VMEM((snaps // size, size, states), snapshots.dtype),
            pltpu.SemaphoreType.DMA,
            pltpu.SemaphoreType.DMA((snaps // size,)),
        ],
        compiler_params=pltpu.CompilerParams(vmem_limit_bytes=55000 * 1024),
        name="project",
    )(basis, snapshots)


def selector_kernel(row_block, col_block, after_ref, left_ref, right_ref):
    modes = after_ref.shape[0]
    cols = round_up(col_block, 16)
    rows = left_ref.shape[0] - cols
    depth = left_ref.shape[1]
    for at, size, first in (
        (0, cols, lax.axis_index("space") * col_block),
        (cols, rows, lax.axis_index("tm") * row_block),
    ):
        left, right = selectors(first, size, modes, depth)
        left_ref[at : at + size] = left
        right_ref[at : at + size] = right


def inner_rates(block, half):
    snaps = block.shape[1]
    lane = lax.rem(lax.broadcasted_iota(jnp.int32, (1, snaps), 1), half)
    rates = (pltpu.roll(block, snaps - 1, 1) - pltpu.roll(block, 1, 1)) * 0.5
    return jnp.where((lane == 0) | (lane == half - 1), 0.0, rates)


def column_side(left_ref, right_ref, parts, rates, cols, col_scratch):
    col_scratch[:cols, : rates.shape[1]] = picked(left_ref[:cols], right_ref[:cols], parts)
    col_scratch[cols:, : rates.shape[1]] = rates.astype(jnp.bfloat16)


def terms_of(left_ref, right_ref, block, half, cols, col_scratch):
    parts = parts_of(block, left_ref.shape[1])
    column_side(left_ref, right_ref, parts, inner_rates(block, half), cols, col_scratch)
    row_features = picked(left_ref[cols:], right_ref[cols:], parts)
    return lax.dot_general(
        col_scratch[:, : block.shape[1]], row_features, NT, preferred_element_type=jnp.float32
    )


def halves_kernel(cols, half, has_before, left_ref, right_ref, *refs):
    before_ref, refs = (refs[0], refs[1:]) if has_before else (None, refs)
    block_refs, acc_ref, col_scratch = refs[:-2], refs[-2], refs[-1]
    block = jnp.concatenate([ref[...] for ref in block_refs], axis=1)
    term = terms_of(left_ref, right_ref, block, half, cols, col_scratch)
    acc_ref[...] = before_ref[...] + term if has_before else term


def edge_columns(halves, starts, ends):
    count, modes, width = starts.shape
    for group, side, block in halves:
        at = 2 * group + side
        starts[at] = block[:, :width]
        ends[at] = block[:, block.shape[1] - width :]
    lane = lax.broadcasted_iota(jnp.int32, (1, width), 1)
    heads = jnp.zeros((modes, width), jnp.float32)
    tails = jnp.zeros((modes, width), jnp.float32)
    for at in range(count):
        pair = (lane == 2 * at) | (lane == 2 * at + 1)
        heads = jnp.where(pair, pltpu.roll(starts[at], 2 * at, 1), heads)
        tails = jnp.where(pair, pltpu.roll(ends[at], (2 * at + 2) % width, 1), tails)
    after = pltpu.roll(heads, width - 1, 1)
    before = pltpu.roll(tails, 1, 1)
    rates = (after - before) * 0.5
    rates = jnp.where(lane == 0, after - heads, rates)
    rates = jnp.where(lane == 2 * count - 1, tails - before, rates)
    edge = jnp.where(lax.rem(lane, 2) == 0, heads, tails)
    inside = lane < 2 * count
    return jnp.where(inside, edge, 0.0), jnp.where(inside, rates, 0.0)


def last_kernel(row_block, col_block, chunks, wholes, left_ref, right_ref, before_ref, reg_ref, *refs):
    each = len(wholes)
    own_ref, got_half_ref, passed_half_ref = refs[:3]
    got_refs, passed_refs, refs = refs[3 : 3 + each], refs[3 + each : 3 + 2 * each], refs[3 + 2 * each :]
    reduced_ref, rates_ref, normal_ref, right_side_ref = refs[:4]
    starts, ends, col_scratch, rates_out, normal_out, right_side_out, sems = refs[4:]
    time_idx = lax.axis_index("tm")
    space_idx = lax.axis_index("space")
    core = space_idx % 2
    modes, snaps = own_ref.shape
    half = snaps // 2
    groups = 2 + 2 * each
    cols = round_up(col_block, 16)
    depth = left_ref.shape[1]
    copies = []

    def send(source, target):
        copies.append(pltpu.make_async_copy(source, target, sems.at[len(copies)]))
        copies[-1].start()

    send(own_ref, reduced_ref)

    def group_at(steps, side):
        return lax.rem(time_idx + groups - jnp.where(side == 0, steps[0], steps[1]), groups)

    halves = [
        (group_at((1, 1), 0), core, got_half_ref[...]),
        (group_at((1, 1), 0), 1 - core, passed_half_ref[...]),
    ]
    blocks = [(time_idx, own_ref)]
    blocks += [(group_at(steps, core), ref) for steps, ref in zip(wholes, got_refs)]
    blocks += [(group_at(steps, 1 - core), ref) for steps, ref in zip(wholes, passed_refs)]
    for group, ref in blocks:
        halves += [(group, side, ref[:, side * half : (side + 1) * half]) for side in range(2)]
    edge, edge_rates = edge_columns(halves, starts, ends)
    own = own_ref[...]
    width = edge.shape[1]
    own_edges = pltpu.roll(edge_rates, lax.rem(width - 4 * time_idx, width), 1)
    lane = lax.broadcasted_iota(jnp.int32, (1, snaps), 1)
    rates = jnp.where(lane == 0, own_edges[:, 0:1], inner_rates(own, snaps))
    rates_out[...] = jnp.where(lane == snaps - 1, own_edges[:, 3:4], rates)
    send(rates_out, rates_ref)

    block = jnp.concatenate([ref[...] for ref in passed_refs], axis=1)
    parts = parts_of(block, depth)
    column_side(left_ref, right_ref, parts, inner_rates(block, half), cols, col_scratch)
    scale = 1.0 / (groups * snaps)
    edge_parts = parts_of(edge, depth)
    edge_rates = edge_rates.astype(jnp.bfloat16)
    for at, size in chunks:
        pick = slice(cols + at, cols + at + round_up(size, 16))
        features = picked(left_ref[pick], right_ref[pick], parts)
        edge_features = picked(left_ref[pick], right_ref[pick], edge_parts)
        total = before_ref[:, at : at + features.shape[0]] + lax.dot_general(
            col_scratch[...], features, NT, preferred_element_type=jnp.float32
        )
        edge_total = lax.dot_general(edge_rates, edge_features, NT, preferred_element_type=jnp.float32)
        col_ids = space_idx * col_block + lax.broadcasted_iota(jnp.int32, (col_block, size), 0)
        row_ids = time_idx * row_block + at + lax.broadcasted_iota(jnp.int32, (col_block, size), 1)
        diagonal = jnp.where(row_ids == col_ids, reg_ref[:, at : at + size], 0.0)
        normal_out[:, at : at + size] = total[:col_block, :size] * scale + diagonal
        right_side_out[:, at : at + size] = (total[cols:] + edge_total)[:, :size] * scale
        send(normal_out.at[:, at : at + size], normal_ref.at[:, at : at + size])
        send(right_side_out.at[:, at : at + size], right_side_ref.at[:, at : at + size])
    for copy in copies:
        copy.wait()


def swapped(value, axis, distance):
    return lax.ppermute(value, axis, [(i, i ^ distance) for i in range(lax.axis_size(axis))])


def shifted(value, distance):
    count = lax.axis_size("space")
    return lax.ppermute(value, "space", [(i, (i + distance) % count) for i in range(count)])


def turned(value, distances):
    tm_count = lax.axis_size("tm")
    space_count = lax.axis_size("space")
    perm = []
    for time in range(tm_count):
        for space in range(space_count):
            target = (time + distances[space % 2]) % tm_count
            perm.append((time * space_count + space, target * space_count + space))
    return lax.ppermute(value, ("tm", "space"), perm)


def local(snapshots, modes_basis, reg_weights):
    feature_count = reg_weights.shape[0]
    snaps_dev = snapshots.shape[0]
    modes = modes_basis.shape[1]
    tm_count = lax.axis_size("tm")
    space_count = lax.axis_size("space")
    row_block = feature_count // tm_count
    col_block = feature_count // space_count
    rows = round_up(row_block, 16)
    cols = round_up(col_block, 16)
    depth = round_up(3 * modes + 1, 128)
    time_idx = lax.axis_index("tm")
    vmem = pl.BlockSpec(memory_space=pltpu.VMEM)
    hbm = pl.BlockSpec(memory_space=pltpu.HBM)
    params = pltpu.CompilerParams(vmem_limit_bytes=32 * 1024 * 1024)

    keep, give = project(snapshots, modes_basis.T)
    half = keep + swapped(give, "space", 1)
    after, half = lax.optimization_barrier((time_idx, half))
    selector = jax.ShapeDtypeStruct((cols + rows, depth), jnp.bfloat16)
    left, right = pl.pallas_call(
        functools.partial(selector_kernel, row_block, col_block),
        out_shape=(selector, selector),
        in_specs=[vmem],
        out_specs=(vmem, vmem),
        compiler_params=params,
        cost_estimate=pl.CostEstimate(flops=10**6, bytes_accessed=10**6, transcendentals=0),
        name="selectors",
    )(half)
    first_row = after * row_block
    reg_rows = lax.dynamic_slice_in_dim(reg_weights, first_row, row_block, 0)[None]

    terms = [shifted(half, step) for step in range(2, space_count, 2)]
    terms = [half] + list(lax.optimization_barrier(tuple(terms[::-1]))[::-1])
    while len(terms) > 1:
        middle = len(terms) // 2
        terms = [terms[i] + terms[i + middle] for i in range(middle)]
    mine, left, right, reg_rows = lax.optimization_barrier((terms[0], left, right, reg_rows))
    core = lax.axis_index("space") % 2
    own_other = swapped(mine, "space", 1)
    got_half = turned(mine, (1, 1))
    own = jnp.concatenate(
        [jnp.where(core == 0, mine, own_other), jnp.where(core == 0, own_other, mine)], axis=1
    )
    wholes = [(2 + k, tm_count - 1 - k) for k in range((tm_count - 2) // 2)]
    got = [turned(own, steps) for steps in wholes]
    acc_shape = jax.ShapeDtypeStruct((cols + modes, rows), jnp.float32)

    def cost(count):
        flops = 4 * count * (2 * depth * (cols + rows) + (cols + modes) * rows)
        return pl.CostEstimate(flops=flops, bytes_accessed=2 * 10**6, transcendentals=0)

    def col_scratch(count):
        return pltpu.VMEM((cols + modes, count), jnp.bfloat16)

    half_snaps = snaps_dev // 2

    def add_terms(acc, blocks):
        count = sum(block.size for block in blocks) // modes
        before = [] if acc is None else [acc]
        return pl.pallas_call(
            functools.partial(halves_kernel, cols, half_snaps, len(before)),
            out_shape=acc_shape,
            in_specs=[vmem] * (2 + len(before) + len(blocks)),
            out_specs=vmem,
            scratch_shapes=[col_scratch(count)],
            input_output_aliases={2: 0} if before else {},
            compiler_params=params,
            cost_estimate=cost(count),
            name="halves",
        )(left, right, *before, *blocks)

    acc = add_terms(None, [own])
    acc, got_half = lax.optimization_barrier((acc, got_half))
    passed_half = swapped(got_half, "space", 1)
    acc = add_terms(acc, [got_half])
    acc, *got = lax.optimization_barrier((acc, *got))
    passed = [swapped(block, "space", 1) for block in got]
    acc = add_terms(acc, [passed_half] + got)
    width = 128
    starts = list(range(0, row_block - width, 2 * width))
    starts = [0] + [start - width for start in starts[1:]] if len(starts) > 1 else [0]
    ends = starts[1:] + [row_block]
    chunks = [(start, end - start) for start, end in zip(starts, ends)][::-1]
    out_shapes = (
        jax.ShapeDtypeStruct((modes, snaps_dev), jnp.float32),
        jax.ShapeDtypeStruct((modes, snaps_dev), jnp.float32),
        jax.ShapeDtypeStruct((col_block, row_block), jnp.float32),
        jax.ShapeDtypeStruct((modes, row_block), jnp.float32),
    )
    outs = pl.pallas_call(
        functools.partial(last_kernel, row_block, col_block, chunks, wholes),
        out_shape=out_shapes,
        in_specs=[vmem] * (7 + 2 * len(wholes)),
        out_specs=(hbm,) * 4,
        scratch_shapes=[
            pltpu.VMEM((2 * tm_count, modes, width), jnp.float32),
            pltpu.VMEM((2 * tm_count, modes, width), jnp.float32),
            col_scratch(len(wholes) * snaps_dev),
            *[pltpu.VMEM(shape.shape, shape.dtype) for shape in out_shapes[1:]],
            pltpu.SemaphoreType.DMA((2 + 2 * len(chunks),)),
        ],
        compiler_params=params,
        cost_estimate=cost(len(wholes) * snaps_dev),
        name="last_half",
    )(left, right, acc, reg_rows, own, got_half, passed_half, *got, *passed)
    return tuple(out.T for out in outs)


def solution(mesh):
    return jax.shard_map(
        local,
        mesh=mesh,
        in_specs=(P("tm", "space"), P("space", None), P()),
        out_specs=(P("tm", None), P("tm", None), P("tm", "space"), P("tm", None)),
        check_vma=False,
    )
```

```python
import functools

import jax
import jax.numpy as jnp
from jax import lax
from jax.experimental import pallas as pl
from jax.experimental.pallas import tpu as pltpu
from jax.sharding import PartitionSpec as P

NT = (((1,), (1,)), ((), ()))


def round_up(value, step):
    return (value + step - 1) // step * step


def tree_sum(terms):
    while len(terms) > 1:
        terms = [terms[i] + terms[i + 1] for i in range(0, len(terms), 2)]
    return terms[0]


def selectors(first, rows, modes, depth):
    feature = first + lax.broadcasted_iota(jnp.int32, (rows, 1), 0)
    mode = lax.broadcasted_iota(jnp.int32, (1, modes), 1)
    start = modes + mode * modes - (mode * (mode - 1)) // 2
    gap = feature - start
    holds = (gap >= 0) & (gap < modes - mode)
    left = jnp.sum(jnp.where(holds, mode, 0), axis=1, keepdims=True)
    right = left + jnp.sum(jnp.where(holds, gap, 0), axis=1, keepdims=True)
    linear = feature < modes
    left = jnp.where(linear, feature, left)
    right = jnp.where(linear, modes, right)
    lane = lax.broadcasted_iota(jnp.int32, (1, depth), 1)
    held = jnp.where(lane < 3 * modes, lax.rem(lane, modes), lane - 2 * modes)
    return (
        jnp.where(held == left, 1.0, 0.0).astype(jnp.bfloat16),
        jnp.where(held == right, 1.0, 0.0).astype(jnp.bfloat16),
    )


def parts_of(block, depth):
    modes, snaps = block.shape
    high = block.astype(jnp.bfloat16)
    rest = block - high.astype(jnp.float32)
    middle = rest.astype(jnp.bfloat16)
    low = (rest - middle.astype(jnp.float32)).astype(jnp.bfloat16)
    tail = depth - 3 * modes
    ones = jnp.where(lax.broadcasted_iota(jnp.int32, (tail, snaps), 0) == 0, 1.0, 0.0)
    return jnp.concatenate([high, middle, low, ones.astype(jnp.bfloat16)], axis=0)


def picked(left, right, parts):
    first = jnp.dot(left, parts, preferred_element_type=jnp.float32)
    second = jnp.dot(right, parts, preferred_element_type=jnp.float32)
    return (first * second).astype(jnp.bfloat16)


def project_kernel(basis_ref, snaps_ref, keep_ref, give_ref, basis, held, basis_sem, sems):
    core = lax.axis_index("space") % 2
    half = held.shape[0] // 2
    states = held.shape[1]
    basis_copy = pltpu.make_async_copy(basis_ref, basis, basis_sem)
    basis_copy.start()
    copies = []
    for slot, (side, at, size) in enumerate(((0, 0, half), (1, 0, half))):
        first = pl.multiple_of((core if side else 1 - core) * half + at, size)
        rows = held.at[pl.ds(side * half + at, size)]
        copies.append(
            (side, at, size, pltpu.make_async_copy(snaps_ref.at[pl.ds(first, size)], rows, sems.at[slot]))
        )
        copies[-1][-1].start()
    basis_copy.wait()
    pieces = 4
    step = states // pieces
    for side, at, size, copy in copies:
        copy.wait()
        rows = slice(side * half + at, side * half + at + size)
        terms = [
            lax.dot_general(
                basis[:, piece * step : (piece + 1) * step],
                held[rows, piece * step : (piece + 1) * step],
                NT,
                preferred_element_type=jnp.float32,
            )
            for piece in range(pieces)
        ]
        (keep_ref if side else give_ref)[:, at : at + size] = tree_sum(terms)


def project(snapshots, basis):
    snaps, states = snapshots.shape
    modes = basis.shape[0]
    hbm = pl.BlockSpec(memory_space=pltpu.HBM)
    vmem = pl.BlockSpec(memory_space=pltpu.VMEM)
    block = jax.ShapeDtypeStruct((modes, snaps // 2), jnp.float32)
    return pl.pallas_call(
        project_kernel,
        out_shape=(block, block),
        in_specs=[hbm, hbm],
        out_specs=(vmem, vmem),
        scratch_shapes=[
            pltpu.VMEM(basis.shape, basis.dtype),
            pltpu.VMEM((snaps, states), snapshots.dtype),
            pltpu.SemaphoreType.DMA,
            pltpu.SemaphoreType.DMA((2,)),
        ],
        compiler_params=pltpu.CompilerParams(vmem_limit_bytes=55000 * 1024),
        name="project",
    )(basis, snapshots)


def selector_kernel(row_block, col_block, after_ref, left_ref, right_ref):
    modes = after_ref.shape[0]
    cols = round_up(col_block, 16)
    rows = left_ref.shape[0] - cols
    depth = left_ref.shape[1]
    for at, size, first in (
        (0, cols, lax.axis_index("space") * col_block),
        (cols, rows, lax.axis_index("tm") * row_block),
    ):
        left, right = selectors(first, size, modes, depth)
        left_ref[at : at + size] = left
        right_ref[at : at + size] = right


def inner_rates(block, half):
    snaps = block.shape[1]
    lane = lax.rem(lax.broadcasted_iota(jnp.int32, (1, snaps), 1), half)
    rates = (pltpu.roll(block, snaps - 1, 1) - pltpu.roll(block, 1, 1)) * 0.5
    return jnp.where((lane == 0) | (lane == half - 1), 0.0, rates)


def column_side(left_ref, right_ref, parts, rates, cols, col_scratch):
    col_scratch[:cols, : rates.shape[1]] = picked(left_ref[:cols], right_ref[:cols], parts)
    col_scratch[cols:, : rates.shape[1]] = rates.astype(jnp.bfloat16)


def terms_of(left_ref, right_ref, block, half, cols, col_scratch):
    parts = parts_of(block, left_ref.shape[1])
    column_side(left_ref, right_ref, parts, inner_rates(block, half), cols, col_scratch)
    row_features = picked(left_ref[cols:], right_ref[cols:], parts)
    return lax.dot_general(
        col_scratch[:, : block.shape[1]], row_features, NT, preferred_element_type=jnp.float32
    )


def halves_kernel(cols, half, has_before, left_ref, right_ref, *refs):
    before_ref, refs = (refs[0], refs[1:]) if has_before else (None, refs)
    block_refs, acc_ref, col_scratch = refs[:-2], refs[-2], refs[-1]
    block = jnp.concatenate([ref[...] for ref in block_refs], axis=1)
    term = terms_of(left_ref, right_ref, block, half, cols, col_scratch)
    acc_ref[...] = before_ref[...] + term if has_before else term


def own_kernel(cols, half, left_ref, right_ref, own_ref, acc_ref, reduced_ref, col_scratch, sem):
    copy = pltpu.make_async_copy(own_ref, reduced_ref, sem)
    copy.start()
    acc_ref[...] = terms_of(left_ref, right_ref, own_ref[...], half, cols, col_scratch)
    copy.wait()


def edge_columns(halves, starts, ends):
    count, modes, width = starts.shape
    for group, side, block in halves:
        at = 2 * group + side
        starts[at] = block[:, :width]
        ends[at] = block[:, block.shape[1] - width :]
    lane = lax.broadcasted_iota(jnp.int32, (1, width), 1)
    heads = jnp.zeros((modes, width), jnp.float32)
    tails = jnp.zeros((modes, width), jnp.float32)
    for at in range(count):
        pair = (lane == 2 * at) | (lane == 2 * at + 1)
        heads = jnp.where(pair, pltpu.roll(starts[at], 2 * at, 1), heads)
        tails = jnp.where(pair, pltpu.roll(ends[at], (2 * at + 2) % width, 1), tails)
    after = pltpu.roll(heads, width - 1, 1)
    before = pltpu.roll(tails, 1, 1)
    rates = (after - before) * 0.5
    rates = jnp.where(lane == 0, after - heads, rates)
    rates = jnp.where(lane == 2 * count - 1, tails - before, rates)
    edge = jnp.where(lax.rem(lane, 2) == 0, heads, tails)
    inside = lane < 2 * count
    return jnp.where(inside, edge, 0.0), jnp.where(inside, rates, 0.0)


def last_kernel(row_block, col_block, chunks, wholes, left_ref, right_ref, before_ref, reg_ref, *refs):
    each = len(wholes)
    own_ref, got_half_ref, passed_half_ref = refs[:3]
    got_refs, passed_refs, refs = refs[3 : 3 + each], refs[3 + each : 3 + 2 * each], refs[3 + 2 * each :]
    rates_ref, normal_ref, right_side_ref = refs[:3]
    starts, ends, col_scratch, rates_out, normal_out, right_side_out, sems = refs[3:]
    time_idx = lax.axis_index("tm")
    space_idx = lax.axis_index("space")
    core = space_idx % 2
    modes, snaps = own_ref.shape
    half = snaps // 2
    groups = 2 + 2 * each
    cols = round_up(col_block, 16)
    depth = left_ref.shape[1]
    copies = []

    def send(source, target):
        copies.append(pltpu.make_async_copy(source, target, sems.at[len(copies)]))
        copies[-1].start()

    def group_at(steps, side):
        return lax.rem(time_idx + groups - jnp.where(side == 0, steps[0], steps[1]), groups)

    halves = [
        (group_at((1, 1), 0), core, got_half_ref[...]),
        (group_at((1, 1), 0), 1 - core, passed_half_ref[...]),
    ]
    blocks = [(time_idx, own_ref)]
    blocks += [(group_at(steps, core), ref) for steps, ref in zip(wholes, got_refs)]
    blocks += [(group_at(steps, 1 - core), ref) for steps, ref in zip(wholes, passed_refs)]
    for group, ref in blocks:
        halves += [(group, side, ref[:, side * half : (side + 1) * half]) for side in range(2)]
    edge, edge_rates = edge_columns(halves, starts, ends)
    own = own_ref[...]
    width = edge.shape[1]
    own_edges = pltpu.roll(edge_rates, lax.rem(width - 4 * time_idx, width), 1)
    lane = lax.broadcasted_iota(jnp.int32, (1, snaps), 1)
    rates = jnp.where(lane == 0, own_edges[:, 0:1], inner_rates(own, snaps))
    rates_out[...] = jnp.where(lane == snaps - 1, own_edges[:, 3:4], rates)
    send(rates_out, rates_ref)

    block = jnp.concatenate([ref[...] for ref in passed_refs], axis=1)
    parts = parts_of(block, depth)
    column_side(left_ref, right_ref, parts, inner_rates(block, half), cols, col_scratch)
    scale = 1.0 / (groups * snaps)
    edge_parts = parts_of(edge, depth)
    edge_rates = edge_rates.astype(jnp.bfloat16)
    for at, size in chunks:
        pick = slice(cols + at, cols + at + round_up(size, 16))
        features = picked(left_ref[pick], right_ref[pick], parts)
        edge_features = picked(left_ref[pick], right_ref[pick], edge_parts)
        total = before_ref[:, at : at + features.shape[0]] + lax.dot_general(
            col_scratch[...], features, NT, preferred_element_type=jnp.float32
        )
        edge_total = lax.dot_general(edge_rates, edge_features, NT, preferred_element_type=jnp.float32)
        col_ids = space_idx * col_block + lax.broadcasted_iota(jnp.int32, (col_block, size), 0)
        row_ids = time_idx * row_block + at + lax.broadcasted_iota(jnp.int32, (col_block, size), 1)
        diagonal = jnp.where(row_ids == col_ids, reg_ref[:, at : at + size], 0.0)
        normal_out[:, at : at + size] = total[:col_block, :size] * scale + diagonal
        right_side_out[:, at : at + size] = (total[cols:] + edge_total)[:, :size] * scale
        send(normal_out.at[:, at : at + size], normal_ref.at[:, at : at + size])
        send(right_side_out.at[:, at : at + size], right_side_ref.at[:, at : at + size])
    for copy in copies:
        copy.wait()


def swapped(value, axis, distance):
    return lax.ppermute(value, axis, [(i, i ^ distance) for i in range(lax.axis_size(axis))])


def shifted(value, distance):
    count = lax.axis_size("space")
    return lax.ppermute(value, "space", [(i, (i + distance) % count) for i in range(count)])


def turned(value, distances):
    tm_count = lax.axis_size("tm")
    space_count = lax.axis_size("space")
    perm = []
    for time in range(tm_count):
        for space in range(space_count):
            target = (time + distances[space % 2]) % tm_count
            perm.append((time * space_count + space, target * space_count + space))
    return lax.ppermute(value, ("tm", "space"), perm)


def local(snapshots, modes_basis, reg_weights):
    feature_count = reg_weights.shape[0]
    snaps_dev = snapshots.shape[0]
    modes = modes_basis.shape[1]
    tm_count = lax.axis_size("tm")
    space_count = lax.axis_size("space")
    row_block = feature_count // tm_count
    col_block = feature_count // space_count
    rows = round_up(row_block, 16)
    cols = round_up(col_block, 16)
    depth = round_up(3 * modes + 1, 128)
    time_idx = lax.axis_index("tm")
    vmem = pl.BlockSpec(memory_space=pltpu.VMEM)
    hbm = pl.BlockSpec(memory_space=pltpu.HBM)
    params = pltpu.CompilerParams(vmem_limit_bytes=32 * 1024 * 1024)

    keep, give = project(snapshots, modes_basis.T)
    half = keep + swapped(give, "space", 1)
    after, half = lax.optimization_barrier((time_idx, half))
    selector = jax.ShapeDtypeStruct((cols + rows, depth), jnp.bfloat16)
    left, right = pl.pallas_call(
        functools.partial(selector_kernel, row_block, col_block),
        out_shape=(selector, selector),
        in_specs=[vmem],
        out_specs=(vmem, vmem),
        compiler_params=params,
        cost_estimate=pl.CostEstimate(flops=10**6, bytes_accessed=10**6, transcendentals=0),
        name="selectors",
    )(half)
    first_row = after * row_block
    reg_rows = lax.dynamic_slice_in_dim(reg_weights, first_row, row_block, 0)[None]

    terms = [shifted(half, step) for step in range(2, space_count, 2)]
    terms = [half] + list(lax.optimization_barrier(tuple(terms[::-1]))[::-1])
    while len(terms) > 1:
        middle = len(terms) // 2
        terms = [terms[i] + terms[i + middle] for i in range(middle)]
    mine, left, right, reg_rows = lax.optimization_barrier((terms[0], left, right, reg_rows))
    core = lax.axis_index("space") % 2
    own_other = swapped(mine, "space", 1)
    got_half = turned(mine, (1, 1))
    own = jnp.concatenate(
        [jnp.where(core == 0, mine, own_other), jnp.where(core == 0, own_other, mine)], axis=1
    )
    wholes = [(tm_count - 1 - k, 2 + k) for k in range((tm_count - 2) // 2)]
    got = [turned(own, steps) for steps in wholes]
    acc_shape = jax.ShapeDtypeStruct((cols + modes, rows), jnp.float32)

    def cost(count):
        flops = 4 * count * (2 * depth * (cols + rows) + (cols + modes) * rows)
        return pl.CostEstimate(flops=flops, bytes_accessed=2 * 10**6, transcendentals=0)

    def col_scratch(count):
        return pltpu.VMEM((cols + modes, count), jnp.bfloat16)

    half_snaps = snaps_dev // 2

    def add_terms(acc, blocks):
        count = sum(block.size for block in blocks) // modes
        before = [] if acc is None else [acc]
        return pl.pallas_call(
            functools.partial(halves_kernel, cols, half_snaps, len(before)),
            out_shape=acc_shape,
            in_specs=[vmem] * (2 + len(before) + len(blocks)),
            out_specs=vmem,
            scratch_shapes=[col_scratch(count)],
            input_output_aliases={2: 0} if before else {},
            compiler_params=params,
            cost_estimate=cost(count),
            name="halves",
        )(left, right, *before, *blocks)

    block_shape = jax.ShapeDtypeStruct((modes, snaps_dev), jnp.float32)
    acc, reduced = pl.pallas_call(
        functools.partial(own_kernel, cols, half_snaps),
        out_shape=(acc_shape, block_shape),
        in_specs=[vmem] * 3,
        out_specs=(vmem, hbm),
        scratch_shapes=[col_scratch(snaps_dev), pltpu.SemaphoreType.DMA],
        compiler_params=params,
        cost_estimate=cost(snaps_dev),
        name="own_group",
    )(left, right, own)
    acc, got_half = lax.optimization_barrier((acc, got_half))
    passed_half = swapped(got_half, "space", 1)
    acc = add_terms(acc, [got_half])
    acc, *got = lax.optimization_barrier((acc, *got))
    passed = [swapped(block, "space", 1) for block in got]
    acc = add_terms(acc, [passed_half] + got)
    width = 128
    firsts = list(range(0, row_block - width, 2 * width))
    firsts = [0] + [first - width for first in firsts[1:]] if len(firsts) > 1 else [0]
    chunks = [(first, end - first) for first, end in zip(firsts, firsts[1:] + [row_block])][::-1]
    out_shapes = (
        block_shape,
        jax.ShapeDtypeStruct((col_block, row_block), jnp.float32),
        jax.ShapeDtypeStruct((modes, row_block), jnp.float32),
    )
    outs = pl.pallas_call(
        functools.partial(last_kernel, row_block, col_block, chunks, wholes),
        out_shape=out_shapes,
        in_specs=[vmem] * (7 + 2 * len(wholes)),
        out_specs=(hbm,) * 3,
        scratch_shapes=[
            pltpu.VMEM((2 * tm_count, modes, width), jnp.float32),
            pltpu.VMEM((2 * tm_count, modes, width), jnp.float32),
            col_scratch(len(wholes) * snaps_dev),
            *[pltpu.VMEM(shape.shape, shape.dtype) for shape in out_shapes],
            pltpu.SemaphoreType.DMA((1 + 2 * len(chunks),)),
        ],
        compiler_params=params,
        cost_estimate=cost(len(wholes) * snaps_dev),
        name="last_half",
    )(left, right, acc, reg_rows, own, got_half, passed_half, *got, *passed)
    return tuple(out.T for out in (reduced, *outs))


def solution(mesh):
    return jax.shard_map(
        local,
        mesh=mesh,
        in_specs=(P("tm", "space"), P("space", None), P()),
        out_specs=(P("tm", None), P("tm", None), P("tm", "space"), P("tm", None)),
        check_vma=False,
    )
```

```python
import functools

import jax
import jax.numpy as jnp
from jax import lax
from jax.experimental import pallas as pl
from jax.experimental.pallas import tpu as pltpu
from jax.sharding import PartitionSpec as P

NT = (((1,), (1,)), ((), ()))


def round_up(value, step):
    return (value + step - 1) // step * step


def tree_sum(terms):
    while len(terms) > 1:
        terms = [terms[i] + terms[i + 1] for i in range(0, len(terms), 2)]
    return terms[0]


def selectors(first, rows, modes, depth):
    feature = first + lax.broadcasted_iota(jnp.int32, (rows, 1), 0)
    mode = lax.broadcasted_iota(jnp.int32, (1, modes), 1)
    start = modes + mode * modes - (mode * (mode - 1)) // 2
    gap = feature - start
    holds = (gap >= 0) & (gap < modes - mode)
    left = jnp.sum(jnp.where(holds, mode, 0), axis=1, keepdims=True)
    right = left + jnp.sum(jnp.where(holds, gap, 0), axis=1, keepdims=True)
    linear = feature < modes
    left = jnp.where(linear, feature, left)
    right = jnp.where(linear, modes, right)
    lane = lax.broadcasted_iota(jnp.int32, (1, depth), 1)
    held = jnp.where(lane < 3 * modes, lax.rem(lane, modes), lane - 2 * modes)
    return (
        jnp.where(held == left, 1.0, 0.0).astype(jnp.bfloat16),
        jnp.where(held == right, 1.0, 0.0).astype(jnp.bfloat16),
    )


def parts_of(block, depth):
    modes, snaps = block.shape
    high = block.astype(jnp.bfloat16)
    rest = block - high.astype(jnp.float32)
    middle = rest.astype(jnp.bfloat16)
    low = (rest - middle.astype(jnp.float32)).astype(jnp.bfloat16)
    tail = depth - 3 * modes
    ones = jnp.where(lax.broadcasted_iota(jnp.int32, (tail, snaps), 0) == 0, 1.0, 0.0)
    return jnp.concatenate([high, middle, low, ones.astype(jnp.bfloat16)], axis=0)


def picked(left, right, parts):
    first = jnp.dot(left, parts, preferred_element_type=jnp.float32)
    second = jnp.dot(right, parts, preferred_element_type=jnp.float32)
    return (first * second).astype(jnp.bfloat16)


def project_kernel(basis_ref, snaps_ref, keep_ref, give_ref, basis, held, basis_sem, sems):
    core = lax.axis_index("space") % 2
    half = held.shape[0] // 2
    states = held.shape[1]
    basis_copy = pltpu.make_async_copy(basis_ref, basis, basis_sem)
    basis_copy.start()
    copies = []
    for slot, (side, at, size) in enumerate(((0, 0, half), (1, 0, half))):
        first = pl.multiple_of((core if side else 1 - core) * half + at, size)
        rows = held.at[pl.ds(side * half + at, size)]
        copies.append(
            (side, at, size, pltpu.make_async_copy(snaps_ref.at[pl.ds(first, size)], rows, sems.at[slot]))
        )
        copies[-1][-1].start()
    basis_copy.wait()
    pieces = 8
    step = states // pieces
    for side, at, size, copy in copies:
        copy.wait()
        rows = slice(side * half + at, side * half + at + size)
        terms = [
            lax.dot_general(
                basis[:, piece * step : (piece + 1) * step],
                held[rows, piece * step : (piece + 1) * step],
                NT,
                preferred_element_type=jnp.float32,
            )
            for piece in range(pieces)
        ]
        (keep_ref if side else give_ref)[:, at : at + size] = tree_sum(terms)


def project(snapshots, basis):
    snaps, states = snapshots.shape
    modes = basis.shape[0]
    hbm = pl.BlockSpec(memory_space=pltpu.HBM)
    vmem = pl.BlockSpec(memory_space=pltpu.VMEM)
    block = jax.ShapeDtypeStruct((modes, snaps // 2), jnp.float32)
    return pl.pallas_call(
        project_kernel,
        out_shape=(block, block),
        in_specs=[hbm, hbm],
        out_specs=(vmem, vmem),
        scratch_shapes=[
            pltpu.VMEM(basis.shape, basis.dtype),
            pltpu.VMEM((snaps, states), snapshots.dtype),
            pltpu.SemaphoreType.DMA,
            pltpu.SemaphoreType.DMA((2,)),
        ],
        compiler_params=pltpu.CompilerParams(vmem_limit_bytes=55000 * 1024),
        name="project",
    )(basis, snapshots)


def selector_kernel(row_block, col_block, after_ref, left_ref, right_ref):
    modes = after_ref.shape[0]
    cols = round_up(col_block, 16)
    rows = left_ref.shape[0] - cols
    depth = left_ref.shape[1]
    for at, size, first in (
        (0, cols, lax.axis_index("space") * col_block),
        (cols, rows, lax.axis_index("tm") * row_block),
    ):
        left, right = selectors(first, size, modes, depth)
        left_ref[at : at + size] = left
        right_ref[at : at + size] = right


def inner_rates(block, half):
    snaps = block.shape[1]
    lane = lax.rem(lax.broadcasted_iota(jnp.int32, (1, snaps), 1), half)
    rates = (pltpu.roll(block, snaps - 1, 1) - pltpu.roll(block, 1, 1)) * 0.5
    return jnp.where((lane == 0) | (lane == half - 1), 0.0, rates)


def column_side(left_ref, right_ref, parts, rates, cols, col_scratch):
    col_scratch[:cols, : rates.shape[1]] = picked(left_ref[:cols], right_ref[:cols], parts)
    col_scratch[cols:, : rates.shape[1]] = rates.astype(jnp.bfloat16)


def terms_of(left_ref, right_ref, block, half, cols, col_scratch):
    parts = parts_of(block, left_ref.shape[1])
    column_side(left_ref, right_ref, parts, inner_rates(block, half), cols, col_scratch)
    row_features = picked(left_ref[cols:], right_ref[cols:], parts)
    return lax.dot_general(
        col_scratch[:, : block.shape[1]], row_features, NT, preferred_element_type=jnp.float32
    )


def halves_kernel(cols, half, has_before, left_ref, right_ref, *refs):
    before_ref, refs = (refs[0], refs[1:]) if has_before else (None, refs)
    block_refs, acc_ref, col_scratch = refs[:-2], refs[-2], refs[-1]
    block = jnp.concatenate([ref[...] for ref in block_refs], axis=1)
    term = terms_of(left_ref, right_ref, block, half, cols, col_scratch)
    acc_ref[...] = before_ref[...] + term if has_before else term


def own_kernel(cols, half, left_ref, right_ref, own_ref, acc_ref, reduced_ref, col_scratch, sem):
    copy = pltpu.make_async_copy(own_ref, reduced_ref, sem)
    copy.start()
    acc_ref[...] = terms_of(left_ref, right_ref, own_ref[...], half, cols, col_scratch)
    copy.wait()


def edge_columns(halves, starts, ends):
    count, modes, width = starts.shape
    for group, side, block in halves:
        at = 2 * group + side
        starts[at] = block[:, :width]
        ends[at] = block[:, block.shape[1] - width :]
    lane = lax.broadcasted_iota(jnp.int32, (1, width), 1)
    heads = jnp.zeros((modes, width), jnp.float32)
    tails = jnp.zeros((modes, width), jnp.float32)
    for at in range(count):
        pair = (lane == 2 * at) | (lane == 2 * at + 1)
        heads = jnp.where(pair, pltpu.roll(starts[at], 2 * at, 1), heads)
        tails = jnp.where(pair, pltpu.roll(ends[at], (2 * at + 2) % width, 1), tails)
    after = pltpu.roll(heads, width - 1, 1)
    before = pltpu.roll(tails, 1, 1)
    rates = (after - before) * 0.5
    rates = jnp.where(lane == 0, after - heads, rates)
    rates = jnp.where(lane == 2 * count - 1, tails - before, rates)
    edge = jnp.where(lax.rem(lane, 2) == 0, heads, tails)
    inside = lane < 2 * count
    return jnp.where(inside, edge, 0.0), jnp.where(inside, rates, 0.0)


def last_kernel(row_block, col_block, chunks, wholes, left_ref, right_ref, before_ref, reg_ref, *refs):
    each = len(wholes)
    own_ref, got_half_ref, passed_half_ref = refs[:3]
    got_refs, passed_refs, refs = refs[3 : 3 + each], refs[3 + each : 3 + 2 * each], refs[3 + 2 * each :]
    rates_ref, normal_ref, right_side_ref = refs[:3]
    starts, ends, col_scratch, rates_out, normal_out, right_side_out, sems = refs[3:]
    time_idx = lax.axis_index("tm")
    space_idx = lax.axis_index("space")
    core = space_idx % 2
    modes, snaps = own_ref.shape
    half = snaps // 2
    groups = 2 + 2 * each
    cols = round_up(col_block, 16)
    depth = left_ref.shape[1]
    copies = []

    def send(source, target):
        copies.append(pltpu.make_async_copy(source, target, sems.at[len(copies)]))
        copies[-1].start()

    def group_at(steps, side):
        return lax.rem(time_idx + groups - jnp.where(side == 0, steps[0], steps[1]), groups)

    halves = [
        (group_at((1, 1), 0), core, got_half_ref[...]),
        (group_at((1, 1), 0), 1 - core, passed_half_ref[...]),
    ]
    blocks = [(time_idx, own_ref)]
    blocks += [(group_at(steps, core), ref) for steps, ref in zip(wholes, got_refs)]
    blocks += [(group_at(steps, 1 - core), ref) for steps, ref in zip(wholes, passed_refs)]
    for group, ref in blocks:
        halves += [(group, side, ref[:, side * half : (side + 1) * half]) for side in range(2)]
    edge, edge_rates = edge_columns(halves, starts, ends)
    own = own_ref[...]
    width = edge.shape[1]
    own_edges = pltpu.roll(edge_rates, lax.rem(width - 4 * time_idx, width), 1)
    lane = lax.broadcasted_iota(jnp.int32, (1, snaps), 1)
    rates = jnp.where(lane == 0, own_edges[:, 0:1], inner_rates(own, snaps))
    rates_out[...] = jnp.where(lane == snaps - 1, own_edges[:, 3:4], rates)
    send(rates_out, rates_ref)

    block = jnp.concatenate([ref[...] for ref in passed_refs], axis=1)
    parts = parts_of(block, depth)
    column_side(left_ref, right_ref, parts, inner_rates(block, half), cols, col_scratch)
    scale = 1.0 / (groups * snaps)
    edge_parts = parts_of(edge, depth)
    edge_rates = edge_rates.astype(jnp.bfloat16)
    for at, size in chunks:
        pick = slice(cols + at, cols + at + round_up(size, 16))
        features = picked(left_ref[pick], right_ref[pick], parts)
        edge_features = picked(left_ref[pick], right_ref[pick], edge_parts)
        total = before_ref[:, at : at + features.shape[0]] + lax.dot_general(
            col_scratch[...], features, NT, preferred_element_type=jnp.float32
        )
        edge_total = lax.dot_general(edge_rates, edge_features, NT, preferred_element_type=jnp.float32)
        col_ids = space_idx * col_block + lax.broadcasted_iota(jnp.int32, (col_block, size), 0)
        row_ids = time_idx * row_block + at + lax.broadcasted_iota(jnp.int32, (col_block, size), 1)
        diagonal = jnp.where(row_ids == col_ids, reg_ref[:, at : at + size], 0.0)
        normal_out[:, at : at + size] = total[:col_block, :size] * scale + diagonal
        right_side_out[:, at : at + size] = (total[cols:] + edge_total)[:, :size] * scale
        send(normal_out.at[:, at : at + size], normal_ref.at[:, at : at + size])
        send(right_side_out.at[:, at : at + size], right_side_ref.at[:, at : at + size])
    for copy in copies:
        copy.wait()


def swapped(value, axis, distance):
    return lax.ppermute(value, axis, [(i, i ^ distance) for i in range(lax.axis_size(axis))])


def shifted(value, distance):
    count = lax.axis_size("space")
    return lax.ppermute(value, "space", [(i, (i + distance) % count) for i in range(count)])


def turned(value, distances):
    tm_count = lax.axis_size("tm")
    space_count = lax.axis_size("space")
    perm = []
    for time in range(tm_count):
        for space in range(space_count):
            target = (time + distances[space % 2]) % tm_count
            perm.append((time * space_count + space, target * space_count + space))
    return lax.ppermute(value, ("tm", "space"), perm)


def local(snapshots, modes_basis, reg_weights):
    feature_count = reg_weights.shape[0]
    snaps_dev = snapshots.shape[0]
    modes = modes_basis.shape[1]
    tm_count = lax.axis_size("tm")
    space_count = lax.axis_size("space")
    row_block = feature_count // tm_count
    col_block = feature_count // space_count
    rows = round_up(row_block, 16)
    cols = round_up(col_block, 16)
    depth = round_up(3 * modes + 1, 128)
    time_idx = lax.axis_index("tm")
    vmem = pl.BlockSpec(memory_space=pltpu.VMEM)
    hbm = pl.BlockSpec(memory_space=pltpu.HBM)
    params = pltpu.CompilerParams(vmem_limit_bytes=32 * 1024 * 1024)

    keep, give = project(snapshots, modes_basis.T)
    half = keep + swapped(give, "space", 1)
    after, half = lax.optimization_barrier((time_idx, half))
    selector = jax.ShapeDtypeStruct((cols + rows, depth), jnp.bfloat16)
    left, right = pl.pallas_call(
        functools.partial(selector_kernel, row_block, col_block),
        out_shape=(selector, selector),
        in_specs=[vmem],
        out_specs=(vmem, vmem),
        compiler_params=params,
        cost_estimate=pl.CostEstimate(flops=10**6, bytes_accessed=10**6, transcendentals=0),
        name="selectors",
    )(half)
    first_row = after * row_block
    reg_rows = lax.dynamic_slice_in_dim(reg_weights, first_row, row_block, 0)[None]

    terms = [shifted(half, step) for step in range(2, space_count, 2)]
    terms = [half] + list(lax.optimization_barrier(tuple(terms[::-1]))[::-1])
    while len(terms) > 1:
        middle = len(terms) // 2
        terms = [terms[i] + terms[i + middle] for i in range(middle)]
    mine, left, right, reg_rows = lax.optimization_barrier((terms[0], left, right, reg_rows))
    core = lax.axis_index("space") % 2
    own_other = swapped(mine, "space", 1)
    got_half = turned(mine, (1, 1))
    own = jnp.concatenate(
        [jnp.where(core == 0, mine, own_other), jnp.where(core == 0, own_other, mine)], axis=1
    )
    wholes = [(tm_count - 1 - k, 2 + k) for k in range((tm_count - 2) // 2)]
    got = [turned(own, steps) for steps in wholes]
    acc_shape = jax.ShapeDtypeStruct((cols + modes, rows), jnp.float32)

    def cost(count):
        flops = 4 * count * (2 * depth * (cols + rows) + (cols + modes) * rows)
        return pl.CostEstimate(flops=flops, bytes_accessed=2 * 10**6, transcendentals=0)

    def col_scratch(count):
        return pltpu.VMEM((cols + modes, count), jnp.bfloat16)

    half_snaps = snaps_dev // 2

    def add_terms(acc, blocks):
        count = sum(block.size for block in blocks) // modes
        before = [] if acc is None else [acc]
        return pl.pallas_call(
            functools.partial(halves_kernel, cols, half_snaps, len(before)),
            out_shape=acc_shape,
            in_specs=[vmem] * (2 + len(before) + len(blocks)),
            out_specs=vmem,
            scratch_shapes=[col_scratch(count)],
            input_output_aliases={2: 0} if before else {},
            compiler_params=params,
            cost_estimate=cost(count),
            name="halves",
        )(left, right, *before, *blocks)

    block_shape = jax.ShapeDtypeStruct((modes, snaps_dev), jnp.float32)
    acc, reduced = pl.pallas_call(
        functools.partial(own_kernel, cols, half_snaps),
        out_shape=(acc_shape, block_shape),
        in_specs=[vmem] * 3,
        out_specs=(vmem, hbm),
        scratch_shapes=[col_scratch(snaps_dev), pltpu.SemaphoreType.DMA],
        compiler_params=params,
        cost_estimate=cost(snaps_dev),
        name="own_group",
    )(left, right, own)
    acc, got_half = lax.optimization_barrier((acc, got_half))
    passed_half = swapped(got_half, "space", 1)
    acc = add_terms(acc, [got_half])
    acc, *got = lax.optimization_barrier((acc, *got))
    passed = [swapped(block, "space", 1) for block in got]
    acc = add_terms(acc, [passed_half] + got)
    width = 128
    firsts = list(range(0, row_block - width, 2 * width))
    firsts = [0] + [first - width for first in firsts[1:]] if len(firsts) > 1 else [0]
    chunks = [(first, end - first) for first, end in zip(firsts, firsts[1:] + [row_block])][::-1]
    out_shapes = (
        block_shape,
        jax.ShapeDtypeStruct((col_block, row_block), jnp.float32),
        jax.ShapeDtypeStruct((modes, row_block), jnp.float32),
    )
    outs = pl.pallas_call(
        functools.partial(last_kernel, row_block, col_block, chunks, wholes),
        out_shape=out_shapes,
        in_specs=[vmem] * (7 + 2 * len(wholes)),
        out_specs=(hbm,) * 3,
        scratch_shapes=[
            pltpu.VMEM((2 * tm_count, modes, width), jnp.float32),
            pltpu.VMEM((2 * tm_count, modes, width), jnp.float32),
            col_scratch(len(wholes) * snaps_dev),
            *[pltpu.VMEM(shape.shape, shape.dtype) for shape in out_shapes],
            pltpu.SemaphoreType.DMA((1 + 2 * len(chunks),)),
        ],
        compiler_params=params,
        cost_estimate=cost(len(wholes) * snaps_dev),
        name="last_half",
    )(left, right, acc, reg_rows, own, got_half, passed_half, *got, *passed)
    return tuple(out.T for out in (reduced, *outs))


def solution(mesh):
    return jax.shard_map(
        local,
        mesh=mesh,
        in_specs=(P("tm", "space"), P("space", None), P()),
        out_specs=(P("tm", None), P("tm", None), P("tm", "space"), P("tm", None)),
        check_vma=False,
    )
```

```python
import functools

import jax
import jax.numpy as jnp
from jax import lax
from jax.experimental import pallas as pl
from jax.experimental.pallas import tpu as pltpu
from jax.sharding import PartitionSpec as P

NT = (((1,), (1,)), ((), ()))


def round_up(value, step):
    return (value + step - 1) // step * step


def tree_sum(terms):
    while len(terms) > 1:
        terms = [terms[i] + terms[i + 1] for i in range(0, len(terms), 2)]
    return terms[0]


def selectors(first, rows, modes, depth):
    feature = first + lax.broadcasted_iota(jnp.int32, (rows, 1), 0)
    mode = lax.broadcasted_iota(jnp.int32, (1, modes), 1)
    start = modes + mode * modes - (mode * (mode - 1)) // 2
    gap = feature - start
    holds = (gap >= 0) & (gap < modes - mode)
    left = jnp.sum(jnp.where(holds, mode, 0), axis=1, keepdims=True)
    right = left + jnp.sum(jnp.where(holds, gap, 0), axis=1, keepdims=True)
    linear = feature < modes
    left = jnp.where(linear, feature, left)
    right = jnp.where(linear, modes, right)
    lane = lax.broadcasted_iota(jnp.int32, (1, depth), 1)
    held = jnp.where(lane < 3 * modes, lax.rem(lane, modes), lane - 2 * modes)
    return (
        jnp.where(held == left, 1.0, 0.0).astype(jnp.bfloat16),
        jnp.where(held == right, 1.0, 0.0).astype(jnp.bfloat16),
    )


def parts_of(block, depth):
    modes, snaps = block.shape
    high = block.astype(jnp.bfloat16)
    rest = block - high.astype(jnp.float32)
    middle = rest.astype(jnp.bfloat16)
    low = (rest - middle.astype(jnp.float32)).astype(jnp.bfloat16)
    tail = depth - 3 * modes
    ones = jnp.where(lax.broadcasted_iota(jnp.int32, (tail, snaps), 0) == 0, 1.0, 0.0)
    return jnp.concatenate([high, middle, low, ones.astype(jnp.bfloat16)], axis=0)


def picked(left, right, parts):
    first = jnp.dot(left, parts, preferred_element_type=jnp.float32)
    second = jnp.dot(right, parts, preferred_element_type=jnp.float32)
    return (first * second).astype(jnp.bfloat16)


def project_kernel(basis_ref, snaps_ref, keep_ref, give_ref, basis, held, basis_sem, sems):
    core = lax.axis_index("space") % 2
    half = held.shape[0] // 2
    states = held.shape[1]
    basis_copy = pltpu.make_async_copy(basis_ref, basis, basis_sem)
    basis_copy.start()
    copies = []
    for slot, (side, at, size) in enumerate(((0, 0, half), (1, 0, half))):
        first = pl.multiple_of((core if side else 1 - core) * half + at, size)
        rows = held.at[pl.ds(side * half + at, size)]
        copies.append(
            (side, at, size, pltpu.make_async_copy(snaps_ref.at[pl.ds(first, size)], rows, sems.at[slot]))
        )
        copies[-1][-1].start()
    basis_copy.wait()
    pieces = 8
    step = states // pieces
    for side, at, size, copy in copies:
        copy.wait()
        rows = slice(side * half + at, side * half + at + size)
        terms = [
            lax.dot_general(
                basis[:, piece * step : (piece + 1) * step],
                held[rows, piece * step : (piece + 1) * step],
                NT,
                preferred_element_type=jnp.float32,
            )
            for piece in range(pieces)
        ]
        (keep_ref if side else give_ref)[:, at : at + size] = tree_sum(terms)


def project(snapshots, basis):
    snaps, states = snapshots.shape
    modes = basis.shape[0]
    hbm = pl.BlockSpec(memory_space=pltpu.HBM)
    vmem = pl.BlockSpec(memory_space=pltpu.VMEM)
    block = jax.ShapeDtypeStruct((modes, snaps // 2), jnp.float32)
    return pl.pallas_call(
        project_kernel,
        out_shape=(block, block),
        in_specs=[hbm, hbm],
        out_specs=(vmem, vmem),
        scratch_shapes=[
            pltpu.VMEM(basis.shape, basis.dtype),
            pltpu.VMEM((snaps, states), snapshots.dtype),
            pltpu.SemaphoreType.DMA,
            pltpu.SemaphoreType.DMA((2,)),
        ],
        compiler_params=pltpu.CompilerParams(vmem_limit_bytes=55000 * 1024),
        name="project",
    )(basis, snapshots)


def selector_kernel(row_block, col_block, after_ref, left_ref, right_ref):
    modes = after_ref.shape[0]
    cols = round_up(col_block, 16)
    rows = left_ref.shape[0] - cols
    depth = left_ref.shape[1]
    for at, size, first in (
        (0, cols, lax.axis_index("space") * col_block),
        (cols, rows, lax.axis_index("tm") * row_block),
    ):
        left, right = selectors(first, size, modes, depth)
        left_ref[at : at + size] = left
        right_ref[at : at + size] = right


def inner_rates(block, half):
    snaps = block.shape[1]
    lane = lax.rem(lax.broadcasted_iota(jnp.int32, (1, snaps), 1), half)
    rates = (pltpu.roll(block, snaps - 1, 1) - pltpu.roll(block, 1, 1)) * 0.5
    return jnp.where((lane == 0) | (lane == half - 1), 0.0, rates)


def column_side(left_ref, right_ref, parts, rates, cols, col_scratch):
    col_scratch[:cols, : rates.shape[1]] = picked(left_ref[:cols], right_ref[:cols], parts)
    col_scratch[cols:, : rates.shape[1]] = rates.astype(jnp.bfloat16)


def terms_of(left_ref, right_ref, block, half, cols, col_scratch):
    parts = parts_of(block, left_ref.shape[1])
    column_side(left_ref, right_ref, parts, inner_rates(block, half), cols, col_scratch)
    row_features = picked(left_ref[cols:], right_ref[cols:], parts)
    return lax.dot_general(
        col_scratch[:, : block.shape[1]], row_features, NT, preferred_element_type=jnp.float32
    )


def halves_kernel(cols, half, has_before, left_ref, right_ref, *refs):
    before_ref, refs = (refs[0], refs[1:]) if has_before else (None, refs)
    block_refs, acc_ref, col_scratch = refs[:-2], refs[-2], refs[-1]
    block = jnp.concatenate([ref[...] for ref in block_refs], axis=1)
    term = terms_of(left_ref, right_ref, block, half, cols, col_scratch)
    acc_ref[...] = before_ref[...] + term if has_before else term


def own_kernel(cols, half, left_ref, right_ref, own_ref, acc_ref, reduced_ref, col_scratch, sem):
    copy = pltpu.make_async_copy(own_ref, reduced_ref, sem)
    copy.start()
    acc_ref[...] = terms_of(left_ref, right_ref, own_ref[...], half, cols, col_scratch)
    copy.wait()


def edge_columns(halves, starts, ends):
    count, modes, width = starts.shape
    for group, side, block in halves:
        at = 2 * group + side
        starts[at] = block[:, :width]
        ends[at] = block[:, block.shape[1] - width :]
    lane = lax.broadcasted_iota(jnp.int32, (1, width), 1)
    heads = jnp.zeros((modes, width), jnp.float32)
    tails = jnp.zeros((modes, width), jnp.float32)
    for at in range(count):
        pair = (lane == 2 * at) | (lane == 2 * at + 1)
        heads = jnp.where(pair, pltpu.roll(starts[at], 2 * at, 1), heads)
        tails = jnp.where(pair, pltpu.roll(ends[at], (2 * at + 2) % width, 1), tails)
    after = pltpu.roll(heads, width - 1, 1)
    before = pltpu.roll(tails, 1, 1)
    rates = (after - before) * 0.5
    rates = jnp.where(lane == 0, after - heads, rates)
    rates = jnp.where(lane == 2 * count - 1, tails - before, rates)
    edge = jnp.where(lax.rem(lane, 2) == 0, heads, tails)
    inside = lane < 2 * count
    return jnp.where(inside, edge, 0.0), jnp.where(inside, rates, 0.0)


def last_kernel(row_block, col_block, chunks, wholes, left_ref, right_ref, before_ref, reg_ref, *refs):
    each = len(wholes)
    own_ref, got_half_ref, passed_half_ref = refs[:3]
    got_refs, passed_refs, refs = refs[3 : 3 + each], refs[3 + each : 3 + 2 * each], refs[3 + 2 * each :]
    rates_ref, normal_ref, right_side_ref = refs[:3]
    starts, ends, col_scratch, rates_out, normal_out, right_side_out, sems = refs[3:]
    time_idx = lax.axis_index("tm")
    space_idx = lax.axis_index("space")
    core = space_idx % 2
    modes, snaps = own_ref.shape
    half = snaps // 2
    groups = 2 + 2 * each
    cols = round_up(col_block, 16)
    depth = left_ref.shape[1]
    copies = []

    def send(source, target):
        copies.append(pltpu.make_async_copy(source, target, sems.at[len(copies)]))
        copies[-1].start()

    def group_at(steps, side):
        return lax.rem(time_idx + groups - jnp.where(side == 0, steps[0], steps[1]), groups)

    halves = [
        (group_at((1, 1), 0), core, got_half_ref[...]),
        (group_at((1, 1), 0), 1 - core, passed_half_ref[...]),
    ]
    blocks = [(time_idx, own_ref)]
    blocks += [(group_at(steps, core), ref) for steps, ref in zip(wholes, got_refs)]
    blocks += [(group_at(steps, 1 - core), ref) for steps, ref in zip(wholes, passed_refs)]
    for group, ref in blocks:
        halves += [(group, side, ref[:, side * half : (side + 1) * half]) for side in range(2)]
    edge, edge_rates = edge_columns(halves, starts, ends)
    own = own_ref[...]
    width = edge.shape[1]
    own_edges = pltpu.roll(edge_rates, lax.rem(width - 4 * time_idx, width), 1)
    lane = lax.broadcasted_iota(jnp.int32, (1, snaps), 1)
    rates = jnp.where(lane == 0, own_edges[:, 0:1], inner_rates(own, snaps))
    rates_out[...] = jnp.where(lane == snaps - 1, own_edges[:, 3:4], rates)
    send(rates_out, rates_ref)

    block = jnp.concatenate([ref[...] for ref in passed_refs], axis=1)
    parts = parts_of(block, depth)
    column_side(left_ref, right_ref, parts, inner_rates(block, half), cols, col_scratch)
    scale = 1.0 / (groups * snaps)
    edge_parts = parts_of(edge, depth)
    edge_rates = edge_rates.astype(jnp.bfloat16)
    for at, size in chunks:
        pick = slice(cols + at, cols + at + round_up(size, 16))
        features = picked(left_ref[pick], right_ref[pick], parts)
        edge_features = picked(left_ref[pick], right_ref[pick], edge_parts)
        total = before_ref[:, at : at + features.shape[0]] + lax.dot_general(
            col_scratch[...], features, NT, preferred_element_type=jnp.float32
        )
        edge_total = lax.dot_general(edge_rates, edge_features, NT, preferred_element_type=jnp.float32)
        col_ids = space_idx * col_block + lax.broadcasted_iota(jnp.int32, (col_block, size), 0)
        row_ids = time_idx * row_block + at + lax.broadcasted_iota(jnp.int32, (col_block, size), 1)
        diagonal = jnp.where(row_ids == col_ids, reg_ref[:, at : at + size], 0.0)
        normal_out[:, at : at + size] = total[:col_block, :size] * scale + diagonal
        right_side_out[:, at : at + size] = (total[cols:] + edge_total)[:, :size] * scale
        send(normal_out.at[:, at : at + size], normal_ref.at[:, at : at + size])
        send(right_side_out.at[:, at : at + size], right_side_ref.at[:, at : at + size])
    for copy in copies:
        copy.wait()


def swapped(value, axis, distance):
    return lax.ppermute(value, axis, [(i, i ^ distance) for i in range(lax.axis_size(axis))])


def shifted(value, distance):
    count = lax.axis_size("space")
    return lax.ppermute(value, "space", [(i, (i + distance) % count) for i in range(count)])


def turned(value, distances):
    tm_count = lax.axis_size("tm")
    space_count = lax.axis_size("space")
    perm = []
    for time in range(tm_count):
        for space in range(space_count):
            target = (time + distances[space % 2]) % tm_count
            perm.append((time * space_count + space, target * space_count + space))
    return lax.ppermute(value, ("tm", "space"), perm)


def local(snapshots, modes_basis, reg_weights):
    feature_count = reg_weights.shape[0]
    snaps_dev = snapshots.shape[0]
    modes = modes_basis.shape[1]
    tm_count = lax.axis_size("tm")
    space_count = lax.axis_size("space")
    row_block = feature_count // tm_count
    col_block = feature_count // space_count
    rows = round_up(row_block, 16)
    cols = round_up(col_block, 16)
    depth = round_up(3 * modes + 1, 128)
    time_idx = lax.axis_index("tm")
    vmem = pl.BlockSpec(memory_space=pltpu.VMEM)
    hbm = pl.BlockSpec(memory_space=pltpu.HBM)
    params = pltpu.CompilerParams(vmem_limit_bytes=32 * 1024 * 1024)

    keep, give = project(snapshots, modes_basis.T)
    half = keep + swapped(give, "space", 1)
    after, half = lax.optimization_barrier((time_idx, half))
    selector = jax.ShapeDtypeStruct((cols + rows, depth), jnp.bfloat16)
    left, right = pl.pallas_call(
        functools.partial(selector_kernel, row_block, col_block),
        out_shape=(selector, selector),
        in_specs=[vmem],
        out_specs=(vmem, vmem),
        compiler_params=params,
        cost_estimate=pl.CostEstimate(flops=10**6, bytes_accessed=10**6, transcendentals=0),
        name="selectors",
    )(half)
    first_row = after * row_block
    reg_rows = lax.dynamic_slice_in_dim(reg_weights, first_row, row_block, 0)[None]

    terms = [shifted(half, step) for step in range(2, space_count, 2)]
    terms = [half] + list(lax.optimization_barrier(tuple(terms[::-1]))[::-1])
    while len(terms) > 1:
        middle = len(terms) // 2
        terms = [terms[i] + terms[i + middle] for i in range(middle)]
    mine, left, right, reg_rows = lax.optimization_barrier((terms[0], left, right, reg_rows))
    core = lax.axis_index("space") % 2
    own_other = swapped(mine, "space", 1)
    got_half = turned(mine, (1, 1))
    own = jnp.concatenate(
        [jnp.where(core == 0, mine, own_other), jnp.where(core == 0, own_other, mine)], axis=1
    )
    wholes = [(tm_count - 1 - k, 2 + k) for k in range((tm_count - 2) // 2)]
    got = [turned(own, steps) for steps in wholes]
    acc_shape = jax.ShapeDtypeStruct((cols + modes, rows), jnp.float32)

    def cost(count):
        flops = 4 * count * (2 * depth * (cols + rows) + (cols + modes) * rows)
        return pl.CostEstimate(flops=flops, bytes_accessed=2 * 10**6, transcendentals=0)

    def col_scratch(count):
        return pltpu.VMEM((cols + modes, count), jnp.bfloat16)

    half_snaps = snaps_dev // 2

    def add_terms(acc, blocks):
        count = sum(block.size for block in blocks) // modes
        before = [] if acc is None else [acc]
        return pl.pallas_call(
            functools.partial(halves_kernel, cols, half_snaps, len(before)),
            out_shape=acc_shape,
            in_specs=[vmem] * (2 + len(before) + len(blocks)),
            out_specs=vmem,
            scratch_shapes=[col_scratch(count)],
            input_output_aliases={2: 0} if before else {},
            compiler_params=params,
            cost_estimate=cost(count),
            name="halves",
        )(left, right, *before, *blocks)

    block_shape = jax.ShapeDtypeStruct((modes, snaps_dev), jnp.float32)
    acc, reduced = pl.pallas_call(
        functools.partial(own_kernel, cols, half_snaps),
        out_shape=(acc_shape, block_shape),
        in_specs=[vmem] * 3,
        out_specs=(vmem, hbm),
        scratch_shapes=[col_scratch(snaps_dev), pltpu.SemaphoreType.DMA],
        compiler_params=params,
        cost_estimate=cost(snaps_dev),
        name="own_group",
    )(left, right, own)
    acc, got_half = lax.optimization_barrier((acc, got_half))
    passed_half = swapped(got_half, "space", 1)
    acc = add_terms(acc, [got_half])
    acc, *got = lax.optimization_barrier((acc, *got))
    passed = [swapped(block, "space", 1) for block in got]
    acc = add_terms(acc, [passed_half] + got)
    width = 128
    firsts = [0, 2 * width] if row_block > 3 * width else [0]
    chunks = [(first, end - first) for first, end in zip(firsts, firsts[1:] + [row_block])][::-1]
    out_shapes = (
        block_shape,
        jax.ShapeDtypeStruct((col_block, row_block), jnp.float32),
        jax.ShapeDtypeStruct((modes, row_block), jnp.float32),
    )
    outs = pl.pallas_call(
        functools.partial(last_kernel, row_block, col_block, chunks, wholes),
        out_shape=out_shapes,
        in_specs=[vmem] * (7 + 2 * len(wholes)),
        out_specs=(hbm,) * 3,
        scratch_shapes=[
            pltpu.VMEM((2 * tm_count, modes, width), jnp.float32),
            pltpu.VMEM((2 * tm_count, modes, width), jnp.float32),
            col_scratch(len(wholes) * snaps_dev),
            *[pltpu.VMEM(shape.shape, shape.dtype) for shape in out_shapes],
            pltpu.SemaphoreType.DMA((1 + 2 * len(chunks),)),
        ],
        compiler_params=params,
        cost_estimate=cost(len(wholes) * snaps_dev),
        name="last_half",
    )(left, right, acc, reg_rows, own, got_half, passed_half, *got, *passed)
    return tuple(out.T for out in (reduced, *outs))


def solution(mesh):
    return jax.shard_map(
        local,
        mesh=mesh,
        in_specs=(P("tm", "space"), P("space", None), P()),
        out_specs=(P("tm", None), P("tm", None), P("tm", "space"), P("tm", None)),
        check_vma=False,
    )
```
